32 devices in a mesh: seq: 8 (over z, y), rep: 4 (over x, core).
Axes of the slice: x: 2, y: 2, z: 4, core: 2. Of those that a mesh axis runs over, the one named last changes fastest.
Arguments:
- tokens: bfloat16 [4, 12288, 768], P('rep', 'seq'), may hold values from -6 to 6
- cotangent: bfloat16 [4, 12288, 768], P('rep', 'seq'), may hold values from -6 to 6
- seq_lengths: int32 [4, 3], P('rep'), may hold values from 129 to 10752, as said below
- in_weight: float32 [768, 3352], P(('seq', 'rep')), may hold values from -0.21875 to 0.21875
- in_first: float32 [768, 3352], P(('seq', 'rep')), may hold values from -0.0008544922 to 0.0008544922
- in_second: float32 [768, 3352], P(('seq', 'rep')), may hold values from 1.3969596e-08 to 5.577215e-08
- out_weight: float32 [1536, 768], P(('seq', 'rep')), may hold values from -0.15625 to 0.15625
- out_first: float32 [1536, 768], P(('seq', 'rep')), may hold values from -0.0008544922 to 0.0008544922
- out_second: float32 [1536, 768], P(('seq', 'rep')), may hold values from 1.3969596e-08 to 5.577215e-08
- conv_weight: float32 [4, 1792], P(None, ('seq', 'rep')), may hold values from -3 to 3
- conv_first: float32 [4, 1792], P(None, ('seq', 'rep')), may hold values from -0.0008544922 to 0.0008544922
- conv_second: float32 [4, 1792], P(None, ('seq', 'rep')), may hold values from 1.3969596e-08 to 5.577215e-08
- vectors: float32 [4096], P(('seq', 'rep')), may hold values from -0.5 to 1.8, as said below
- vec_first: float32 [4096], P(('seq', 'rep')), may hold values from -0.0034179688 to 0.0034179688
- vec_second: float32 [4096], P(('seq', 'rep')), may hold values from 2.230886e-07 to 8.9501026e-07
- head_params: float32 [3, 24], replicated, may hold values from -6 to 1.5
- head_first: float32 [3, 24], replicated, may hold values from -0.0034179688 to 0.0034179688
- head_second: float32 [3, 24], replicated, may hold values from 2.230886e-07 to 8.9501026e-07
Outputs:
- block_out: bfloat16 [4, 12288, 768], P('rep', 'seq')
- input_grad: bfloat16 [4, 12288, 768], P('rep', 'seq')
- grad_norm: float32 [], replicated
- in_clipped: float32 [768, 3352], P(('seq', 'rep'))
- in_first_new: float32 [768, 3352], P(('seq', 'rep'))
- in_second_new: float32 [768, 3352], P(('seq', 'rep'))
- in_master: float32 [768, 3352], P(('seq', 'rep'))
- in_copy: bfloat16 [768, 3352], P(('seq', 'rep'))
- out_clipped: float32 [1536, 768], P(('seq', 'rep'))
- out_first_new: float32 [1536, 768], P(('seq', 'rep'))
- out_second_new: float32 [1536, 768], P(('seq', 'rep'))
- out_master: float32 [1536, 768], P(('seq', 'rep'))
- out_copy: bfloat16 [1536, 768], P(('seq', 'rep'))
- conv_clipped: float32 [4, 1792], P(None, ('seq', 'rep'))
- conv_first_new: float32 [4, 1792], P(None, ('seq', 'rep'))
- conv_second_new: float32 [4, 1792], P(None, ('seq', 'rep'))
- conv_master: float32 [4, 1792], P(None, ('seq', 'rep'))
- conv_copy: bfloat16 [4, 1792], P(None, ('seq', 'rep'))
- vec_clipped: float32 [4096], P(('seq', 'rep'))
- vec_first_new: float32 [4096], P(('seq', 'rep'))
- vec_second_new: float32 [4096], P(('seq', 'rep'))
- vec_master: float32 [4096], P(('seq', 'rep'))
- vec_copy: bfloat16 [4096], P(('seq', 'rep'))
- head_clipped: float32 [3, 24], replicated
- head_first_new: float32 [3, 24], replicated
- head_second_new: float32 [3, 24], replicated
- head_master: float32 [3, 24], replicated
- head_copy: bfloat16 [3, 24], replicated
The draws below stay inside these ranges and needn't reach their ends.
Inputs may be any that keep to these rules, and one draw needn't show every extreme that they name: `seq_lengths`: in each group the lengths, each rounded up to a multiple of 256, add up to 12288; the second sequence of each group has exactly 10752 tokens, and the first and the third together round up to 6 blocks. `vectors`: the 2304 gains are positive.
All inputs are finite; a program needn't handle non-finite values.
Results may differ from the reference program's by a relative error of at most 0.012.
Values may be sent and summed in bfloat16 or wider, within the bound.
No kernel may reach another device: no remote copies, remote signals or barrier semaphores. Data moves between devices by JAX's collectives and lax.ppermute only.
A program may use at most 320 MiB of HBM per device.

```python
import math
import jax
import jax.numpy as jnp
from jax import lax

D = 768
H = 24
P_SIZE = 64
NS = 128
SPAN = 256
STEP = 10
CH_DEV = 6
DI = 1536
CW = 1792
PW = 3352
GROUP_TOK = 12288
MOSTCH = 42
NPAR = 3765320
N_REP = 4


def draw_seq_lengths(key, part):
    key = jax.random.fold_in(key, 11)

    def one_group(group_key):
        split_key, pad_key = jax.random.split(group_key)
        lead_blocks = jax.random.randint(split_key, (), 1, CH_DEV)
        trail_blocks = CH_DEV - lead_blocks
        pad_rows = jax.random.randint(pad_key, (2,), 0, SPAN // 2)
        return jnp.stack([lead_blocks * SPAN - pad_rows[0], jnp.int32(MOSTCH * SPAN), trail_blocks * SPAN - pad_rows[1]])
    return jax.vmap(one_group)(jax.random.split(key, N_REP)).astype(jnp.int32)


def rising(count_rows, lowest):
    steps_up = jnp.arange(count_rows, dtype=jnp.float32) / count_rows
    return lowest + steps_up


def draw_vectors(key, part):
    key = jax.random.fold_in(key, 23)
    first_key, second_key, third_key = jax.random.split(key, 3)
    lowest = 0.5
    norm_gain = rising(D, lowest) * jax.random.uniform(first_key, (D,), jnp.float32, 0.8, 1.2)
    gate_gain = rising(DI, lowest) * jax.random.uniform(second_key, (DI,), jnp.float32, 0.8, 1.2)
    conv_bias = jax.random.uniform(third_key, (CW,), jnp.float32, -0.5, 0.5)
    return jnp.concatenate([norm_gain, gate_gain, conv_bias])


def draw_head_params(key, part):
    key = jax.random.fold_in(key, 37)
    bias_key, rate_key, skip_key = jax.random.split(key, 3)
    dt_bias = jax.random.uniform(bias_key, (H,), jnp.float32, -6.0, -2.0)
    a_log = jax.random.uniform(rate_key, (H,), jnp.float32, -3.0, 1.5)
    skip_gain = jax.random.uniform(skip_key, (H,), jnp.float32, 0.5, 1.5)
    return jnp.stack([dt_bias, a_log, skip_gain])


def shard_levels(key, dims, cuts, smallest, largest):
    gain, own = 1.0, jax.random.fold_in(key, 6)
    for dim, blocks in cuts:
        heights = jnp.exp(jax.random.uniform(jax.random.fold_in(own, dim), (blocks,), jnp.float32, smallest / len(cuts), largest / len(cuts)))
        gain = gain * jnp.repeat(heights, dims[dim] // blocks).reshape([-1 if axis == dim else 1 for axis in range(len(dims))])
    return gain


def centred(key, shape, width, bound, cuts=(), held_as=jnp.bfloat16):
    values = jax.random.normal(key, shape, jnp.float32) * width
    if len(cuts) > 0:
        values = shard_levels(key, shape, cuts, -0.22, 0.18) * values
    return jnp.clip(values, min=-bound, max=bound).astype(held_as)


def setup_inputs(seed: int = 0) -> dict:
    streams_of = jax.random.split(jax.random.key(seed), 19)
    tokens = centred(streams_of[0], (N_REP, GROUP_TOK, D), 1.0, 6.0, ((0, 4), (1, 8)))
    cotangent = centred(streams_of[1], (N_REP, GROUP_TOK, D), 1.0, 6.0, ((0, 4), (1, 8)))
    seq_lengths = draw_seq_lengths(jax.random.fold_in(streams_of[18], 71), 0)
    in_weight = centred(streams_of[3], (D, PW), D ** -0.5, 0.21875, ((0, 32),), jnp.float32)
    in_first = centred(streams_of[4], (D, PW), (0.111 / NPAR ** 0.5), 0.0008544922, ((0, 32),), jnp.float32)
    in_second = jnp.clip(jnp.exp(math.log(5.5772151341670906e-08) - 1.3843914 * jax.random.uniform(streams_of[5], (D, PW), jnp.float32) ** shard_levels(streams_of[5], (D, PW), ((0, 32),), -0.2, 0.2)), 1.39695961465236e-08, 5.5772151341670906e-08)
    out_weight = centred(streams_of[6], (DI, D), DI ** -0.5, 0.15625, ((0, 32),), jnp.float32)
    out_first = centred(streams_of[7], (DI, D), (0.111 / NPAR ** 0.5), 0.0008544922, ((0, 32),), jnp.float32)
    out_second = jnp.clip(jnp.exp(math.log(5.5772151341670906e-08) - 1.3843914 * jax.random.uniform(streams_of[8], (DI, D), jnp.float32) ** shard_levels(streams_of[8], (DI, D), ((0, 32),), -0.2, 0.2)), 1.39695961465236e-08, 5.5772151341670906e-08)
    conv_weight = centred(streams_of[9], (4, CW), 4 ** -0.5, 3.0, ((1, 32),), jnp.float32)
    conv_first = centred(streams_of[10], (4, CW), (0.111 / NPAR ** 0.5), 0.0008544922, ((1, 32),), jnp.float32)
    conv_second = jnp.clip(jnp.exp(math.log(5.5772151341670906e-08) - 1.3843914 * jax.random.uniform(streams_of[11], (4, CW), jnp.float32) ** shard_levels(streams_of[11], (4, CW), ((1, 32),), -0.2, 0.2)), 1.39695961465236e-08, 5.5772151341670906e-08)
    vectors = draw_vectors(jax.random.fold_in(streams_of[18], 71), 0)
    vec_first = centred(streams_of[13], (D + DI + CW,), (0.444 / NPAR ** 0.5), 0.0034179688, ((0, 32),), jnp.float32)
    vec_second = jnp.clip(jnp.exp(math.log(8.950102596827492e-07) - 1.38926616 * jax.random.uniform(streams_of[14], (D + DI + CW,), jnp.float32) ** shard_levels(streams_of[14], (D + DI + CW,), ((0, 32),), -0.2, 0.2)), 2.2308860536668362e-07, 8.950102596827492e-07)
    head_params = draw_head_params(jax.random.fold_in(streams_of[18], 71), 0)
    head_first = centred(streams_of[16], (3, H), (0.444 / NPAR ** 0.5), 0.0034179688, (), jnp.float32)
    head_second = jnp.clip(jnp.exp(jax.random.uniform(streams_of[17], (3, H), jnp.float32, math.log(2.2308860536668362e-07), math.log(8.950102596827492e-07))), 2.2308860536668362e-07, 8.950102596827492e-07)
    return dict(tokens=tokens, cotangent=cotangent, seq_lengths=seq_lengths, in_weight=in_weight, in_first=in_first, in_second=in_second, out_weight=out_weight, out_first=out_first, out_second=out_second, conv_weight=conv_weight, conv_first=conv_first, conv_second=conv_second, vectors=vectors, vec_first=vec_first, vec_second=vec_second, head_params=head_params, head_first=head_first, head_second=head_second)


EPS_NORM = 1e-05
MAX_NORM = 1.0
BETA_ONE = 0.9
BETA_TWO = 0.95
ADAM_EPS = 1e-08
DECAY_MAT = 0.1
RATE_MAT = 0.05
RATE_CONV = 0.5
RATE_VEC = 1.0
RATE_HEAD = 2.0
PRECISE = lax.Precision.HIGHEST

@jax.custom_vjp
def low(v):
    return lax.optimization_barrier(v.astype(jnp.bfloat16)).astype(jnp.float32)

@jax.custom_vjp
def low_back(v):
    return v

def low_keep(v):
    return (low(v), None)

def low_pass(kept, grad):
    return (grad,)

def back_keep(v):
    return (v, None)

def back_low(kept, grad):
    return (low(grad),)
low.defvjp(low_keep, low_pass)
low_back.defvjp(back_keep, back_low)

def widen(values):
    return lax.optimization_barrier(values.astype(jnp.bfloat16)).astype(jnp.float32)

def seq_layout(seq_lengths, position):
    blocks = (seq_lengths + SPAN - 1) // SPAN
    seq_ends = SPAN * jnp.cumsum(blocks, axis=-1)
    begins = seq_ends - SPAN * blocks
    is_after = position[:, None] >= begins[..., None, :]
    inside = is_after & (position[:, None] < (begins + seq_lengths)[..., None, :])
    live_mask = lax.optimization_barrier(jnp.sum(inside.astype(jnp.int32), axis=-1)).astype(jnp.float32)
    seq_first = lax.optimization_barrier(jnp.max(jnp.where(is_after, begins[..., None, :], 0), axis=-1))
    starts_at = position[::SPAN]
    resets = jnp.any(starts_at[:, None] == begins[..., None, :], axis=-1).astype(jnp.float32)
    return (live_mask, seq_first, resets)

def forward(in_w, out_w, conv_w, vec_w, head_w, inputs, live_mask, seq_first, resets):
    norm_gain = vec_w[:D]
    gate_gain = vec_w[D:D + DI]
    conv_bias = vec_w[D + DI:]
    dt_bias = head_w[0]
    a_log = head_w[1]
    skip_gain = head_w[2]
    groups = inputs.shape[0]
    length = inputs.shape[1]
    factor = lax.rsqrt(lax.optimization_barrier(jnp.mean(inputs * inputs, axis=-1, keepdims=True)) + EPS_NORM)
    normed = low(inputs * factor * norm_gain)
    projected = low(low_back(jnp.einsum('rtd,dk->rtk', normed, in_w, precision=PRECISE)))
    gate_in = projected[..., :DI]
    conv_in = projected[..., DI:DI + CW]
    dt_raw = projected[..., DI + CW:]
    padded = jnp.pad(conv_in, ((0, 0), (3, 0), (0, 0)))
    position = jnp.arange(length, dtype=jnp.int32)
    summed = conv_bias
    for tap_index in range(4):
        valid_rows = (position - (3 - tap_index) >= seq_first).astype(jnp.float32)
        summed = summed + conv_w[tap_index] * padded[:, tap_index:tap_index + length] * valid_rows[..., None]
    activated = low(low_back(jax.nn.silu(summed)))
    x_values = activated[..., :DI].reshape(groups, length, H, P_SIZE)
    b_values = activated[..., DI:DI + NS]
    c_values = activated[..., DI + NS:]
    dt_values = live_mask[..., None] * jax.nn.softplus(dt_raw + dt_bias)
    log_decay = -jnp.exp(a_log) * dt_values

    def to_spans(values):
        shaped = values.reshape((groups, length // SPAN, SPAN) + values.shape[2:])
        return jnp.moveaxis(shaped, 1, 0)
    pieces = (to_spans(x_values), to_spans(b_values), to_spans(c_values), to_spans(log_decay), to_spans(dt_values), jnp.moveaxis(resets, 1, 0))
    lower_mask = jnp.arange(SPAN)[:, None] >= jnp.arange(SPAN)[None, :]

    def span_step(carried, piece):
        x_block, b_block, c_block, decay_block, dt_block, reset_block = piece
        cumul = jnp.cumsum(decay_block, axis=1)
        last_log = cumul[:, -1]
        scores = jnp.einsum('rtn,rsn->rts', c_block, b_block, precision=PRECISE)
        log_diffs = cumul[:, :, None, :] - cumul[:, None, :, :]
        decays = jnp.exp(jnp.where(lower_mask[None, :, :, None], log_diffs, -jnp.inf))
        mix_weights = low(low_back(scores[..., None] * decays * dt_block[:, None, :, :]))
        intra_part = jnp.einsum('rtsh,rshp->rthp', mix_weights, x_block, precision=PRECISE)
        incoming = (1.0 - reset_block)[:, None, None, None] * carried
        inter_part = jnp.exp(cumul)[..., None] * jnp.einsum('rtn,rhpn->rthp', c_block, incoming, precision=PRECISE)
        weights = jnp.exp(last_log[:, None, :] - cumul) * dt_block
        local_state = jnp.einsum('rshp,rsn->rhpn', x_block * weights[..., None], b_block, precision=PRECISE)
        return (jnp.exp(last_log)[..., None, None] * incoming + local_state, intra_part + inter_part)
    zero_state = jnp.zeros((groups, H, P_SIZE, NS), jnp.float32)
    _, outputs = lax.scan(jax.checkpoint(span_step), zero_state, pieces)
    ssd_rows = jnp.moveaxis(outputs, 0, 1).reshape(groups, length, H, P_SIZE)
    mixed_out = low_back((ssd_rows + skip_gain[:, None] * x_values).reshape(groups, length, DI))
    gated_rows = mixed_out * jax.nn.silu(gate_in)
    gate_factor = lax.rsqrt(lax.optimization_barrier(jnp.mean(gated_rows * gated_rows, axis=-1, keepdims=True)) + EPS_NORM)
    gated_low = low(gated_rows * gate_factor * gate_gain)
    branch = jnp.einsum('rtk,kd->rtd', gated_low, out_w, precision=PRECISE)
    return inputs + live_mask[..., None] * branch

def adam_step(master, clipped, first_m, second_m, step_rate, decay_rate):
    first_new = BETA_ONE * first_m + (1.0 - BETA_ONE) * clipped
    second_new = BETA_TWO * second_m + (1.0 - BETA_TWO) * clipped * clipped
    first_hat = first_new / (1.0 - BETA_ONE ** STEP)
    second_hat = second_new / (1.0 - BETA_TWO ** STEP)
    master_new = master - step_rate * (first_hat / (jnp.sqrt(second_hat) + ADAM_EPS) + decay_rate * master)
    return (first_new, second_new, master_new, master_new.astype(jnp.bfloat16))

def reference(tokens, cotangent, seq_lengths, in_weight, in_first, in_second, out_weight, out_first, out_second, conv_weight, conv_first, conv_second, vectors, vec_first, vec_second, head_params, head_first, head_second):
    position = jnp.arange(tokens.shape[1], dtype=jnp.int32)
    live_mask, seq_first, resets = seq_layout(seq_lengths, position)
    inputs = tokens.astype(jnp.float32)

    def run(in_w, out_w, conv_w, vec_w, head_w, rows_in):
        return forward(in_w, out_w, conv_w, vec_w, head_w, rows_in, live_mask, seq_first, resets)
    result, pullback = jax.vjp(run, widen(in_weight), widen(out_weight), widen(conv_weight), widen(vectors), head_params, inputs)
    in_grad, out_grad, conv_grad, vec_grad, head_grad, rows_grad = pullback(cotangent.astype(jnp.float32))
    norm_sq = jnp.sum(in_grad * in_grad) + jnp.sum(out_grad * out_grad) + jnp.sum(conv_grad * conv_grad) + jnp.sum(vec_grad * vec_grad) + jnp.sum(head_grad * head_grad)
    grad_norm = jnp.sqrt(norm_sq)
    factor = jnp.minimum(1.0, MAX_NORM / (grad_norm + 1e-06))
    in_clipped = in_grad * factor
    out_clipped = out_grad * factor
    conv_clipped = conv_grad * factor
    vec_clipped = vec_grad * factor
    head_clipped = head_grad * factor
    in_first_new, in_second_new, in_master, in_copy = adam_step(in_weight, in_clipped, in_first, in_second, RATE_MAT, DECAY_MAT)
    out_first_new, out_second_new, out_master, out_copy = adam_step(out_weight, out_clipped, out_first, out_second, RATE_MAT, DECAY_MAT)
    conv_first_new, conv_second_new, conv_master, conv_copy = adam_step(conv_weight, conv_clipped, conv_first, conv_second, RATE_CONV, DECAY_MAT)
    vec_first_new, vec_second_new, vec_master, vec_copy = adam_step(vectors, vec_clipped, vec_first, vec_second, RATE_VEC, 0.0)
    head_first_new, head_second_new, head_master, head_copy = adam_step(head_params, head_clipped, head_first, head_second, RATE_HEAD, 0.0)
    return (result.astype(jnp.bfloat16), rows_grad.astype(jnp.bfloat16), grad_norm, in_clipped, in_first_new, in_second_new, in_master, in_copy, out_clipped, out_first_new, out_second_new, out_master, out_copy, conv_clipped, conv_first_new, conv_second_new, conv_master, conv_copy, vec_clipped, vec_first_new, vec_second_new, vec_master, vec_copy, head_clipped, head_first_new, head_second_new, head_master, head_copy)
```

```python
from functools import partial

import jax
import jax.numpy as jnp
from jax import lax
from jax.experimental import pallas as pl
from jax.experimental.pallas import tpu as pltpu
from jax.sharding import PartitionSpec as P

SPAN = 256
HALF = 128
LANES = 128
STRIP = 256
TILE = 64
STEP = 10

EPS_NORM = 1e-05
MAX_NORM = 1.0
BETA_ONE = 0.9
BETA_TWO = 0.95
ADAM_EPS = 1e-08
DECAY_MAT = 0.1
RATE_MAT = 0.05
RATE_CONV = 0.5
RATE_VEC = 1.0
RATE_HEAD = 2.0
VMEM_BYTES = 56 * 1024 * 1024

f32 = jnp.float32
bf16 = jnp.bfloat16


def dot(a, b):
    return jnp.dot(a, b, preferred_element_type=f32)


def dot_nt(a, b):
    return lax.dot_general(a, b, (((1,), (1,)), ((), ())), preferred_element_type=f32)


def dot_tn(a, b):
    return lax.dot_general(a, b, (((0,), (0,)), ((), ())), preferred_element_type=f32)


def two_terms(v):
    high = v.astype(bf16)
    return high, (v - high.astype(f32)).astype(bf16)


def split_lanes(v):
    return jnp.concatenate(two_terms(v), axis=-1)


def exact_dot(ones_matrix, v):
    high, rest = two_terms(v)
    middle, low = two_terms(v - high.astype(f32))
    return dot(ones_matrix, high) + (dot(ones_matrix, middle) + dot(ones_matrix, low))


def head_sums(v, reducer):
    high, low = two_terms(v)
    return dot(high, reducer) + dot(low, reducer)


def sigmoid(v):
    return 0.5 * jnp.tanh(0.5 * v) + 0.5


def block_diag(pair):
    low_lanes = lax.broadcasted_iota(jnp.int32, pair.shape, 1) < LANES // 2
    none = jnp.zeros_like(pair)
    return jnp.concatenate(
        [jnp.where(low_lanes, pair, none), jnp.where(low_lanes, none, pair)], axis=0
    )


def eight_rows(v):
    return jnp.sum(v.reshape(v.shape[0] // 8, 8, v.shape[1]), axis=0)


def row_norm(rows, gain):
    wide = rows.astype(f32)
    factor = lax.rsqrt(jnp.mean(wide * wide, axis=-1, keepdims=True) + EPS_NORM)
    return (wide * factor * gain).astype(bf16)


def front_kernel(
    u_ref, before_ref, meta_ref, w_ref, gain_ref, taps_ref, bias_ref, heads_ref, ex_ref, tri_ref,
    normed_ref, conv_ref, act_ref, slope_ref, dt_ref, cum_ref, cumdev_ref, raw_ref, inc_ref,
    rim_ref, state_out_ref, total_ref,
    ext, state, offset,
    *, conv_dim, inner, places,
):
    step = pl.program_id(0)
    gain = gain_ref[...]
    keep = meta_ref[0:1, 3:4]

    @pl.when(step == 0)
    def _():
        rim = dot(row_norm(before_ref[...], gain), w_ref[:, :conv_dim]).astype(bf16)
        rim_ref[...] = rim
        ext[0:8, :] = rim[8:16].astype(f32) * keep
        state[...] = jnp.zeros_like(state)
        offset[...] = jnp.zeros_like(offset)

    @pl.when(step > 0)
    def _():
        ext[0:8, :] = ext[SPAN : SPAN + 8, :] * keep

    normed_ref[...] = row_norm(u_ref[...], gain)
    for s in range(0, conv_dim, STRIP):
        cols = slice(s, s + STRIP)
        piece = dot(normed_ref[...], w_ref[:, cols]).astype(bf16)
        conv_ref[:, cols] = piece
        ext[8 : 8 + SPAN, cols] = piece.astype(f32)
    raw = dot(normed_ref[...], w_ref[:, conv_dim : conv_dim + LANES]).astype(bf16).astype(f32)
    raw = raw + heads_ref[0:1, :]
    raw_ref[...] = raw
    dt_values = meta_ref[:, 0:1] * (jnp.maximum(raw, 0.0) + jnp.log1p(jnp.exp(-jnp.abs(raw))))
    dt_ref[...] = dt_values
    for s in range(0, conv_dim, STRIP):
        cols = slice(s, s + STRIP)
        for base in range(0, SPAN, TILE):
            total = bias_ref[0:1, cols]
            for k in range(4):
                total = total + taps_ref[k : k + 1, cols] * ext[base + 5 + k : base + 5 + k + TILE, cols]
            gate = sigmoid(total)
            value = total * gate
            act_ref[base : base + TILE, cols] = value.astype(bf16)
            slope_ref[base : base + TILE, cols] = (gate + value * (1.0 - gate)).astype(bf16)
    for c in range(SPAN // HALF):
        rows = slice(c * HALF, (c + 1) * HALF)
        dt_here = dt_values[rows]
        cumul = exact_dot(tri_ref[...], heads_ref[1:2, :] * dt_here)
        cum_ref[rows, :] = cumul
        cumdev_ref[rows, :] = offset[0:1, :] + cumul
        last = cumul[HALF - 1 : HALF]
        offset[...] = offset[...] + last
        keep_here = meta_ref[c * HALF : c * HALF + 1, 3:4]
        weights = split_lanes(jnp.exp(last - cumul) * dt_here)
        fade = split_lanes(jnp.broadcast_to(jnp.exp(last), (8, LANES)))
        b_rows = act_ref[rows, inner : inner + LANES]
        for s in range(0, inner, STRIP):
            cols = slice(s, s + STRIP)
            scaled = (act_ref[rows, cols].astype(f32) * dot(weights, ex_ref[:, cols])).astype(bf16)
            arrived = keep_here * state[:, cols]
            inc_ref[rows, cols] = arrived.astype(bf16)
            state[:, cols] = dot(fade, ex_ref[:, cols])[0:1] * arrived + dot_tn(b_rows, scaled)

    @pl.when(step == pl.num_programs(0) - 1)
    def _():
        state_out_ref[:, :inner] = state[...].astype(bf16)
        gain_row = jnp.exp(offset[0:1, :]) * meta_ref[SPAN - 1 : SPAN, 1:2]
        high, low = two_terms(jnp.broadcast_to(gain_row, (HALF, LANES)))
        place = lax.broadcasted_iota(jnp.int32, (HALF, LANES), 0) % (HALF // places)
        none = jnp.zeros_like(high)
        state_out_ref[:, inner:] = jnp.where(
            place == 0, high, jnp.where(place == 1, low, none)
        )
        total_ref[...] = offset[...]


def chain_kernel(states_ref, gains_ref, ex_ref, out_ref, *, reverse):
    places, rows, inner = out_ref.shape
    gains = jnp.concatenate([gains_ref[:, 0, :], gains_ref[:, 1, :]], axis=1)
    wide = dot(gains, ex_ref[...])
    running = jnp.zeros((rows, inner), f32)
    for k in range(places):
        at = places - 1 - k if reverse else k
        out_ref[at] = running.astype(bf16)
        running = wide[at : at + 1] * running + states_ref[at, :, :inner].astype(f32)


def intra_kernel(
    act_ref, dt_ref, cum_ref, inc_ref, normed_ref, w_ref, ex_ref, y_ref, gate_ref, *, inner
):
    for s in range(0, inner, STRIP):
        cols = slice(s, s + STRIP)
        gate_ref[:, cols] = dot(normed_ref[...], w_ref[:, cols]).astype(bf16)
    at_row = lax.broadcasted_iota(jnp.int32, (HALF, HALF), 0)
    at_col = lax.broadcasted_iota(jnp.int32, (HALF, HALF), 1)
    for c in range(SPAN // HALF):
        rows = slice(c * HALF, (c + 1) * HALF)
        b_rows = act_ref[rows, inner : inner + LANES]
        c_rows = act_ref[rows, inner + LANES : inner + 2 * LANES]
        scores = jnp.where(at_row >= at_col, dot_nt(c_rows, b_rows), 0.0)
        cumul = cum_ref[rows, :]
        across = cumul.T
        dt_split = split_lanes(dt_ref[rows, :])
        grown = split_lanes(jnp.exp(cumul))
        for s in range(0, inner, STRIP):
            cols = slice(s, s + STRIP)
            steps = (act_ref[rows, cols].astype(f32) * dot(dt_split, ex_ref[:, cols])).astype(bf16)
            inter = dot(c_rows, inc_ref[rows, cols]) * dot(grown, ex_ref[:, cols])
            for q in range(STRIP // LANES):
                mixes = []
                for h in (s // 64 + 2 * q, s // 64 + 2 * q + 1):
                    fall = jnp.minimum(cumul[:, h : h + 1] - across[h : h + 1, :], 0.0)
                    mixes.append((scores * jnp.exp(fall)).astype(bf16))
                lanes = slice(q * LANES, (q + 1) * LANES)
                y_ref[rows, s + q * LANES : s + (q + 1) * LANES] = (
                    dot(jnp.concatenate(mixes, axis=1), block_diag(steps[:, lanes]))
                    + inter[:, lanes]
                )


def gate_kernel(
    y_ref, act_ref, prefix_ref, cumdev_ref, meta_ref, gate_ref, w_ref, cot_ref, skip_ref, gain_ref,
    ex_ref, red_ref,
    low_ref, gm_ref, dgate_ref, back_ref, r_ref, gdev_ref, sums_ref,
    y_all, g_all, d_all, e_all, gdev,
    *, inner,
):
    step = pl.program_id(0)

    @pl.when(step == 0)
    def _():
        gdev[...] = jnp.zeros_like(gdev)
        sums_ref[...] = jnp.zeros_like(sums_ref)

    c_rows = act_ref[:, inner + LANES : inner + 2 * LANES]
    reach = split_lanes(jnp.exp(cumdev_ref[...]) * meta_ref[:, 1:2])
    back = (meta_ref[:, 0:1] * cot_ref[...].astype(f32)).astype(bf16)
    back_ref[...] = back
    tiles = [slice(base, base + TILE) for base in range(0, SPAN, TILE)]
    squares = [jnp.zeros((TILE, 1), f32) for _ in tiles]
    for s in range(0, inner, STRIP):
        cols = slice(s, s + STRIP)
        e_all[:, cols] = dot(reach, ex_ref[:, cols])
        y_all[:, cols] = dot(c_rows, prefix_ref[:, cols])
        d_all[:, cols] = dot_nt(back, w_ref[cols, :])
        for at, rows in enumerate(tiles):
            y = y_ref[rows, cols] + e_all[rows, cols] * y_all[rows, cols]
            y_all[rows, cols] = y
            z = gate_ref[rows, cols].astype(f32)
            mixed = y + skip_ref[0:1, cols] * act_ref[rows, cols].astype(f32)
            g = mixed * (z * sigmoid(z))
            g_all[rows, cols] = g
            squares[at] = squares[at] + jnp.sum(g * g, axis=1, keepdims=True)
    factors = [lax.rsqrt(v / inner + EPS_NORM) for v in squares]
    inner_sums = [jnp.zeros((TILE, 1), f32) for _ in tiles]
    for s in range(0, inner, STRIP):
        cols = slice(s, s + STRIP)
        gain = gain_ref[0:1, cols]
        gain_sum = jnp.zeros((8, STRIP), f32)
        for at, rows in enumerate(tiles):
            gn = g_all[rows, cols] * factors[at]
            g_all[rows, cols] = gn
            low_ref[rows, cols] = (gn * gain).astype(bf16)
            raw = d_all[rows, cols]
            gain_sum = gain_sum + eight_rows(raw * gn)
            d = raw * gain
            d_all[rows, cols] = d
            inner_sums[at] = inner_sums[at] + jnp.sum(d * gn, axis=1, keepdims=True)
        sums_ref[0:8, cols] = sums_ref[0:8, cols] + gain_sum
    means = [v / inner for v in inner_sums]
    r_parts = [jnp.zeros((TILE, LANES), f32) for _ in tiles]
    for s in range(0, inner, STRIP):
        cols = slice(s, s + STRIP)
        skip_sum = jnp.zeros((8, STRIP), f32)
        for at, rows in enumerate(tiles):
            dg = factors[at] * (d_all[rows, cols] - g_all[rows, cols] * means[at])
            z = gate_ref[rows, cols].astype(f32)
            sg = sigmoid(z)
            sl = z * sg
            x = act_ref[rows, cols].astype(f32)
            y = y_all[rows, cols]
            mixed = y + skip_ref[0:1, cols] * x
            gm_low = (dg * sl).astype(bf16)
            gm_ref[rows, cols] = gm_low
            dgate_ref[rows, cols] = (dg * mixed * (sg + sl * (1.0 - sg))).astype(bf16)
            gm = gm_low.astype(f32)
            skip_sum = skip_sum + eight_rows(gm * x)
            r_parts[at] = r_parts[at] + head_sums(gm * y, red_ref[cols, :])
            e_all[rows, cols] = gm * e_all[rows, cols]
        sums_ref[8:16, cols] = sums_ref[8:16, cols] + skip_sum
        gdev[:, cols] = gdev[:, cols] + dot_tn(c_rows, e_all[:, cols].astype(bf16))
    for at, rows in enumerate(tiles):
        r_ref[rows, :] = r_parts[at]

    @pl.when(step == pl.num_programs(0) - 1)
    def _():
        gdev_ref[...] = gdev[...].astype(bf16)


def intra_back_kernel(
    act_ref, gm_ref, dt_ref, cum_ref, cumdev_ref, meta_ref, inc_ref, prefix_ref, r_ref, ex_ref,
    red_ref, tri_up_ref,
    dx_ref, dbc_ref, xd_ref, da_ref,
    de, dlast,
    *, inner,
):
    @pl.when(pl.program_id(0) == 0)
    def _():
        de[...] = jnp.zeros_like(de)
        dlast[...] = jnp.zeros_like(dlast)

    at_row = lax.broadcasted_iota(jnp.int32, (HALF, HALF), 0)
    at_col = lax.broadcasted_iota(jnp.int32, (HALF, HALF), 1)
    upper = at_row <= at_col
    for c in reversed(range(SPAN // HALF)):
        rows = slice(c * HALF, (c + 1) * HALF)
        first = slice(c * HALF, c * HALF + 1)
        b_rows = act_ref[rows, inner : inner + LANES]
        c_rows = act_ref[rows, inner + LANES : inner + 2 * LANES]
        scores = jnp.where(upper, dot_nt(b_rows, c_rows), 0.0)
        cumul = cum_ref[rows, :]
        across = cumul.T
        last = cumul[HALF - 1 : HALF]
        dt_split = split_lanes(dt_ref[rows, :])
        grown = split_lanes(jnp.exp(cumul))
        left = split_lanes(jnp.exp(last - cumul))
        fade = split_lanes(jnp.broadcast_to(jnp.exp(last), (8, LANES)))
        start = jnp.exp(cumdev_ref[first, :] - cum_ref[first, :]) * meta_ref[first, 1:2]
        start = split_lanes(jnp.broadcast_to(start, (8, LANES)))
        keep = meta_ref[first, 3:4]
        d_scores = jnp.zeros((HALF, HALF), f32)
        d_c = jnp.zeros((HALF, LANES), f32)
        d_b = jnp.zeros((HALF, LANES), f32)
        x_dot = jnp.zeros((HALF, LANES), f32)
        d_end = jnp.zeros((8, LANES), f32)
        for s in range(0, inner, STRIP):
            cols = slice(s, s + STRIP)
            x = act_ref[rows, cols].astype(f32)
            left_wide = dot(left, ex_ref[:, cols])
            steps = (x * dot(dt_split, ex_ref[:, cols])).astype(bf16)
            gm = gm_ref[rows, cols]
            gm_grown = (gm.astype(f32) * dot(grown, ex_ref[:, cols])).astype(bf16)
            start_wide = dot(start, ex_ref[:, cols])[0:1]
            arrived = inc_ref[rows, cols].astype(f32) + start_wide * prefix_ref[:, cols].astype(f32)
            d_c = d_c + dot_nt(gm_grown, arrived.astype(bf16))
            de_here = de[:, cols]
            de_low = de_here.astype(bf16)
            dx_far = left_wide * dot(b_rows, de_low)
            d_b = d_b + dot_nt((steps.astype(f32) * left_wide).astype(bf16), de_low)
            for q in range(STRIP // LANES):
                lanes = slice(q * LANES, (q + 1) * LANES)
                gm_diag = block_diag(gm[:, lanes])
                d_mix = dot_nt(steps[:, lanes], gm_diag)
                mixes = []
                for k in range(2):
                    h = s // 64 + 2 * q + k
                    decay = jnp.exp(jnp.minimum(across[h : h + 1, :] - cumul[:, h : h + 1], 0.0))
                    mixes.append((scores * decay).astype(bf16))
                    d_scores = d_scores + d_mix[:, k * HALF : (k + 1) * HALF] * decay
                dx = dot(jnp.concatenate(mixes, axis=1), gm_diag) + dx_far[:, lanes]
                wide = slice(s + q * LANES, s + (q + 1) * LANES)
                dx_ref[rows, wide] = dx.astype(bf16)
                x_dot = x_dot + head_sums(x[:, lanes] * dx, red_ref[wide, :])
            de_new = keep * (
                dot_tn(c_rows, gm_grown) + dot(fade, ex_ref[:, cols])[0:1] * de_here
            )
            de[:, cols] = de_new
            d_end = d_end + head_sums(eight_rows(de_new * arrived), red_ref[cols, :])
        xd_ref[rows, :] = x_dot
        da_ref[rows, :] = (
            exact_dot(tri_up_ref[...], r_ref[rows, :] - dt_ref[rows, :] * x_dot) + dlast[0:1, :]
        )
        dlast[...] = jnp.broadcast_to(jnp.sum(d_end, axis=0, keepdims=True), dlast.shape)
        d_low = jnp.where(upper, d_scores, 0.0).astype(bf16)
        dbc_ref[rows, :LANES] = dot(d_low, c_rows) + d_b
        dbc_ref[rows, LANES:] = dot_tn(d_low, b_rows) + d_c


def outer_kernel(
    u_ref, meta_ref, low_ref, back_ref, normed_ref, dgate_ref, w_ref,
    out_ref, out_grad_ref, gate_grad_ref,
    out_sum, gate_sum,
):
    step = pl.program_id(0)

    @pl.when(step == 0)
    def _():
        out_sum[...] = jnp.zeros_like(out_sum)
        gate_sum[...] = jnp.zeros_like(gate_sum)

    branch = dot(low_ref[...], w_ref[...])
    out_ref[...] = (u_ref[...].astype(f32) + meta_ref[:, 0:1] * branch).astype(bf16)
    out_sum[...] = out_sum[...] + dot_tn(low_ref[...], back_ref[...])
    gate_sum[...] = gate_sum[...] + dot_tn(normed_ref[...], dgate_ref[...])

    @pl.when(step == pl.num_programs(0) - 1)
    def _():
        out_grad_ref[...] = out_sum[...].astype(bf16)
        gate_grad_ref[...] = gate_sum[...].astype(bf16)


def conv_back_kernel(
    act_ref, slope_ref, conv_ref, dx_ref, gm_ref, dbc_ref, dt_ref, cumdev_ref, raw_ref, xd_ref,
    da_ref, meta_ref, above_ref, prefix_ref, total_ref, pre_ref, skip_ref, taps_ref, heads_ref, rim_ref,
    ex_ref, red_ref, tri_ref,
    dconv_ref, first_ref, sums_ref, hsums_ref,
    fresh, kept, ext, dt_fresh, dt_kept, flow,
    *, inner, conv_dim, num_heads,
):
    step = pl.program_id(0)
    blocks = pl.num_programs(0) - 1
    keep = meta_ref[0:1, 3:4]

    @pl.when(step == 0)
    def _():
        ext[0:8, :] = rim_ref[8:16, :].astype(f32) * keep
        sums_ref[...] = jnp.zeros_like(sums_ref)
        hsums_ref[...] = jnp.zeros_like(hsums_ref)
        start = jnp.zeros((8, LANES), f32)
        for s in range(0, inner, STRIP):
            cols = slice(s, s + STRIP)
            both = above_ref[:, cols].astype(f32) * prefix_ref[:, cols].astype(f32)
            start = start + head_sums(eight_rows(both), red_ref[cols, :])
        start = jnp.sum(start, axis=0, keepdims=True)
        flow[...] = start * jnp.exp(total_ref[...]) * pre_ref[...]

    @pl.when((step > 0) & (step < blocks))
    def _():
        ext[0:8, :] = ext[SPAN : SPAN + 8, :] * keep

    @pl.when(step < blocks)
    def _():
        ext[8 : 8 + SPAN, :] = conv_ref[...].astype(f32)
        for c in range(SPAN // HALF):
            rows = slice(c * HALF, (c + 1) * HALF)
            b_rows = act_ref[rows, inner : inner + LANES]
            dt_here = dt_ref[rows, :]
            ahead = split_lanes(jnp.exp(total_ref[0:1, :] - cumdev_ref[rows, :]) * meta_ref[rows, 2:3])
            dt_split = split_lanes(dt_here)
            x_dot = jnp.zeros((HALF, LANES), f32)
            d_b = dbc_ref[rows, :LANES]
            for s in range(0, inner, STRIP):
                cols = slice(s, s + STRIP)
                x = act_ref[rows, cols].astype(f32)
                dt_wide = dot(dt_split, ex_ref[:, cols])
                ahead_wide = dot(ahead, ex_ref[:, cols])
                far = ahead_wide * dot(b_rows, above_ref[:, cols])
                dx = dt_wide * (dx_ref[rows, cols].astype(f32) + far)
                dx = dx + skip_ref[0:1, cols] * gm_ref[rows, cols].astype(f32)
                fresh[rows, cols] = dx * slope_ref[rows, cols].astype(f32)
                x_dot = x_dot + head_sums(x * far, red_ref[cols, :])
                d_b = d_b + dot_nt((x * dt_wide * ahead_wide).astype(bf16), above_ref[:, cols])
            b_cols = slice(inner, inner + LANES)
            c_cols = slice(inner + LANES, inner + 2 * LANES)
            fresh[rows, b_cols] = d_b * slope_ref[rows, b_cols].astype(f32)
            fresh[rows, c_cols] = dbc_ref[rows, LANES:] * slope_ref[rows, c_cols].astype(f32)
            passed = dt_here * x_dot
            da = da_ref[rows, :] + flow[0:1, :] + exact_dot(tri_ref[...], passed) - passed
            flow[...] = flow[...] + jnp.sum(passed, axis=0, keepdims=True)
            rate = heads_ref[1:2, :]
            hsums_ref[8:16, :] = hsums_ref[8:16, :] + eight_rows(da * rate * dt_here)
            d_dt = xd_ref[rows, :] + x_dot + rate * da
            d_raw = meta_ref[rows, 0:1] * sigmoid(raw_ref[rows, :]) * d_dt
            real = lax.broadcasted_iota(jnp.int32, d_raw.shape, 1) < num_heads
            d_raw = jnp.where(real, d_raw, 0.0)
            hsums_ref[0:8, :] = hsums_ref[0:8, :] + eight_rows(d_raw)
            dt_fresh[rows, :] = d_raw.astype(bf16)
        for s in range(0, conv_dim, STRIP):
            cols = slice(s, s + STRIP)
            sums = [jnp.zeros((8, STRIP), f32) for _ in range(5)]
            for base in range(0, SPAN, TILE):
                d = fresh[base : base + TILE, cols]
                sums[4] = sums[4] + eight_rows(d)
                for k in range(4):
                    sums[k] = sums[k] + eight_rows(d * ext[base + 5 + k : base + 5 + k + TILE, cols])
            for k in range(5):
                at = slice(8 * k, 8 * k + 8)
                sums_ref[at, cols] = sums_ref[at, cols] + sums[k]

    @pl.when(step == 0)
    def _():
        first_ref[...] = fresh[0:8, :] * keep

    @pl.when(step > 0)
    def _():
        inside = (step < blocks).astype(f32)
        kept[SPAN : SPAN + 8, :] = fresh[0:8, :] * (keep * inside)
        for s in range(0, conv_dim, STRIP):
            cols = slice(s, s + STRIP)
            for base in range(0, SPAN, TILE):
                total = taps_ref[3:4, cols] * kept[base : base + TILE, cols]
                for k in range(3):
                    total = total + taps_ref[k : k + 1, cols] * kept[base + 3 - k : base + 3 - k + TILE, cols]
                dconv_ref[base : base + TILE, cols] = total.astype(bf16)
        dconv_ref[:, conv_dim:] = dt_kept[...]

    kept[0:SPAN, :] = fresh[...]
    dt_kept[...] = dt_fresh[...]


def weight_grad_kernel(normed_ref, dconv_ref, small_ref, out_ref, total, *, conv_dim):
    step = pl.program_id(0)

    @pl.when(step == 0)
    def _():
        total[...] = jnp.zeros_like(total)

    total[...] = total[...] + dot_tn(normed_ref[...], dconv_ref[...])

    @pl.when(step == pl.num_programs(0) - 1)
    def _():
        width = total.shape[1]
        out_ref[:, :conv_dim] = total[:, :conv_dim].astype(bf16)
        out_ref[:, conv_dim:] = (total[:, conv_dim:] + small_ref[...]).astype(bf16)


def input_grad_kernel(
    dconv_ref, dgate_ref, wc_ref, wg_ref, u_ref, cot_ref, gain_ref, out_ref, sums_ref
):
    @pl.when(pl.program_id(0) == 0)
    def _():
        sums_ref[...] = jnp.zeros_like(sums_ref)

    grad = dot_nt(dconv_ref[...], wc_ref[...]) + dot_nt(dgate_ref[...], wg_ref[...])
    wide = u_ref[...].astype(f32)
    factor = lax.rsqrt(jnp.mean(wide * wide, axis=-1, keepdims=True) + EPS_NORM)
    unit = wide * factor
    sums_ref[...] = sums_ref[...] + eight_rows(grad * unit)
    d = grad * gain_ref[...]
    du = factor * (d - unit * jnp.mean(d * unit, axis=-1, keepdims=True))
    out_ref[...] = (cot_ref[...].astype(f32) + du).astype(bf16)


def adam_step(master, clipped, first_m, second_m, step_rate, decay_rate):
    first_new = BETA_ONE * first_m + (1.0 - BETA_ONE) * clipped
    second_new = BETA_TWO * second_m + (1.0 - BETA_TWO) * clipped * clipped
    first_hat = first_new / (1.0 - BETA_ONE**STEP)
    second_hat = second_new / (1.0 - BETA_TWO**STEP)
    master_new = master - step_rate * (
        first_hat / (jnp.sqrt(second_hat) + ADAM_EPS) + decay_rate * master
    )
    return (first_new, second_new, master_new, master_new.astype(jnp.bfloat16))


def shift(value, axis, steps):
    count = lax.axis_size(axis)
    initial, last = (max(0, -steps), min(count, count - steps))
    return lax.ppermute(value, axis, [(source, source + steps) for source in range(initial, last)])


def axis_bits(axis):
    return [(axis, 1 << k) for k in reversed(range(lax.axis_size(axis).bit_length() - 1))]


def swap(value, axis, bit):
    count = lax.axis_size(axis)
    return lax.ppermute(value, axis, [(k, k ^ bit) for k in range(count)])


def my_bit(axis, bit):
    return (lax.axis_index(axis) // bit) % 2


def gather_rows(shard):
    bits = axis_bits("seq") + axis_bits("rep")
    value = shard
    known = []
    for axis, bit in bits:
        other = swap(value, axis, bit)
        mine = my_bit(axis, bit)
        place = len(known)
        pair = jnp.where(
            mine == 0,
            jnp.stack([value, other], axis=place),
            jnp.stack([other, value], axis=place),
        )
        value = pair
        known.append((axis, bit))
    return value.reshape((-1,) + shard.shape[1:])


def scatter_sum(whole):
    bits = axis_bits("seq") + axis_bits("rep")
    count = lax.axis_size("seq") * lax.axis_size("rep")
    value = whole.reshape((2,) * len(bits) + (whole.shape[0] // count,) + whole.shape[1:])
    for axis, bit in reversed(bits):
        place = bits.index((axis, bit))
        mine = my_bit(axis, bit)
        given = lax.dynamic_index_in_dim(value, 1 - mine, place, keepdims=False)
        held = lax.dynamic_index_in_dim(value, mine, place, keepdims=False)
        got = swap(given, axis, bit)
        value = (held.astype(f32) + got.astype(f32)).astype(bf16)
        bits = bits[:place] + bits[place + 1 :]
    return value.astype(f32)


def call(kernel, grid, ins, in_blocks, outs, out_blocks, scratch, flops, **fixed):
    moved = sum(v.size * v.dtype.itemsize for v in ins) + sum(v.size * v.dtype.itemsize for v in outs)
    return pl.pallas_call(
        partial(kernel, **fixed),
        grid=(grid,),
        in_specs=in_blocks,
        out_specs=out_blocks,
        out_shape=outs,
        scratch_shapes=scratch,
        compiler_params=pltpu.CompilerParams(
            dimension_semantics=("arbitrary",), vmem_limit_bytes=VMEM_BYTES
        ),
        cost_estimate=pl.CostEstimate(flops=int(flops), bytes_accessed=moved, transcendentals=0),
    )(*ins)


def full(shape):
    return pl.BlockSpec(shape, lambda i: (0,) * len(shape))


def rows_of(count, width, index=lambda i: i):
    return pl.BlockSpec((count, width), lambda i: (index(i), 0))


def like(*shape, dtype=f32):
    return jax.ShapeDtypeStruct(shape, dtype)


def seq_meta(lengths, offset, row_count):
    blocks = (lengths + SPAN - 1) // SPAN
    seq_ends = SPAN * jnp.cumsum(blocks)
    begins = seq_ends - SPAN * blocks
    position = offset + jnp.arange(row_count, dtype=jnp.int32)
    is_after = position[:, None] >= begins[None, :]
    inside = is_after & (position[:, None] < (begins + lengths)[None, :])
    live = jnp.any(inside, axis=1)
    first = jnp.max(jnp.where(is_after, begins[None, :], 0), axis=1)
    chunk_start = position - position % HALF
    flags = [live, first < offset, first == first[-1], first < chunk_start]
    return jnp.stack([flag.astype(f32) for flag in flags] + [jnp.zeros_like(position, f32)] * 4, axis=1)


def shards(
    tokens,
    cotangent,
    seq_lengths,
    in_weight,
    in_first,
    in_second,
    out_weight,
    out_first,
    out_second,
    conv_weight,
    conv_first,
    conv_second,
    vectors,
    vec_first,
    vec_second,
    head_params,
    head_first,
    head_second,
):
    u = tokens[0]
    cot = cotangent[0]
    rows, model = u.shape
    ranks = lax.axis_size("seq") * lax.axis_size("rep")
    places = lax.axis_size("seq")
    own_rows = in_weight.shape[0]
    taps_own = conv_weight.shape[1]
    vecs_own = vectors.shape[0]
    conv_dim = taps_own * ranks
    inner = out_weight.shape[0] * ranks
    heads = head_params.shape[1]
    head_dim = inner // heads
    nblk = rows // SPAN
    spare = LANES - heads
    smalls = 4 * taps_own + vecs_own

    meta = seq_meta(seq_lengths[0], lax.axis_index("seq") * rows, rows)
    before = shift(u[rows - 16 :], "seq", 1)

    in_low = in_weight.astype(bf16)
    packed = jnp.concatenate([conv_weight.reshape(-1), vectors]).astype(bf16)
    packed = jnp.pad(packed, (0, own_rows * spare - smalls)).reshape(own_rows, spare)
    conv_shard = jnp.concatenate([in_low[:, inner:], packed], axis=1)
    w_conv = gather_rows(conv_shard)
    w_gate = lax.all_gather(in_low[:, :inner], ("seq", "rep"), axis=0, tiled=True)
    w_out = lax.all_gather(out_weight.astype(bf16), ("seq", "rep"), axis=0, tiled=True)

    small = w_conv[:, conv_dim + heads :].reshape(ranks, own_rows * spare).astype(f32)
    taps = small[:, : 4 * taps_own].reshape(ranks, 4, taps_own).transpose(1, 0, 2).reshape(4, conv_dim)
    vecs = small[:, 4 * taps_own : smalls].reshape(-1)
    norm_gain = vecs[None, :model]
    gate_gain = vecs[None, model : model + inner]
    conv_bias = vecs[None, model + inner :]
    head_rows = jnp.stack([head_params[0], -jnp.exp(head_params[1]), head_params[2]])
    head_rows = jnp.pad(head_rows, ((0, 5), (0, spare)))
    skip_wide = jnp.repeat(head_params[2], head_dim)[None]

    lane_head = jnp.arange(inner, dtype=jnp.int32) // head_dim
    spread = (jnp.arange(LANES, dtype=jnp.int32)[:, None] == lane_head[None]).astype(bf16)
    ex = jnp.concatenate([spread, spread], axis=0)
    red = (lane_head[:, None] == jnp.arange(LANES, dtype=jnp.int32)[None]).astype(bf16)
    order = jnp.arange(HALF, dtype=jnp.int32)
    tri = (order[:, None] >= order[None]).astype(bf16)
    tri_up = (order[:, None] <= order[None]).astype(bf16)

    wide = conv_dim + LANES
    b_act = rows_of(SPAN, conv_dim)
    b_in = rows_of(SPAN, inner)
    b_lane = rows_of(SPAN, LANES)
    b_model = rows_of(SPAN, model)
    b_meta = rows_of(SPAN, 8)
    b_ex = full((2 * LANES, inner))
    b_red = full((inner, LANES))
    b_tri = full((HALF, HALF))
    b_heads = full((8, LANES))
    lane_out = like(rows, LANES)

    (
        normed, conv_in, act, slope, dt_values, cumul, cumdev, raw, own_inc, rim, state_out, total
    ) = call(
        front_kernel,
        nblk,
        [u, before, meta, w_conv, norm_gain, taps, conv_bias, head_rows, ex, tri],
        [
            b_model, full((16, model)), b_meta, full((model, wide)), full((1, model)),
            full((4, conv_dim)), full((1, conv_dim)), b_heads, b_ex, b_tri,
        ],
        [
            like(rows, model, dtype=bf16), like(rows, conv_dim, dtype=bf16),
            like(rows, conv_dim, dtype=bf16), like(rows, conv_dim, dtype=bf16),
            lane_out, lane_out, lane_out, lane_out, like(rows, inner, dtype=bf16),
            like(16, conv_dim, dtype=bf16), like(LANES, inner + LANES, dtype=bf16), like(8, LANES),
        ],
        [
            b_model, b_act, b_act, b_act, b_lane, b_lane, b_lane, b_lane, b_in,
            full((16, conv_dim)), full((LANES, inner + LANES)), b_heads,
        ],
        [
            pltpu.VMEM((8 + SPAN, conv_dim), f32),
            pltpu.VMEM((LANES, inner), f32),
            pltpu.VMEM((8, LANES), f32),
        ],
        2 * rows * model * wide * 4,
        conv_dim=conv_dim,
        inner=inner,
        places=places,
    )

    def through(states, gains, reverse):
        whole = (places, LANES // places, inner)
        chained = call(
            chain_kernel, 1, [states, gains, ex],
            [full(states.shape), full(gains.shape), b_ex],
            [like(*whole, dtype=bf16)], [full(whole)], [], 1e7, reverse=reverse,
        )[0]
        return lax.all_to_all(chained, "seq", 0, 0, tiled=True).reshape(LANES, inner)

    arrived = lax.all_to_all(
        state_out.reshape(places, LANES // places, inner + LANES), "seq", 0, 0, tiled=True
    )
    gains = arrived[:, :2, inner:]
    prefix = through(arrived, gains, False)

    y_own, gate_in = call(
        intra_kernel,
        nblk,
        [act, dt_values, cumul, own_inc, normed, w_gate, ex],
        [b_act, b_lane, b_lane, b_in, b_model, full((model, inner)), b_ex],
        [like(rows, inner), like(rows, inner, dtype=bf16)],
        [b_in, b_in],
        [],
        2 * rows * model * inner * 4,
        inner=inner,
    )

    gated_low, grad_mixed, grad_gate, back_rows, r_sums, gdev, gate_sums = call(
        gate_kernel,
        nblk,
        [y_own, act, prefix, cumdev, meta, gate_in, w_out, cot, skip_wide, gate_gain, ex, red],
        [
            b_in, b_act, full((LANES, inner)), b_lane, b_meta, b_in, full((inner, model)), b_model,
            full((1, inner)), full((1, inner)), b_ex, b_red,
        ],
        [
            like(rows, inner, dtype=bf16), like(rows, inner, dtype=bf16), like(rows, inner, dtype=bf16),
            like(rows, model, dtype=bf16), lane_out, like(LANES, inner, dtype=bf16), like(16, inner),
        ],
        [b_in, b_in, b_in, b_model, b_lane, full((LANES, inner)), full((16, inner))],
        [pltpu.VMEM((SPAN, inner), f32)] * 4 + [pltpu.VMEM((LANES, inner), f32)],
        2 * rows * model * inner * 4,
        inner=inner,
    )

    above = through(
        lax.all_to_all(gdev.reshape(places, LANES // places, inner), "seq", 0, 0, tiled=True),
        gains, True,
    )

    flip = lambda i: nblk - 1 - i
    f_lane = rows_of(SPAN, LANES, flip)
    f_in = rows_of(SPAN, inner, flip)
    dx_own, dbc_own, xd_own, da_own = call(
        intra_back_kernel,
        nblk,
        [act, grad_mixed, dt_values, cumul, cumdev, meta, own_inc, prefix, r_sums, ex, red, tri_up],
        [
            rows_of(SPAN, conv_dim, flip), f_in, f_lane, f_lane, f_lane, rows_of(SPAN, 8, flip), f_in,
            full((LANES, inner)), f_lane, b_ex, b_red, b_tri,
        ],
        [like(rows, inner, dtype=bf16), like(rows, 2 * LANES), lane_out, lane_out],
        [f_in, rows_of(SPAN, 2 * LANES, flip), f_lane, f_lane],
        [pltpu.VMEM((LANES, inner), f32), pltpu.VMEM((8, LANES), f32)],
        2 * rows * model * inner * 6,
        inner=inner,
    )
    block_out, out_grad, gate_grad = call(
        outer_kernel,
        nblk,
        [u, meta, gated_low, back_rows, normed, grad_gate, w_out],
        [b_model, b_meta, b_in, b_model, b_model, b_in, full((inner, model))],
        [
            like(rows, model, dtype=bf16), like(inner, model, dtype=bf16),
            like(model, inner, dtype=bf16),
        ],
        [b_model, full((inner, model)), full((model, inner))],
        [pltpu.VMEM((inner, model), f32), pltpu.VMEM((model, inner), f32)],
        2 * rows * model * inner * 3,
    )
    out_sum = scatter_sum(out_grad)
    gate_sum = scatter_sum(gate_grad)

    capped = lambda i: jnp.minimum(i, nblk - 1)
    late = lambda i: jnp.maximum(i - 1, 0)
    c_lane = rows_of(SPAN, LANES, capped)
    c_in = rows_of(SPAN, inner, capped)
    c_act = rows_of(SPAN, conv_dim, capped)
    pre_last = jnp.broadcast_to(meta[rows - 1 :, 1:2], (8, LANES))
    dconv, first_rows, conv_sums, head_sum_rows = call(
        conv_back_kernel,
        nblk + 1,
        [
            act, slope, conv_in, dx_own, grad_mixed, dbc_own, dt_values, cumdev, raw, xd_own, da_own,
            meta, above, prefix, total, pre_last, skip_wide, taps, head_rows, rim, ex, red, tri,
        ],
        [
            c_act, c_act, c_act, c_in, c_in, rows_of(SPAN, 2 * LANES, capped), c_lane, c_lane, c_lane,
            c_lane, c_lane, rows_of(SPAN, 8, capped), full((LANES, inner)), full((LANES, inner)),
            b_heads, b_heads, full((1, inner)), full((4, conv_dim)), b_heads, full((16, conv_dim)),
            b_ex, b_red, b_tri,
        ],
        [
            like(rows, wide, dtype=bf16), like(8, conv_dim), like(40, conv_dim), like(16, LANES),
        ],
        [rows_of(SPAN, wide, late), full((8, conv_dim)), full((40, conv_dim)), full((16, LANES))],
        [
            pltpu.VMEM((SPAN, conv_dim), f32),
            pltpu.VMEM((SPAN + 8, conv_dim), f32),
            pltpu.VMEM((SPAN + 8, conv_dim), f32),
            pltpu.VMEM((SPAN, LANES), bf16),
            pltpu.VMEM((SPAN, LANES), bf16),
            pltpu.VMEM((8, LANES), f32),
        ],
        2 * rows * model * inner * 3,
        inner=inner,
        conv_dim=conv_dim,
        num_heads=heads,
    )

    after = shift(first_rows, "seq", -1)
    late_rows = jnp.stack(
        [sum(taps[k] * after[j - k] for k in range(j + 1)) for j in range(3)]
    )
    tail = dconv[rows - 16 :, :conv_dim].astype(f32) + jnp.pad(late_rows, ((13, 0), (0, 0)))
    dconv = lax.dynamic_update_slice(dconv, tail.astype(bf16), (rows - 16, 0))

    input_grad, norm_sums = call(
        input_grad_kernel,
        nblk,
        [dconv, grad_gate, w_conv, w_gate, u, cot, norm_gain],
        [
            rows_of(SPAN, wide), b_in, full((model, wide)), full((model, inner)), b_model, b_model,
            full((1, model)),
        ],
        [like(rows, model, dtype=bf16), like(8, model)],
        [b_model, full((8, model))],
        [],
        2 * rows * model * (wide + inner),
    )

    grad_taps = jnp.sum(conv_sums.reshape(5, 8, conv_dim), axis=1)
    grad_vecs = jnp.concatenate(
        [jnp.sum(norm_sums, axis=0), jnp.sum(gate_sums[:8], axis=0), grad_taps[4]]
    )
    grad_skip = jnp.sum(jnp.sum(gate_sums[8:], axis=0).reshape(heads, head_dim), axis=1)
    head_local = jnp.concatenate(
        [
            jnp.sum(head_sum_rows.reshape(2, 8, LANES), axis=1)[:, :heads].reshape(-1),
            grad_skip,
        ]
    )
    small_grads = jnp.concatenate(
        [
            grad_taps[:4].reshape(4, ranks, taps_own).transpose(1, 0, 2).reshape(ranks, 4 * taps_own),
            grad_vecs.reshape(ranks, vecs_own),
        ],
        axis=1,
    )
    small_grads = jnp.pad(small_grads, ((0, 0), (0, own_rows * spare - smalls)))
    small_grads = jnp.pad(small_grads.reshape(model, spare), ((0, 0), (heads, 0)))
    conv_grad = call(
        partial(weight_grad_kernel, conv_dim=conv_dim),
        nblk,
        [normed, dconv, small_grads],
        [b_model, rows_of(SPAN, wide), full((model, LANES))],
        [like(model, wide, dtype=bf16)],
        [full((model, wide))],
        [pltpu.VMEM((model, wide), f32)],
        2 * rows * model * wide,
    )[0]
    conv_all = scatter_sum(conv_grad)

    in_sum = jnp.concatenate([gate_sum, conv_all[:, : conv_dim + heads]], axis=1)
    small_sum = conv_all[:, conv_dim + heads :].reshape(-1)
    conv_sum = small_sum[: 4 * taps_own].reshape(4, taps_own)
    vec_sum = small_sum[4 * taps_own : smalls]
    owned_sq = (
        jnp.sum(in_sum * in_sum)
        + jnp.sum(out_sum * out_sum)
        + jnp.sum(conv_sum * conv_sum)
        + jnp.sum(vec_sum * vec_sum)
    )
    row = jnp.concatenate([head_local, owned_sq[None]])
    row = jnp.pad(row, (0, LANES - row.shape[0]))
    all_rows = lax.all_to_all(
        jnp.broadcast_to(row[None, None], (ranks, 1, LANES)), ("seq", "rep"), 0, 0, tiled=True
    )
    summed = jnp.sum(all_rows, axis=(0, 1))
    head_sum = summed[: 3 * heads].reshape(3, heads)
    norm_sq = summed[3 * heads] + jnp.sum(head_sum * head_sum)
    grad_norm = jnp.sqrt(norm_sq)
    factor = jnp.minimum(1.0, MAX_NORM / (grad_norm + 1e-06))
    results = [block_out[None], input_grad[None], grad_norm]
    for summed_grad, master, first, second, rate, decay in (
        (in_sum, in_weight, in_first, in_second, RATE_MAT, DECAY_MAT),
        (out_sum, out_weight, out_first, out_second, RATE_MAT, DECAY_MAT),
        (conv_sum, conv_weight, conv_first, conv_second, RATE_CONV, DECAY_MAT),
        (vec_sum, vectors, vec_first, vec_second, RATE_VEC, 0.0),
        (head_sum, head_params, head_first, head_second, RATE_HEAD, 0.0),
    ):
        clipped = summed_grad * factor
        results.append(clipped)
        results.extend(adam_step(master, clipped, first, second, rate, decay))
    return tuple(results)


def solution(mesh):
    tokens = P("rep", "seq", None)
    row_split = P(("seq", "rep"), None)
    column_split = P(None, ("seq", "rep"))
    flat_split = P(("seq", "rep"))
    return jax.shard_map(
        shards,
        mesh=mesh,
        in_specs=(tokens, tokens, P("rep", None))
        + (row_split,) * 6
        + (column_split,) * 3
        + (flat_split,) * 3
        + (P(),) * 3,
        out_specs=(tokens, tokens, P())
        + (row_split,) * 10
        + (column_split,) * 5
        + (flat_split,) * 5
        + (P(),) * 5,
        check_vma=False,
    )
```

```python
import jax
import jax.numpy as jnp
import numpy as np
from jax import lax
from jax.experimental import pallas as pl
from jax.experimental.pallas import tpu as pltpu
from jax.sharding import PartitionSpec as P

SPAN = 256
HALF = 128
LANES = 128
STRIP = 256
TILE = 64
STEP = 10

EPS_NORM = 1e-05
MAX_NORM = 1.0
BETA_ONE = 0.9
BETA_TWO = 0.95
ADAM_EPS = 1e-08
DECAY_MAT = 0.1
RATE_MAT = 0.05
RATE_CONV = 0.5
RATE_VEC = 1.0
RATE_HEAD = 2.0
LOG2E = 1.4426950408889634
VMEM_BYTES = 58 * 1024 * 1024

f32 = jnp.float32
bf16 = jnp.bfloat16


def dot(a, b):
    return jnp.dot(a, b, preferred_element_type=f32)


def dot_nt(a, b):
    return lax.dot_general(a, b, (((1,), (1,)), ((), ())), preferred_element_type=f32)


def dot_tn(a, b):
    return lax.dot_general(a, b, (((0,), (0,)), ((), ())), preferred_element_type=f32)


def two_terms(v):
    high = v.astype(bf16)
    return high, (v - high.astype(f32)).astype(bf16)


def split_lanes(v):
    return jnp.concatenate(two_terms(v), axis=-1)


def exact_dot(ones_matrix, v):
    high, rest = two_terms(v)
    middle, low = two_terms(v - high.astype(f32))
    return dot(ones_matrix, high) + (dot(ones_matrix, middle) + dot(ones_matrix, low))


def sigmoid(v):
    return 0.5 * jnp.tanh(0.5 * v) + 0.5


def low_half(shape):
    return lax.broadcasted_iota(jnp.int32, shape, 1) < LANES // 2


def block_diag(pair):
    low_lanes = low_half(pair.shape)
    none = jnp.zeros_like(pair)
    return jnp.concatenate(
        [jnp.where(low_lanes, pair, none), jnp.where(low_lanes, none, pair)], axis=0
    )


def column(v, h):
    return jnp.broadcast_to(v[:, h : h + 1], (v.shape[0], LANES))


def eight_rows(v):
    return jnp.sum(v.reshape(v.shape[0] // 8, 8, v.shape[1]), axis=0)


def row_norm(rows, gain):
    wide = rows.astype(f32)
    factor = lax.rsqrt(jnp.mean(wide * wide, axis=-1, keepdims=True) + EPS_NORM)
    return (wide * factor * gain).astype(bf16)


def strips_of(width):
    return [(j, slice(j * LANES, (j + 1) * LANES)) for j in range(width // LANES)]


def shifted_sum(taps_ref, lanes, source, q, start, total):
    for k in range(4):
        total = total + taps_ref[k : k + 1, lanes] * source[q, pl.ds(start + k, TILE), :]
    return total


def front_kernel(
    lengths_ref, offset_ref, u_ref, before_ref, near_ref, far_ref, gain_ref, taps_ref, bias_ref, heads_ref,
    ex_ref, tri_ref,
    unit_ref, normed_ref, conv_ref, act_ref, slope_ref, meta_ref, dt_ref, cum_ref, cumdev_ref, raw_ref,
    inc_ref, start_ref, rim_ref, rim_unit_ref, state_out_ref, total_ref,
    state, offset, *ext,
    conv_dim, inner, places, num_rows,
):
    step = pl.program_id(0)
    gain = gain_ref[...]
    cut = near_ref.shape[1]

    device_start = offset_ref[0, 0]
    row = lax.broadcasted_iota(jnp.int32, (SPAN, 8), 0)
    flag = lax.broadcasted_iota(jnp.int32, (SPAN, 8), 1)
    position = device_start + step * SPAN + row
    begin = jnp.int32(0)
    first = jnp.zeros((SPAN, 8), jnp.int32)
    last_first = jnp.int32(0)
    live = jnp.zeros((SPAN, 8), jnp.bool_)
    for k in range(lengths_ref.shape[1]):
        length = lengths_ref[0, k]
        after = position >= begin
        first = jnp.where(after, begin, first)
        last_first = jnp.where(device_start + num_rows - 1 >= begin, begin, last_first)
        live = live | (after & (position < begin + length))
        begin = begin + (length + SPAN - 1) // SPAN * SPAN
    meta = jnp.where(
        flag == 0,
        live.astype(f32),
        jnp.where(
            flag == 1,
            (first < device_start).astype(f32),
            jnp.where(
                flag == 2,
                (first == last_first).astype(f32),
                (first < position - (row & (HALF - 1))).astype(f32),
            ),
        ),
    )
    meta_ref[...] = meta
    keep = meta[0:1, 3:4]

    @pl.when(step == 0)
    def _():
        normed_rim = row_norm(before_ref[...], gain)
        rim_unit_ref[...] = row_norm(before_ref[...], 1.0)
        rim = jnp.concatenate(
            [dot(normed_rim, near_ref[...]), dot(normed_rim, far_ref[:, : conv_dim - cut])], axis=1
        ).astype(bf16)
        rim_ref[...] = rim
        for j, lanes in strips_of(conv_dim):
            ext[j // 2][j % 2, 0:8, :] = rim[8:16, lanes].astype(f32) * keep
        state[...] = jnp.zeros_like(state)
        offset[...] = jnp.zeros_like(offset)

    @pl.when(step > 0)
    def _():
        for part in ext:
            part[:, 0:8, :] = part[:, SPAN : SPAN + 8, :] * keep

    wide_u = u_ref[...].astype(f32)
    unit = wide_u * lax.rsqrt(jnp.mean(wide_u * wide_u, axis=-1, keepdims=True) + EPS_NORM)
    unit_ref[...] = unit.astype(bf16)
    normed_ref[...] = (unit * gain).astype(bf16)
    raw = dot(normed_ref[...], far_ref[:, conv_dim - cut :]).astype(bf16).astype(f32)
    raw = raw + heads_ref[0:1, :]
    raw_ref[...] = raw
    dt_values = meta[:, 0:1] * (jnp.maximum(raw, 0.0) + jnp.log1p(jnp.exp(-jnp.abs(raw))))
    dt_ref[...] = dt_values

    parts, fades, starts = [], [], []
    for c in range(SPAN // HALF):
        rows = slice(c * HALF, (c + 1) * HALF)
        dt_here = dt_values[rows]
        cumul = exact_dot(tri_ref[...], heads_ref[1:2, :] * dt_here)
        cum_ref[rows, :] = cumul
        cumdev_ref[rows, :] = offset[0:1, :] + cumul
        last = cumul[HALF - 1 : HALF]
        parts.append(jnp.exp(last - cumul) * dt_here)
        fades.append(jnp.broadcast_to(jnp.exp(last), (8, LANES)))
        starts.append(jnp.exp(offset[...]) * meta[c * HALF : c * HALF + 1, 1:2])
        offset[...] = offset[...] + last
    spread = split_lanes(jnp.concatenate(parts + fades + starts, axis=0))
    origin = pl.multiple_of(offset_ref[0, 1], 8)

    def project(s):
        part = ext[s // STRIP]
        w_here = near_ref[:, s : s + STRIP] if s < cut else far_ref[:, s - cut : s - cut + STRIP]
        piece = dot(normed_ref[...], w_here).astype(bf16)
        conv_ref[:, s : s + STRIP] = piece
        for q in range(STRIP // LANES):
            part[q, 8 : 8 + SPAN, :] = piece[:, q * LANES : (q + 1) * LANES].astype(f32)

    def activate(s):
        part = ext[s // STRIP]
        for q in range(STRIP // LANES):
            lanes = slice(s + q * LANES, s + (q + 1) * LANES)
            for base in range(0, SPAN, TILE):
                half = shifted_sum(taps_ref, lanes, part, q, origin + base + 5, bias_ref[0:1, lanes])
                turn = jnp.tanh(half)
                value = half + half * turn
                act_ref[base : base + TILE, lanes] = value.astype(bf16)
                slope_ref[base : base + TILE, lanes] = (
                    (1.0 + value) + turn * (1.0 - value)
                ).astype(bf16)

    def accumulate(s):
        cols = slice(s, s + STRIP)
        wide = dot(spread, ex_ref[:, cols])
        start_ref[:, cols] = wide[SPAN + 16 :]
        for c in range(SPAN // HALF):
            rows = slice(c * HALF, (c + 1) * HALF)
            b_rows = act_ref[rows, inner : inner + LANES]
            scaled = (act_ref[rows, cols].astype(f32) * wide[rows]).astype(bf16)
            arrived = meta[c * HALF : c * HALF + 1, 3:4] * state[:, cols]
            inc_ref[rows, cols] = arrived.astype(bf16)
            fade = wide[SPAN + 8 * c : SPAN + 8 * c + 1]
            state[:, cols] = fade * arrived + dot_tn(b_rows, scaled)

    order = [inner] + list(range(0, inner, STRIP))
    for k in range(len(order) + 2):
        if k < len(order):
            project(order[k])
        if 2 <= k and order[k - 2] != inner:
            accumulate(order[k - 2])
        if 1 <= k <= len(order):
            activate(order[k - 1])

    @pl.when(step == pl.num_programs(0) - 1)
    def _():
        state_out_ref[:, :inner] = state[...].astype(bf16)
        gain_row = jnp.exp(offset[0:1, :]) * meta[SPAN - 1 : SPAN, 1:2]
        high, low = two_terms(jnp.broadcast_to(gain_row, (HALF, LANES)))
        place = lax.broadcasted_iota(jnp.int32, (HALF, LANES), 0) % (HALF // places)
        none = jnp.zeros_like(high)
        state_out_ref[:, inner:] = jnp.where(
            place == 0, high, jnp.where(place == 1, low, none)
        )
        total_ref[...] = offset[...]


def chain_kernel(states_ref, gains_ref, ex_ref, out_ref, *, reverse):
    places, rows, inner = out_ref.shape
    gains = jnp.concatenate([gains_ref[:, 0, :], gains_ref[:, 1, :]], axis=1)
    wide = dot(gains, ex_ref[...])
    running = jnp.zeros((rows, inner), f32)
    for k in range(places):
        at = places - 1 - k if reverse else k
        out_ref[at] = running.astype(bf16)
        running = wide[at : at + 1] * running + states_ref[at, :, :inner].astype(f32)


def project_kernel(
    normed_ref, meta_ref, cot_ref, wo_ref, *refs, inner
):
    gate_ref, gg_ref, back_ref = refs[-3:]
    width = refs[0].shape[1]
    back = (meta_ref[:, 0:1] * cot_ref[...].astype(f32)).astype(bf16)
    back_ref[...] = back
    for s in range(0, inner, STRIP):
        cols = slice(s, s + STRIP)
        w_here = refs[s // width][:, s % width : s % width + STRIP]
        gate_ref[:, cols] = dot(normed_ref[...], w_here).astype(bf16)
        gg_ref[:, cols] = dot_nt(back, wo_ref[cols, :]).astype(bf16)


def intra_kernel(act_ref, dt_ref, cum_ref, inc_ref, y_ref, *, inner):
    at_row = lax.broadcasted_iota(jnp.int32, (HALF, HALF), 0)
    at_col = lax.broadcasted_iota(jnp.int32, (HALF, HALF), 1)
    first_head = low_half((HALF, LANES))
    for c in range(SPAN // HALF):
        rows = slice(c * HALF, (c + 1) * HALF)
        b_rows = act_ref[rows, inner : inner + LANES]
        c_rows = act_ref[rows, inner + LANES : inner + 2 * LANES]
        scores = jnp.where(at_row >= at_col, dot_nt(c_rows, b_rows), 0.0)
        cumul = LOG2E * cum_ref[rows, :]
        dt_here = dt_ref[rows, :]
        across = cumul.T
        for s in range(0, inner, STRIP):
            inter = dot(c_rows, inc_ref[rows, s : s + STRIP])
            for q in range(STRIP // LANES):
                wide = slice(s + q * LANES, s + (q + 1) * LANES)
                h = s // 64 + 2 * q
                falls = [column(cumul, h), column(cumul, h + 1)]
                mixes = [
                    (scores * jnp.exp2(jnp.minimum(fall - across[h + k : h + k + 1, :], 0.0))).astype(bf16)
                    for k, fall in enumerate(falls)
                ]
                grown = jnp.exp2(jnp.where(first_head, falls[0], falls[1]))
                dt_wide = jnp.where(first_head, column(dt_here, h), column(dt_here, h + 1))
                steps = (act_ref[rows, wide].astype(f32) * dt_wide).astype(bf16)
                y_ref[rows, wide] = (
                    dot(jnp.concatenate(mixes, axis=1), block_diag(steps))
                    + inter[:, q * LANES : (q + 1) * LANES] * grown
                )


def gate_kernel(
    y_ref, act_ref, prefix_ref, cumdev_ref, meta_ref, gate_ref, gg_ref, skip_ref, gain_ref,
    ex_ref, red_ref,
    low_ref, gm_ref, dgate_ref, r_ref, gdev_ref, sums_ref,
    y_all, g_all, d_all, s_all, t_all, e_all, v_all, gdev,
    *, inner,
):
    step = pl.program_id(0)

    @pl.when(step == 0)
    def _():
        gdev[...] = jnp.zeros_like(gdev)
        sums_ref[...] = jnp.zeros_like(sums_ref)

    c_rows = act_ref[:, inner + LANES : inner + 2 * LANES]
    reach = split_lanes(jnp.exp(cumdev_ref[...]) * meta_ref[:, 1:2])
    tiles = [slice(base, base + TILE) for base in range(0, SPAN, TILE)]
    squares = [jnp.zeros((TILE, 1), f32) for _ in tiles]
    for s in range(0, inner, STRIP):
        cols = slice(s, s + STRIP)
        reached = dot(reach, ex_ref[:, cols])
        e_all[:, cols] = reached.astype(bf16)
        from_prefix = dot(c_rows, prefix_ref[:, cols])
        for at, rows in enumerate(tiles):
            y = y_ref[rows, cols] + reached[rows] * from_prefix[rows]
            y_all[rows, cols] = y
            z = gate_ref[rows, cols].astype(f32)
            mixed = y + skip_ref[0:1, cols] * act_ref[rows, cols].astype(f32)
            half = 0.5 * z
            turn = jnp.tanh(half)
            raised = 1.0 + turn
            sl = half * raised
            g = mixed * sl
            g_all[rows, cols] = g
            s_all[rows, cols] = sl
            t_all[rows, cols] = mixed * (raised + sl * (1.0 - turn))
            squares[at] = squares[at] + jnp.sum(g * g, axis=1, keepdims=True)
    factors = [lax.rsqrt(v / inner + EPS_NORM) for v in squares]
    inner_sums = [jnp.zeros((TILE, 1), f32) for _ in tiles]
    for s in range(0, inner, STRIP):
        cols = slice(s, s + STRIP)
        gain = gain_ref[0:1, cols]
        gain_sum = jnp.zeros((8, STRIP), f32)
        for at, rows in enumerate(tiles):
            gn = g_all[rows, cols] * factors[at]
            g_all[rows, cols] = gn
            low_ref[rows, cols] = (gn * gain).astype(bf16)
            raw = gg_ref[rows, cols].astype(f32)
            both = raw * gn
            gain_sum = gain_sum + eight_rows(both)
            d_all[rows, cols] = raw * gain
            inner_sums[at] = inner_sums[at] + jnp.sum(both * gain, axis=1, keepdims=True)
        sums_ref[:, cols] = sums_ref[:, cols] + gain_sum
    means = [v / inner for v in inner_sums]
    for s in range(0, inner, STRIP):
        cols = slice(s, s + STRIP)
        for at, rows in enumerate(tiles):
            dg = factors[at] * (d_all[rows, cols] - g_all[rows, cols] * means[at])
            gm = dg * s_all[rows, cols]
            gm_low = gm.astype(bf16)
            gm_ref[rows, cols] = gm_low
            dgate_ref[rows, cols] = (dg * t_all[rows, cols]).astype(bf16)
            v_all[rows, cols] = (gm_low.astype(f32) * y_all[rows, cols]).astype(bf16)
            e_all[rows, cols] = gm_low * e_all[rows, cols]
        gdev[:, cols] = gdev[:, cols] + dot_tn(c_rows, e_all[:, cols])
    r_ref[...] = dot(v_all[...], red_ref[...])

    @pl.when(step == pl.num_programs(0) - 1)
    def _():
        gdev_ref[...] = gdev[...].astype(bf16)


def intra_back_kernel(
    act_ref, gm_ref, dt_ref, cum_ref, meta_ref, inc_ref, start_ref, prefix_ref, r_ref,
    red_ref, tri_up_ref,
    dx_ref, dbc_ref, xd_ref, da_ref, skip_ref,
    de, dlast, v_all,
    *, inner,
):
    @pl.when(pl.program_id(0) == 0)
    def _():
        de[...] = jnp.zeros_like(de)
        dlast[...] = jnp.zeros_like(dlast)
        skip_ref[...] = jnp.zeros_like(skip_ref)

    at_row = lax.broadcasted_iota(jnp.int32, (HALF, HALF), 0)
    at_col = lax.broadcasted_iota(jnp.int32, (HALF, HALF), 1)
    first_head = low_half((HALF, LANES))
    upper = at_row <= at_col
    halves = SPAN // HALF
    for c in reversed(range(halves)):
        rows = slice(c * HALF, (c + 1) * HALF)
        b_rows = act_ref[rows, inner : inner + LANES]
        c_rows = act_ref[rows, inner + LANES : inner + 2 * LANES]
        scores = jnp.where(upper, dot_nt(b_rows, c_rows), 0.0)
        cumul = LOG2E * cum_ref[rows, :]
        dt_here = dt_ref[rows, :]
        across = cumul.T
        keep = meta_ref[c * HALF : c * HALF + 1, 3:4]
        d_scores = jnp.zeros((HALF, HALF), f32)
        d_c = jnp.zeros((HALF, LANES), f32)
        d_b = jnp.zeros((HALF, LANES), f32)
        for s in range(0, inner, STRIP):
            cols = slice(s, s + STRIP)
            pairs = [(q, s // 64 + 2 * q, slice(s + q * LANES, s + (q + 1) * LANES)) for q in range(2)]
            falls = [[column(cumul, h), column(cumul, h + 1)] for _, h, _ in pairs]
            cum_wide = jnp.concatenate(
                [jnp.where(first_head, a, b) for a, b in falls], axis=1
            )
            grown = jnp.exp2(cum_wide)
            left = jnp.exp2(cum_wide[HALF - 1 : HALF] - cum_wide)
            dt_wide = jnp.concatenate(
                [jnp.where(first_head, column(dt_here, h), column(dt_here, h + 1)) for _, h, _ in pairs],
                axis=1,
            )
            x = act_ref[rows, cols].astype(f32)
            gm = gm_ref[rows, cols]
            gm_wide = gm.astype(f32)
            skip_ref[:, cols] = skip_ref[:, cols] + eight_rows(gm_wide * x)
            steps_wide = x * dt_wide
            steps = steps_wide.astype(bf16)
            gm_grown = (gm_wide * grown).astype(bf16)
            arrived = inc_ref[rows, cols].astype(f32) + start_ref[8 * c : 8 * c + 1, cols] * prefix_ref[
                :, cols
            ].astype(f32)
            d_c = d_c + dot_nt(gm_grown, arrived.astype(bf16))
            de_here = de[:, cols]
            de_low = de_here.astype(bf16)
            dx_far = left * dot(b_rows, de_low)
            d_b = d_b + dot_nt((steps_wide * left).astype(bf16), de_low)
            for (q, h, wide), fall in zip(pairs, falls):
                lanes = slice(q * LANES, (q + 1) * LANES)
                gm_diag = block_diag(gm[:, lanes])
                d_mix = dot_nt(steps[:, lanes], gm_diag)
                mixes = []
                for k in range(2):
                    decay = jnp.exp2(jnp.minimum(across[h + k : h + k + 1, :] - fall[k], 0.0))
                    mixes.append((scores * decay).astype(bf16))
                    d_scores = d_scores + d_mix[:, k * HALF : (k + 1) * HALF] * decay
                dx = dot(jnp.concatenate(mixes, axis=1), gm_diag) + dx_far[:, lanes]
                dx_ref[rows, wide] = dx.astype(bf16)
                high, low = two_terms(x[:, lanes] * dx)
                v_all[rows, wide] = high
                v_all[SPAN + c * HALF : SPAN + (c + 1) * HALF, wide] = low
            de_new = keep * (dot_tn(c_rows, gm_grown) + grown[HALF - 1 : HALF] * de_here)
            de[:, cols] = de_new
            v_all[2 * SPAN + 16 * c : 2 * SPAN + 16 * (c + 1), cols] = jnp.concatenate(
                two_terms(eight_rows(de_new * arrived)), axis=0
            )
        d_low = jnp.where(upper, d_scores, 0.0).astype(bf16)
        dbc_ref[rows, :LANES] = dot(d_low, c_rows) + d_b
        dbc_ref[rows, LANES:] = dot_tn(d_low, b_rows) + d_c
    reduced = dot(v_all[...], red_ref[...])
    x_dot = reduced[:SPAN] + reduced[SPAN : 2 * SPAN]
    xd_ref[...] = x_dot
    d_cum = r_ref[...] - dt_ref[...] * x_dot
    for c in reversed(range(halves)):
        rows = slice(c * HALF, (c + 1) * HALF)
        da_ref[rows, :] = exact_dot(tri_up_ref[...], d_cum[rows]) + dlast[0:1, :]
        ends = reduced[2 * SPAN + 16 * c : 2 * SPAN + 16 * (c + 1)]
        dlast[...] = jnp.broadcast_to(jnp.sum(ends, axis=0, keepdims=True), dlast.shape)


def store_blocks(out_ref, parts):
    count = out_ref.shape[0] * out_ref.shape[1] * out_ref.shape[2]
    cores, sides, places = out_ref.shape[:3]
    for at in range(count):
        place, rest = at // (cores * sides), at % (cores * sides)
        rows = [part[at * (part.shape[0] // count) : (at + 1) * (part.shape[0] // count), :] for part in parts]
        block = rows[0] if len(rows) == 1 else jnp.concatenate(rows, axis=0)
        out_ref[rest % cores, rest // cores, place] = block.astype(bf16)


def outer_kernel(low_ref, back_ref, unit_ref, dgate_ref, out_ref, out_sum, *gate_sums):
    step = pl.program_id(0)
    width = gate_sums[0].shape[1]

    @pl.when(step == 0)
    def _():
        out_sum[...] = dot_tn(low_ref[...], back_ref[...])
        for k, part in enumerate(gate_sums):
            part[...] = dot_tn(unit_ref[...], dgate_ref[:, k * width : (k + 1) * width])

    @pl.when(step > 0)
    def _():
        out_sum[...] = out_sum[...] + dot_tn(low_ref[...], back_ref[...])
        for k, part in enumerate(gate_sums):
            part[...] = part[...] + dot_tn(unit_ref[...], dgate_ref[:, k * width : (k + 1) * width])

    @pl.when(step == pl.num_programs(0) - 1)
    def _():
        store_blocks(out_ref, [out_sum] + list(gate_sums))


def conv_back_kernel(
    act_ref, slope_ref, conv_ref, dx_ref, gm_ref, dbc_ref, dt_ref, cumdev_ref, raw_ref, xd_ref,
    da_ref, meta_ref, above_ref, prefix_ref, total_ref, pre_ref, skip_ref, taps_ref, heads_ref, rim_ref,
    ex_ref, red_ref, tri_ref, origin_ref, u_ref, low_ref, w_ref, unit_ref, rim_unit_ref,
    dconv_ref, first_ref, sums_ref, hsums_ref, out_ref, grad_ref,
    dt_fresh, dt_kept, flow, v_all, turned, grad, *scratch,
    inner, conv_dim, num_heads,
):
    step = pl.program_id(0)
    blocks = pl.num_programs(0) - 1
    keep = meta_ref[0:1, 3:4]
    strips = conv_dim // STRIP
    fresh, kept, ext = scratch[:strips], scratch[strips : 2 * strips], scratch[2 * strips :]
    tiles = [slice(base, base + TILE) for base in range(0, SPAN, TILE)]
    origin = pl.multiple_of(origin_ref[0, 1], 8)

    def finish(s):
        part = kept[s // STRIP]
        for q in range(STRIP // LANES):
            lanes = slice(s + q * LANES, s + (q + 1) * LANES)
            for base in range(0, SPAN, TILE):
                total = taps_ref[3:4, lanes] * part[q, base : base + TILE, :]
                for k in range(3):
                    total = total + taps_ref[k : k + 1, lanes] * part[
                        q, pl.ds(origin + base + 3 - k, TILE), :
                    ]
                dconv_ref[base : base + TILE, lanes] = total.astype(bf16)

    def add_grad(cols):
        grad[:, cols] = grad[:, cols] + dot(turned[...], dconv_ref[:, cols])

    dconv_ref[:, conv_dim:] = dt_kept[...]

    @pl.when(step == 0)
    def _():
        rim_rows = jnp.concatenate(
            [jnp.zeros((SPAN - 16, rim_unit_ref.shape[1]), f32), rim_unit_ref[...].astype(f32)], axis=0
        )
        turned[...] = rim_rows.T.astype(bf16)
        grad[...] = jnp.zeros_like(grad)
        dt_kept[...] = jnp.zeros_like(dt_kept)
        dconv_ref[:, conv_dim:] = jnp.zeros_like(dt_kept)
        for part in kept:
            part[...] = jnp.zeros_like(part)
        for j, lanes in strips_of(conv_dim):
            ext[j // 2][j % 2, 0:8, :] = rim_ref[8:16, lanes].astype(f32) * keep
        sums_ref[...] = jnp.zeros_like(sums_ref)
        hsums_ref[...] = jnp.zeros_like(hsums_ref)
        start = jnp.zeros((16, LANES), f32)
        for s in range(0, inner, STRIP):
            cols = slice(s, s + STRIP)
            both = above_ref[:, cols].astype(f32) * prefix_ref[:, cols].astype(f32)
            start = start + dot(
                jnp.concatenate(two_terms(eight_rows(both)), axis=0), red_ref[cols, :]
            )
        start = jnp.sum(start, axis=0, keepdims=True)
        flow[...] = start * jnp.exp(total_ref[...]) * pre_ref[...]

    @pl.when(step > 0)
    def _():
        turned[...] = unit_ref[...].astype(f32).T.astype(bf16)

    @pl.when((step > 0) & (step < blocks))
    def _():
        for part in ext:
            part[:, 0:8, :] = part[:, SPAN : SPAN + 8, :] * keep

    @pl.when(step < blocks)
    def _():
        b_rows = act_ref[:, inner : inner + LANES]
        dt_here = dt_ref[...]
        ahead = jnp.exp(total_ref[0:1, :] - cumdev_ref[...]) * meta_ref[:, 2:3]
        spread = split_lanes(jnp.concatenate([dt_here, ahead], axis=0))
        d_b = dbc_ref[:, :LANES]
        pending = [slice(conv_dim, conv_dim + LANES)]
        for n, s in enumerate(list(range(0, inner, STRIP)) + [inner]):
            cols = slice(s, s + STRIP)
            new, old, rows_in = fresh[s // STRIP], kept[s // STRIP], ext[s // STRIP]
            for q in range(STRIP // LANES):
                lanes = slice(s + q * LANES, s + (q + 1) * LANES)
                rows_in[q, 8 : 8 + SPAN, :] = conv_ref[:, lanes].astype(f32)
            if s < inner:
                wide = dot(spread, ex_ref[:, cols])
                passed = dot(b_rows, above_ref[:, cols])
                lows = []
                for rows in tiles:
                    dt_wide = wide[rows]
                    ahead_wide = wide[SPAN + rows.start : SPAN + rows.stop]
                    x = act_ref[rows, cols].astype(f32)
                    far = ahead_wide * passed[rows]
                    dx = dt_wide * (dx_ref[rows, cols].astype(f32) + far)
                    dx = dx + skip_ref[0:1, cols] * gm_ref[rows, cols].astype(f32)
                    dx = dx * slope_ref[rows, cols].astype(f32)
                    for q in range(STRIP // LANES):
                        new[q, rows, :] = dx[:, q * LANES : (q + 1) * LANES]
                    v_all[rows, cols] = (x * far).astype(bf16)
                    lows.append((x * dt_wide * ahead_wide).astype(bf16))
                d_b = d_b + dot_nt(jnp.concatenate(lows, axis=0), above_ref[:, cols])
            else:
                b_cols = slice(inner, inner + LANES)
                c_cols = slice(inner + LANES, inner + 2 * LANES)
                new[0, :, :] = d_b * slope_ref[:, b_cols].astype(f32)
                new[1, :, :] = dbc_ref[:, LANES:] * slope_ref[:, c_cols].astype(f32)
            add_grad(pending.pop())
            if n % 2 == 1 and n // 2 * STRIP < out_ref.shape[1]:
                wide_out = slice(n // 2 * STRIP, n // 2 * STRIP + STRIP)
                branch = meta_ref[:, 0:1] * dot(low_ref[...], w_ref[:, wide_out])
                out_ref[:, wide_out] = (u_ref[:, wide_out].astype(f32) + branch).astype(bf16)
            for q in range(STRIP // LANES):
                lanes = slice(s + q * LANES, s + (q + 1) * LANES)
                sums = [jnp.zeros((8, LANES), f32) for _ in range(5)]
                for base in range(0, SPAN, TILE):
                    d = new[q, base : base + TILE, :]
                    sums[4] = sums[4] + eight_rows(d)
                    for k in range(4):
                        shifted = rows_in[q, pl.ds(origin + base + 5 + k, TILE), :]
                        sums[k] = sums[k] + eight_rows(d * shifted)
                for k in range(5):
                    here = slice(8 * k, 8 * k + 8)
                    sums_ref[here, lanes] = sums_ref[here, lanes] + sums[k]
            old[:, SPAN : SPAN + 8, :] = new[:, 0:8, :] * keep
            finish(s)
            pending.append(cols)
            old[:, 0:SPAN, :] = new[...]
        add_grad(pending.pop())
        x_dot = dot(v_all[...], red_ref[...])
        moved = dt_here * x_dot
        rate = heads_ref[1:2, :]
        for c in range(SPAN // HALF):
            rows = slice(c * HALF, (c + 1) * HALF)
            da = da_ref[rows, :] + flow[0:1, :] + exact_dot(tri_ref[...], moved[rows]) - moved[rows]
            flow[...] = flow[...] + jnp.sum(moved[rows], axis=0, keepdims=True)
            hsums_ref[8:16, :] = hsums_ref[8:16, :] + eight_rows(da * rate * dt_here[rows])
            d_dt = xd_ref[rows, :] + x_dot[rows] + rate * da
            d_raw = meta_ref[rows, 0:1] * sigmoid(raw_ref[rows, :]) * d_dt
            real = lax.broadcasted_iota(jnp.int32, d_raw.shape, 1) < num_heads
            d_raw = jnp.where(real, d_raw, 0.0)
            hsums_ref[0:8, :] = hsums_ref[0:8, :] + eight_rows(d_raw)
            dt_fresh[rows, :] = d_raw.astype(bf16)

    @pl.when(step == 0)
    def _():
        for j, lanes in strips_of(conv_dim):
            first_ref[:, lanes] = fresh[j // 2][j % 2, 0:8, :] * keep

    @pl.when(step == blocks)
    def _():
        for s in range(0, conv_dim, STRIP):
            kept[s // STRIP][:, SPAN : SPAN + 8, :] = jnp.zeros((2, 8, LANES), f32)
            finish(s)
            add_grad(slice(s, s + STRIP))
        add_grad(slice(conv_dim, conv_dim + LANES))
        store_blocks(grad_ref, [grad])

    dt_kept[...] = dt_fresh[...]


def input_grad_kernel(
    dconv_ref, dgate_ref, near_ref, far_ref, u_ref, cot_ref, gain_ref, *refs
):
    cut = near_ref.shape[1]
    grad = dot_nt(dconv_ref[:, :cut], near_ref[...]) + dot_nt(dconv_ref[:, cut:], far_ref[...])
    out_ref = refs[-1]
    width = refs[0].shape[1]
    side = dot_nt(dgate_ref[:, :width], refs[0][...])
    for k in range(1, len(refs) - 1):
        side = side + dot_nt(dgate_ref[:, k * width : (k + 1) * width], refs[k][...])
    grad = grad + 0.5 * side
    for base in range(0, u_ref.shape[0], TILE):
        rows = slice(base, base + TILE)
        wide = u_ref[rows, :].astype(f32)
        factor = lax.rsqrt(jnp.mean(wide * wide, axis=-1, keepdims=True) + EPS_NORM)
        unit = wide * factor
        d = grad[rows] * gain_ref[...]
        mean = jnp.mean(d * unit, axis=-1, keepdims=True)
        du = factor * (d - unit * mean)
        out_ref[rows, :] = (cot_ref[rows, :].astype(f32) + du).astype(bf16)


def owner_kernel(
    conv_ref, both_ref, small_ref, w_ref, gain_ref, heads_ref, in_ref, out_ref, small_sum_ref, row_ref,
    *, num_heads,
):
    conv = jnp.sum(conv_ref[...].astype(f32), axis=0)
    both = jnp.sum(both_ref[...].astype(f32), axis=0)
    small = jnp.sum(small_ref[...], axis=0)
    own_rows, width = in_ref.shape
    out_rows, side = out_ref.shape
    out_sum = both[:out_rows]
    out_ref[...] = out_sum
    small_sum_ref[...] = small
    gates = (both.shape[0] - out_rows) // own_rows
    gain = gain_ref[...]
    squares = jnp.sum(out_sum * out_sum) + jnp.sum(small * small)
    norm_rows = jnp.zeros((own_rows, 1), f32)
    tail = width - gates * side
    pieces = [
        (k * side, 0.5 * both[out_rows + k * own_rows : out_rows + (k + 1) * own_rows]) for k in range(gates)
    ] + [(gates * side, conv[:, :tail])]
    for at, piece in pieces:
        cols = slice(at, at + piece.shape[1])
        scaled = piece * gain
        in_ref[:, cols] = scaled
        squares = squares + jnp.sum(scaled * scaled)
        norm_rows = norm_rows + jnp.sum(
            piece * w_ref[:, cols].astype(bf16).astype(f32), axis=1, keepdims=True
        )
    squares = squares + jnp.sum(norm_rows * norm_rows)
    lane = lax.broadcasted_iota(jnp.int32, (own_rows, LANES), 1)
    row = lax.broadcasted_iota(jnp.int32, (own_rows, LANES), 0)
    spread = jnp.where(lane == 3 * num_heads + 1 + row, jnp.broadcast_to(norm_rows, lane.shape), 0.0)
    first_lane = lax.broadcasted_iota(jnp.int32, (1, LANES), 1)
    packed = (
        heads_ref[...]
        + jnp.where(first_lane == 3 * num_heads, squares, 0.0)
        + jnp.sum(spread, axis=0, keepdims=True)
    )
    row_ref[...] = jnp.broadcast_to(packed[None], row_ref.shape)


def update_kernel(*refs, num_heads, own_rows, taps_own):
    rank_ref, rows_ref, in_sum_ref, out_sum_ref, small_ref = refs[:5]
    states, norm_ref, outs = refs[5:20], refs[20], refs[21:]
    rows = rows_ref[:, 0, :]
    total = jnp.sum(rows, axis=0, keepdims=True)
    lane = lax.broadcasted_iota(jnp.int32, (1, LANES), 1)
    heads = jnp.concatenate(
        [total[:, k * num_heads : (k + 1) * num_heads] for k in range(3)], axis=0
    )
    norm_sq = (
        jnp.sum(jnp.where(lane == 3 * num_heads, total, 0.0), axis=1, keepdims=True)
        + jnp.sum(jnp.sum(heads * heads, axis=0, keepdims=True), axis=1, keepdims=True)
    )
    grad_norm = jnp.sqrt(norm_sq)
    norm_ref[...] = grad_norm
    factor = jnp.minimum(1.0, MAX_NORM / (grad_norm + 1e-06))
    vec_width = states[9].shape[1]
    place = lax.broadcasted_iota(jnp.int32, (rows.shape[0], vec_width), 0)
    wanted = rank_ref[0, 0] * vec_width + lax.broadcasted_iota(jnp.int32, (rows.shape[0], vec_width), 1)
    mine = jnp.zeros((rows.shape[0], vec_width), f32)
    for j in range(own_rows):
        at = 3 * num_heads + 1 + j
        here = jnp.broadcast_to(rows[:, at : at + 1], mine.shape)
        mine = mine + jnp.where(place * own_rows + j == wanted, here, 0.0)
    vec = small_ref[0:1, :vec_width] + jnp.sum(mine, axis=0, keepdims=True)
    sums = (in_sum_ref[...], out_sum_ref[...], small_ref[1:5, :taps_own], vec, heads)
    rates = (
        (RATE_MAT, DECAY_MAT), (RATE_MAT, DECAY_MAT), (RATE_CONV, DECAY_MAT), (RATE_VEC, 0.0),
        (RATE_HEAD, 0.0),
    )
    for k, (summed, (rate, decay)) in enumerate(zip(sums, rates)):
        master, first, second = (ref[...] for ref in states[3 * k : 3 * k + 3])
        clipped_ref, first_ref, second_ref, master_ref, copy_ref = outs[5 * k : 5 * k + 5]
        clipped = summed * factor
        clipped_ref[...] = clipped
        first = BETA_ONE * first + (1.0 - BETA_ONE) * clipped
        second = BETA_TWO * second + (1.0 - BETA_TWO) * clipped * clipped
        first_ref[...] = first
        second_ref[...] = second
        first_hat = first / (1.0 - BETA_ONE**STEP)
        second_hat = second / (1.0 - BETA_TWO**STEP)
        master = master - rate * (first_hat / (jnp.sqrt(second_hat) + ADAM_EPS) + decay * master)
        master_ref[...] = master
        copy_ref[...] = master.astype(bf16)


def shift(value, axis, steps):
    count = lax.axis_size(axis)
    initial, last = (max(0, -steps), min(count, count - steps))
    return lax.ppermute(value, axis, [(source, source + steps) for source in range(initial, last)])


def axis_bits(axis):
    return [(axis, 1 << k) for k in reversed(range(lax.axis_size(axis).bit_length() - 1))]


def swap(value, axis, bit):
    count = lax.axis_size(axis)
    return lax.ppermute(value, axis, [(k, k ^ bit) for k in range(count)])


def my_bit(axis, bit):
    return (lax.axis_index(axis) // bit) % 2


def zero_from(value):
    return jnp.minimum(jnp.abs(value[(0,) * value.ndim].astype(f32)), 0.0)


def rank_bits():
    return axis_bits("seq") + axis_bits("rep")


def gather_step(value, known, axis, bit):
    order = rank_bits()
    place = sum(order.index(k) < order.index((axis, bit)) for k in known)
    other = swap(value, axis, bit)
    value = jnp.where(
        my_bit(axis, bit) == 0,
        jnp.stack([value, other], axis=place),
        jnp.stack([other, value], axis=place),
    )
    return value, known + [(axis, bit)]


def gather_steps(value, known, steps):
    for axis, bit in steps:
        value, known = gather_step(value, known, axis, bit)
    return value, known


def halve_step(value, axis, bit, token=0, done=0):
    mine = my_bit(axis, bit)
    given = lax.dynamic_index_in_dim(value, 1 - mine + token, 0, keepdims=False)
    held = lax.dynamic_index_in_dim(value, mine + done, 0, keepdims=False)
    return (held.astype(f32) + swap(given, axis, bit).astype(f32)).astype(bf16)


def call(kernel, grid, ins, in_blocks, outs, out_blocks, scratch, flops, after=(), token=False, **fixed):
    first = len(after)
    if token:
        outs = outs + [like(1, 1, dtype=jnp.int32)]
        out_blocks = out_blocks + [pl.BlockSpec(memory_space=pltpu.SMEM)]

    def body(*refs):
        refs = list(refs[first:])
        if token:
            refs.pop(count_in + len(outs) - 1)[0, 0] = jnp.int32(0)
        kernel(*refs, **fixed)

    count_in = len(ins)
    ins = list(after) + ins
    in_blocks = [pl.BlockSpec(memory_space=pl.ANY)] * first + in_blocks
    moved = sum(v.size * v.dtype.itemsize for v in ins) + sum(v.size * v.dtype.itemsize for v in outs)
    return pl.pallas_call(
        body,
        name=kernel.__name__,
        grid=(grid,),
        in_specs=in_blocks,
        out_specs=out_blocks,
        out_shape=outs,
        scratch_shapes=scratch,
        compiler_params=pltpu.CompilerParams(
            dimension_semantics=("arbitrary",), vmem_limit_bytes=VMEM_BYTES
        ),
        cost_estimate=pl.CostEstimate(flops=int(flops), bytes_accessed=moved, transcendentals=0),
    )(*ins)


def full(shape):
    return pl.BlockSpec(shape, lambda i: (0,) * len(shape))


def rows_of(count, width, index=lambda i: i):
    return pl.BlockSpec((count, width), lambda i: (index(i), 0))


def like(*shape, dtype=f32):
    return jax.ShapeDtypeStruct(shape, dtype)


def shards(
    tokens,
    cotangent,
    seq_lengths,
    in_weight,
    in_first,
    in_second,
    out_weight,
    out_first,
    out_second,
    conv_weight,
    conv_first,
    conv_second,
    vectors,
    vec_first,
    vec_second,
    head_params,
    head_first,
    head_second,
):
    u = tokens[0]
    cot = cotangent[0]
    rows, model = u.shape
    places = lax.axis_size("seq")
    ranks = places * lax.axis_size("rep")
    taps_own = conv_weight.shape[1]
    vecs_own = vectors.shape[0]
    conv_dim = taps_own * ranks
    inner = out_weight.shape[0] * ranks
    heads = head_params.shape[1]
    head_dim = inner // heads
    nblk = rows // SPAN
    quarter = rows // 4
    third = rows // 3
    wide = conv_dim + LANES
    cut = -(-wide // (2 * STRIP)) * STRIP

    own_rows, out_rows = in_weight.shape[0], out_weight.shape[0]
    sides = inner // model
    start = (lax.axis_index("seq") * rows).astype(jnp.int32)
    offset = jnp.stack([start, jnp.zeros_like(start)]).reshape(1, 2)
    bits = rank_bits()
    far_steps = [k for k in bits if k[0] == "seq" and k[1] > 1][::-1]
    near_step, rep_steps = ("seq", 1), axis_bits("rep")
    before = shift(u[rows - 16 :], "seq", 1)
    in_low = in_weight.astype(bf16)
    conv_shard = jnp.pad(in_low[:, inner:], ((0, 0), (0, LANES - heads)))
    shard, known = gather_steps(conv_shard, [], far_steps[:1])
    packed = jnp.concatenate([vectors, conv_weight.reshape(-1)]).astype(bf16)
    packed = packed + zero_from(shard).astype(bf16)
    small = lax.all_to_all(
        jnp.broadcast_to(packed[None, None], (ranks, 1, packed.shape[0])), ("seq", "rep"), 0, 0, tiled=True
    )[:, 0].astype(f32)
    shard, known = gather_steps(shard, known, far_steps[1:])
    w_near, known_near = gather_steps(shard[..., :cut], known, [near_step] + rep_steps[:1])
    w_far, known_far = gather_steps(shard[..., cut:], known, rep_steps[:1] + [near_step])
    w_near, _ = gather_steps(w_near, known_near, rep_steps[1:])
    w_far, _ = gather_steps(w_far, known_far, rep_steps[1:])
    w_near = w_near.reshape(model, cut)
    w_far = w_far.reshape(model, wide - cut)
    others = [out_weight.astype(bf16)] + [in_low[:, s : s + model] for s in range(0, inner, model)]
    others = lax.all_gather(jnp.concatenate(others, axis=0), ("seq", "rep"), axis=0)
    w_out = others[:, :out_rows].reshape(inner, model)
    w_gates = [
        others[:, out_rows + k * own_rows : out_rows + (k + 1) * own_rows].reshape(model, model)
        for k in range(sides)
    ]

    taps = small[:, vecs_own:].reshape(ranks, 4, taps_own).transpose(1, 0, 2).reshape(4, conv_dim)
    vecs = small[:, :vecs_own].reshape(-1)
    norm_gain = vecs[None, :model]
    gate_gain = vecs[None, model : model + inner]
    half_bias = 0.5 * vecs[None, model + inner :]
    half_taps = 0.5 * taps
    head_rows = jnp.stack([head_params[0], -jnp.exp(head_params[1])])
    head_rows = jnp.pad(head_rows, ((0, 6), (0, LANES - heads)))
    skip_wide = jnp.repeat(head_params[2], head_dim)[None]

    lane_head = np.arange(inner) // head_dim
    spread = (np.arange(LANES)[:, None] == lane_head[None]).astype(np.float32)
    ex = jnp.asarray(np.concatenate([spread, spread], axis=0), bf16)
    red = jnp.asarray(spread.T, bf16)
    order = np.arange(HALF)
    tri = jnp.asarray((order[:, None] >= order[None]).astype(np.float32), bf16)
    tri_up = jnp.asarray((order[:, None] <= order[None]).astype(np.float32), bf16)

    b_act = rows_of(SPAN, conv_dim)
    b_in = rows_of(SPAN, inner)
    b_lane = rows_of(SPAN, LANES)
    b_model = rows_of(SPAN, model)
    b_meta = rows_of(SPAN, 8)
    b_ex = full((2 * LANES, inner))
    b_red = full((inner, LANES))
    b_tri = full((HALF, HALF))
    b_heads = full((8, LANES))
    b_state = full((LANES, inner))
    b_one = full((1, inner))
    b_scalar = pl.BlockSpec(memory_space=pltpu.SMEM)
    q_model = rows_of(quarter, model)
    q_in = rows_of(quarter, inner)
    q_meta = rows_of(quarter, 8)
    t_model = rows_of(third, model)
    t_in = rows_of(third, inner)
    lane_out = like(rows, LANES)
    low_in = like(rows, inner, dtype=bf16)
    low_conv = like(rows, conv_dim, dtype=bf16)
    low_model = like(rows, model, dtype=bf16)
    strip_scratch = pltpu.VMEM((STRIP // LANES, SPAN + 8, LANES), f32)
    strips = conv_dim // STRIP

    (
        unit, normed, conv_in, act, slope, meta, dt_values, cumul, cumdev, raw, own_inc, starts, rim,
        rim_unit, state_out, total,
    ) = call(
        front_kernel,
        nblk,
        [
            seq_lengths, offset, u, before, w_near, w_far, norm_gain, half_taps, half_bias, head_rows,
            ex, tri,
        ],
        [
            b_scalar, b_scalar, b_model, full((16, model)), full((model, cut)),
            full((model, wide - cut)), full((1, model)), full((4, conv_dim)), full((1, conv_dim)),
            b_heads, b_ex, b_tri,
        ],
        [
            low_model, low_model, low_conv, low_conv, low_conv, like(rows, 8),
            lane_out, lane_out, lane_out, lane_out, low_in, like(16 * nblk, inner),
            like(16, conv_dim, dtype=bf16), like(16, model, dtype=bf16),
            like(LANES, inner + LANES, dtype=bf16), like(8, LANES),
        ],
        [
            b_model, b_model, b_act, b_act, b_act, b_meta, b_lane, b_lane, b_lane, b_lane, b_in,
            rows_of(16, inner), full((16, conv_dim)), full((16, model)),
            full((LANES, inner + LANES)), b_heads,
        ],
        [pltpu.VMEM((LANES, inner), f32), pltpu.VMEM((8, LANES), f32)] + [strip_scratch] * strips,
        2 * rows * model * wide * 4,
        conv_dim=conv_dim,
        inner=inner,
        places=places,
        num_rows=rows,
    )

    def chain(states, gains, reverse, after=()):
        whole = (places, LANES // places, inner)
        return call(
            chain_kernel, 1, [states, gains, ex],
            [full(states.shape), full(gains.shape), b_ex],
            [like(*whole, dtype=bf16)], [full(whole)], [], 1e7, after, token=True, reverse=reverse,
        )

    def exchange(blocks):
        return lax.all_to_all(blocks, "seq", 0, 0, tiled=True)

    arrived = exchange(state_out.reshape(places, LANES // places, inner + LANES))
    gains = arrived[:, :2, inner:]
    y_own = call(
        intra_kernel,
        nblk,
        [act, dt_values, cumul, own_inc],
        [b_act, b_lane, b_lane, b_in],
        [like(rows, inner)],
        [b_in],
        [],
        2 * rows * model * inner * 4,
        inner=inner,
    )[0]
    chained, _ = chain(arrived, gains, False, [y_own])
    prefix = exchange(chained).reshape(LANES, inner)
    gate_in, grad_gated, back_rows = call(
        project_kernel,
        4,
        [normed, meta, cot, w_out] + w_gates,
        [q_model, q_meta, q_model, full((inner, model))] + [full((model, model))] * sides,
        [low_in, low_in, low_model],
        [q_in, q_in, q_model],
        [],
        2 * rows * model * inner * 2,
        [chained],
        inner=inner,
    )

    wide_scratch = pltpu.VMEM((SPAN, inner), f32)
    gated_low, grad_mixed, grad_gate, r_sums, gdev, gate_sums = call(
        gate_kernel,
        nblk,
        [
            y_own, act, prefix, cumdev, meta, gate_in, grad_gated, skip_wide, gate_gain, ex, red,
        ],
        [b_in, b_act, b_state, b_lane, b_meta, b_in, b_in, b_one, b_one, b_ex, b_red],
        [low_in, low_in, low_in, lane_out, like(LANES, inner, dtype=bf16), like(8, inner)],
        [b_in, b_in, b_in, b_lane, b_state, full((8, inner))],
        [wide_scratch] * 5
        + [
            pltpu.VMEM((SPAN, inner), bf16),
            pltpu.VMEM((SPAN, inner), bf16),
            pltpu.VMEM((LANES, inner), f32),
        ],
        2 * rows * model * inner * 3,
        inner=inner,
    )

    gathered = exchange(gdev.reshape(places, LANES // places, inner))
    block_shape = tuple(lax.axis_size("rep") // 2 if k == 0 else 2 for k in range(2))[::-1] + (places,)
    both_grad = call(
        outer_kernel,
        3,
        [gated_low, back_rows, unit, grad_gate],
        [t_in, t_model, t_model, t_in],
        [like(*block_shape, out_rows + sides * own_rows, model, dtype=bf16)],
        [full(block_shape + (out_rows + sides * own_rows, model))],
        [pltpu.VMEM((inner, model), f32)] + [pltpu.VMEM((model, model), f32)] * sides,
        2 * rows * model * inner * 2,
    )[0]
    chained_back, chain_token = chain(gathered, gains, True, [both_grad])
    above = exchange(chained_back).reshape(LANES, inner)
    both = halve_step(both_grad, *rep_steps[1], chain_token[0, 0])

    flip = lambda i: nblk - 1 - i
    f_lane = rows_of(SPAN, LANES, flip)
    f_in = rows_of(SPAN, inner, flip)
    dx_own, dbc_own, xd_own, da_own, skip_sums, back_token = call(
        intra_back_kernel,
        nblk,
        [
            act, grad_mixed, dt_values, cumul, meta, own_inc, starts, prefix, r_sums, red, tri_up,
        ],
        [
            rows_of(SPAN, conv_dim, flip), f_in, f_lane, f_lane, rows_of(SPAN, 8, flip), f_in,
            rows_of(16, inner, flip), b_state, f_lane, b_red, b_tri,
        ],
        [low_in, like(rows, 2 * LANES), lane_out, lane_out, like(8, inner)],
        [f_in, rows_of(SPAN, 2 * LANES, flip), f_lane, f_lane, full((8, inner))],
        [
            pltpu.VMEM((LANES, inner), f32),
            pltpu.VMEM((8, LANES), f32),
            pltpu.VMEM((2 * SPAN + 32, inner), bf16),
        ],
        2 * rows * model * inner * 6,
        [both, chained_back],
        token=True,
        inner=inner,
    )
    both = halve_step(both, *rep_steps[0], done=back_token[0, 0])

    capped = lambda i: jnp.minimum(i, nblk - 1)
    late = lambda i: jnp.maximum(i - 1, 0)
    c_lane = rows_of(SPAN, LANES, capped)
    c_in = rows_of(SPAN, inner, capped)
    c_act = rows_of(SPAN, conv_dim, capped)
    pre_last = jnp.broadcast_to(meta[rows - 1 :, 1:2], (8, LANES))
    dconv, first_rows, conv_sums, head_sum_rows, block_out, conv_grad = call(
        conv_back_kernel,
        nblk + 1,
        [
            act, slope, conv_in, dx_own, grad_mixed, dbc_own, dt_values, cumdev, raw, xd_own, da_own,
            meta, above, prefix, total, pre_last, skip_wide, half_taps, head_rows, rim, ex, red, tri,
            offset, u, gated_low, w_out, unit, rim_unit,
        ],
        [
            c_act, c_act, c_act, c_in, c_in, rows_of(SPAN, 2 * LANES, capped), c_lane, c_lane, c_lane,
            c_lane, c_lane, rows_of(SPAN, 8, capped), b_state, b_state,
            b_heads, b_heads, b_one, full((4, conv_dim)), b_heads, full((16, conv_dim)),
            b_ex, b_red, b_tri, b_scalar, rows_of(SPAN, model, capped), c_in, full((inner, model)),
            rows_of(SPAN, model, late), full((16, model)),
        ],
        [
            like(rows, wide, dtype=bf16), like(8, conv_dim), like(40, conv_dim), like(16, LANES),
            low_model, like(*block_shape, own_rows, wide, dtype=bf16),
        ],
        [
            rows_of(SPAN, wide, late), full((8, conv_dim)), full((40, conv_dim)), full((16, LANES)),
            rows_of(SPAN, model, capped), full(block_shape + (own_rows, wide)),
        ],
        [
            pltpu.VMEM((SPAN, LANES), bf16),
            pltpu.VMEM((SPAN, LANES), bf16),
            pltpu.VMEM((8, LANES), f32),
            pltpu.VMEM((SPAN, inner), bf16),
            pltpu.VMEM((model, SPAN), bf16),
            pltpu.VMEM((model, wide), f32),
        ]
        + [pltpu.VMEM((STRIP // LANES, SPAN, LANES), f32)] * strips
        + [strip_scratch] * (2 * strips),
        2 * rows * model * inner * 3,
        [both],
        inner=inner,
        conv_dim=conv_dim,
        num_heads=heads,
    )
    both_all = exchange(both)

    after = shift(first_rows, "seq", -1)
    late_rows = jnp.stack(
        [sum(half_taps[k] * after[j - k] for k in range(j + 1)) for j in range(3)]
    )
    tail = dconv[rows - 16 :, :conv_dim].astype(f32) + jnp.pad(late_rows, ((13, 0), (0, 0)))
    dconv = lax.dynamic_update_slice(dconv, tail.astype(bf16), (rows - 16, 0))


    grad_taps = 0.5 * jnp.sum(conv_sums.reshape(5, 8, conv_dim), axis=1)
    grad_vecs = jnp.concatenate(
        [jnp.zeros((model,), f32), jnp.sum(gate_sums, axis=0), grad_taps[4]]
    ).reshape(ranks, 1, vecs_own)
    tap_rows = grad_taps[:4].reshape(4, ranks, taps_own).transpose(1, 0, 2)
    small_grads = jnp.concatenate(
        [jnp.pad(v, ((0, 0), (0, 0), (0, LANES - v.shape[2]))) for v in (grad_vecs, tap_rows)], axis=1
    )
    small_all = lax.all_to_all(
        jnp.pad(small_grads, ((0, 0), (0, 3), (0, 0))), ("seq", "rep"), 0, 0, tiled=True
    )

    conv_part = halve_step(conv_grad, *rep_steps[1])
    input_grad, grad_token = call(
        input_grad_kernel,
        4,
        [dconv, grad_gate, w_near, w_far, u, cot, norm_gain] + w_gates,
        [
            rows_of(quarter, wide), q_in, full((model, cut)), full((model, wide - cut)),
            q_model, q_model, full((1, model)),
        ]
        + [full((model, model))] * sides,
        [low_model],
        [q_model],
        [],
        2 * rows * model * (wide + inner),
        [conv_part, small_all],
        token=True,
    )
    conv_part = halve_step(conv_part, *rep_steps[0], done=grad_token[0, 0])
    conv_all = exchange(conv_part)

    rank = lax.axis_index("seq") * lax.axis_size("rep") + lax.axis_index("rep")
    own_gain = lax.dynamic_slice_in_dim(norm_gain[0], rank * own_rows, own_rows)[:, None]
    grad_skip = jnp.sum(jnp.sum(skip_sums, axis=0).reshape(heads, head_dim), axis=1)
    head_local = jnp.concatenate(
        [
            jnp.sum(head_sum_rows.reshape(2, 8, LANES), axis=1)[:, :heads].reshape(-1),
            grad_skip,
        ]
    )
    head_local = jnp.pad(head_local, (0, LANES - 3 * heads))[None]
    small_shape = small_all.shape[1:]
    in_sum, out_sum, small_sum, row = call(
        owner_kernel,
        1,
        [conv_all, both_all, small_all, in_weight, own_gain, head_local],
        [
            full(v.shape)
            for v in (conv_all, both_all, small_all, in_weight, own_gain, head_local)
        ],
        [like(*in_weight.shape), like(*out_weight.shape), like(*small_shape), like(ranks, 1, LANES)],
        [full(in_weight.shape), full(out_weight.shape), full(small_shape), full((ranks, 1, LANES))],
        [],
        1e6,
        num_heads=heads,
    )
    all_rows = lax.all_to_all(row, ("seq", "rep"), 0, 0, tiled=True)
    states = [
        in_weight, in_first, in_second, out_weight, out_first, out_second, conv_weight, conv_first,
        conv_second, vectors[None], vec_first[None], vec_second[None], head_params, head_first, head_second,
    ]
    shapes = [states[3 * k].shape for k in range(5)]
    updated = call(
        update_kernel,
        1,
        [rank.astype(jnp.int32).reshape(1, 1), all_rows, in_sum, out_sum, small_sum] + states,
        [b_scalar]
        + [full(v.shape) for v in [all_rows, in_sum, out_sum, small_sum] + states],
        [like(1, 1)]
        + [like(*shape, dtype=kind) for shape in shapes for kind in (f32, f32, f32, f32, bf16)],
        [full((1, 1))] + [full(shape) for shape in shapes for _ in range(5)],
        [],
        1e6,
        num_heads=heads,
        own_rows=own_rows,
        taps_own=taps_own,
    )
    grad_norm, updated = updated[0][0, 0], list(updated[1:])
    updated[15:20] = [v[0] for v in updated[15:20]]
    return (block_out[None], input_grad[None], grad_norm) + tuple(updated)


def solution(mesh):
    tokens = P("rep", "seq", None)
    row_split = P(("seq", "rep"), None)
    column_split = P(None, ("seq", "rep"))
    flat_split = P(("seq", "rep"))
    return jax.shard_map(
        shards,
        mesh=mesh,
        in_specs=(tokens, tokens, P("rep", None))
        + (row_split,) * 6
        + (column_split,) * 3
        + (flat_split,) * 3
        + (P(),) * 3,
        out_specs=(tokens, tokens, P())
        + (row_split,) * 10
        + (column_split,) * 5
        + (flat_split,) * 5
        + (P(),) * 5,
        check_vma=False,
    )
```

```python
import jax
import jax.numpy as jnp
import numpy as np
from jax import lax
from jax.experimental import pallas as pl
from jax.experimental.pallas import tpu as pltpu
from jax.sharding import PartitionSpec as P

SPAN = 256
HALF = 128
LANES = 128
STRIP = 256
TILE = 64
STEP = 10

EPS_NORM = 1e-05
MAX_NORM = 1.0
BETA_ONE = 0.9
BETA_TWO = 0.95
ADAM_EPS = 1e-08
DECAY_MAT = 0.1
RATE_MAT = 0.05
RATE_CONV = 0.5
RATE_VEC = 1.0
RATE_HEAD = 2.0
LOG2E = 1.4426950408889634
VMEM_BYTES = 58 * 1024 * 1024

f32 = jnp.float32
bf16 = jnp.bfloat16


def dot(a, b):
    return jnp.dot(a, b, preferred_element_type=f32)


def dot_nt(a, b):
    return lax.dot_general(a, b, (((1,), (1,)), ((), ())), preferred_element_type=f32)


def dot_tn(a, b):
    return lax.dot_general(a, b, (((0,), (0,)), ((), ())), preferred_element_type=f32)


def two_terms(v):
    high = v.astype(bf16)
    return high, (v - high.astype(f32)).astype(bf16)


def split_lanes(v):
    return jnp.concatenate(two_terms(v), axis=-1)


def exact_dot(ones_matrix, v):
    high, rest = two_terms(v)
    middle, low = two_terms(v - high.astype(f32))
    return dot(ones_matrix, high) + (dot(ones_matrix, middle) + dot(ones_matrix, low))


def sigmoid(v):
    return 0.5 * jnp.tanh(0.5 * v) + 0.5


def low_half(shape):
    return lax.broadcasted_iota(jnp.int32, shape, 1) < LANES // 2


def block_diag(pair):
    low_lanes = low_half(pair.shape)
    none = jnp.zeros_like(pair)
    return jnp.concatenate(
        [jnp.where(low_lanes, pair, none), jnp.where(low_lanes, none, pair)], axis=0
    )


def column(v, h):
    return jnp.broadcast_to(v[:, h : h + 1], (v.shape[0], LANES))


def eight_rows(v):
    return jnp.sum(v.reshape(v.shape[0] // 8, 8, v.shape[1]), axis=0)


def row_norm(rows, gain):
    wide = rows.astype(f32)
    factor = lax.rsqrt(jnp.mean(wide * wide, axis=-1, keepdims=True) + EPS_NORM)
    return (wide * factor * gain).astype(bf16)


def strips_of(width):
    return [(j, slice(j * LANES, (j + 1) * LANES)) for j in range(width // LANES)]


def shifted_sum(taps_ref, lanes, source, q, start, total):
    for k in range(4):
        total = total + taps_ref[k : k + 1, lanes] * source[q, pl.ds(start + k, TILE), :]
    return total


def front_kernel(
    lengths_ref, offset_ref, u_ref, before_ref, near_ref, far_ref, heads_ref,
    ex_ref, tri_ref,
    unit_ref, normed_ref, conv_ref, act_ref, slope_ref, meta_ref, dt_ref, cum_ref, cumdev_ref, raw_ref,
    inc_ref, start_ref, rim_ref, rim_unit_ref, state_out_ref, total_ref, taps_ref, gain_ref,
    gate_gain_ref, bias_ref, state, offset, *ext,
    conv_dim, inner, places, num_rows, own_rows, slots, heads,
):
    step = pl.program_id(0)
    cut = near_ref.shape[1]

    @pl.when(step == 0)
    def _():
        spare = far_ref[:, conv_dim - cut :].astype(f32)
        model = spare.shape[0]

        def piece(r, k):
            row, lane, size = slots[k]
            return spare[r * own_rows + row : r * own_rows + row + 1, heads + lane : heads + lane + size]

        ranks = range(model // own_rows)
        for k in range(4):
            taps_ref[k : k + 1, :] = 0.5 * jnp.concatenate([piece(r, k) for r in ranks], axis=1)
        vecs = jnp.concatenate([piece(r, k) for r in ranks for k in range(4, len(slots))], axis=1)
        gain_ref[...] = vecs[:, :model]
        gate_gain_ref[...] = vecs[:, model : model + inner]
        bias_ref[...] = 0.5 * vecs[:, model + inner :]

    gain = gain_ref[...]

    device_start = offset_ref[0, 0]
    row = lax.broadcasted_iota(jnp.int32, (SPAN, 8), 0)
    flag = lax.broadcasted_iota(jnp.int32, (SPAN, 8), 1)
    position = device_start + step * SPAN + row
    begin = jnp.int32(0)
    first = jnp.zeros((SPAN, 8), jnp.int32)
    last_first = jnp.int32(0)
    live = jnp.zeros((SPAN, 8), jnp.bool_)
    for k in range(lengths_ref.shape[1]):
        length = lengths_ref[0, k]
        after = position >= begin
        first = jnp.where(after, begin, first)
        last_first = jnp.where(device_start + num_rows - 1 >= begin, begin, last_first)
        live = live | (after & (position < begin + length))
        begin = begin + (length + SPAN - 1) // SPAN * SPAN
    meta = jnp.where(
        flag == 0,
        live.astype(f32),
        jnp.where(
            flag == 1,
            (first < device_start).astype(f32),
            jnp.where(
                flag == 2,
                (first == last_first).astype(f32),
                (first < position - (row & (HALF - 1))).astype(f32),
            ),
        ),
    )
    meta_ref[...] = meta
    keep = meta[0:1, 3:4]

    @pl.when(step == 0)
    def _():
        normed_rim = row_norm(before_ref[...], gain)
        rim_unit_ref[...] = row_norm(before_ref[...], 1.0)
        rim = jnp.concatenate(
            [dot(normed_rim, near_ref[...]), dot(normed_rim, far_ref[:, : conv_dim - cut])], axis=1
        ).astype(bf16)
        rim_ref[...] = rim
        for j, lanes in strips_of(conv_dim):
            ext[j // 2][j % 2, 0:8, :] = rim[8:16, lanes].astype(f32) * keep
        state[...] = jnp.zeros_like(state)
        offset[...] = jnp.zeros_like(offset)

    @pl.when(step > 0)
    def _():
        for part in ext:
            part[:, 0:8, :] = part[:, SPAN : SPAN + 8, :] * keep

    wide_u = u_ref[...].astype(f32)
    unit = wide_u * lax.rsqrt(jnp.mean(wide_u * wide_u, axis=-1, keepdims=True) + EPS_NORM)
    unit_ref[...] = unit.astype(bf16)
    normed_ref[...] = (unit * gain).astype(bf16)
    raw = dot(normed_ref[...], far_ref[:, conv_dim - cut :]).astype(bf16).astype(f32)
    raw = raw + heads_ref[0:1, :]
    raw_ref[...] = raw
    dt_values = meta[:, 0:1] * (jnp.maximum(raw, 0.0) + jnp.log1p(jnp.exp(-jnp.abs(raw))))
    dt_ref[...] = dt_values

    parts, fades, starts = [], [], []
    for c in range(SPAN // HALF):
        rows = slice(c * HALF, (c + 1) * HALF)
        dt_here = dt_values[rows]
        cumul = exact_dot(tri_ref[...], heads_ref[1:2, :] * dt_here)
        cum_ref[rows, :] = cumul
        cumdev_ref[rows, :] = offset[0:1, :] + cumul
        last = cumul[HALF - 1 : HALF]
        parts.append(jnp.exp(last - cumul) * dt_here)
        fades.append(jnp.broadcast_to(jnp.exp(last), (8, LANES)))
        starts.append(jnp.exp(offset[...]) * meta[c * HALF : c * HALF + 1, 1:2])
        offset[...] = offset[...] + last
    spread = split_lanes(jnp.concatenate(parts + fades + starts, axis=0))
    origin = pl.multiple_of(offset_ref[0, 1], 8)

    def project(s):
        part = ext[s // STRIP]
        w_here = near_ref[:, s : s + STRIP] if s < cut else far_ref[:, s - cut : s - cut + STRIP]
        piece = dot(normed_ref[...], w_here).astype(bf16)
        conv_ref[:, s : s + STRIP] = piece
        for q in range(STRIP // LANES):
            part[q, 8 : 8 + SPAN, :] = piece[:, q * LANES : (q + 1) * LANES].astype(f32)

    def activate(s):
        part = ext[s // STRIP]
        for q in range(STRIP // LANES):
            lanes = slice(s + q * LANES, s + (q + 1) * LANES)
            for base in range(0, SPAN, TILE):
                half = shifted_sum(taps_ref, lanes, part, q, origin + base + 5, bias_ref[0:1, lanes])
                turn = jnp.tanh(half)
                value = half + half * turn
                act_ref[base : base + TILE, lanes] = value.astype(bf16)
                slope_ref[base : base + TILE, lanes] = (
                    (1.0 + value) + turn * (1.0 - value)
                ).astype(bf16)

    def accumulate(s):
        cols = slice(s, s + STRIP)
        wide = dot(spread, ex_ref[:, cols])
        start_ref[:, cols] = wide[SPAN + 16 :]
        for c in range(SPAN // HALF):
            rows = slice(c * HALF, (c + 1) * HALF)
            b_rows = act_ref[rows, inner : inner + LANES]
            scaled = (act_ref[rows, cols].astype(f32) * wide[rows]).astype(bf16)
            arrived = meta[c * HALF : c * HALF + 1, 3:4] * state[:, cols]
            inc_ref[rows, cols] = arrived.astype(bf16)
            fade = wide[SPAN + 8 * c : SPAN + 8 * c + 1]
            state[:, cols] = fade * arrived + dot_tn(b_rows, scaled)

    order = [inner] + list(range(0, inner, STRIP))
    for k in range(len(order) + 2):
        if k < len(order):
            project(order[k])
        if 2 <= k and order[k - 2] != inner:
            accumulate(order[k - 2])
        if 1 <= k <= len(order):
            activate(order[k - 1])

    @pl.when(step == pl.num_programs(0) - 1)
    def _():
        state_out_ref[:, :inner] = state[...].astype(bf16)
        gain_row = jnp.exp(offset[0:1, :]) * meta[SPAN - 1 : SPAN, 1:2]
        high, low = two_terms(jnp.broadcast_to(gain_row, (HALF, LANES)))
        place = lax.broadcasted_iota(jnp.int32, (HALF, LANES), 0) % (HALF // places)
        none = jnp.zeros_like(high)
        state_out_ref[:, inner:] = jnp.where(
            place == 0, high, jnp.where(place == 1, low, none)
        )
        total_ref[0:8, :] = offset[...]
        total_ref[8:16, :] = jnp.broadcast_to(meta[SPAN - 1 : SPAN, 1:2], offset.shape)


def chain_kernel(states_ref, gains_ref, ex_ref, out_ref, *, reverse):
    places, rows, inner = out_ref.shape
    gains = jnp.concatenate([gains_ref[:, 0, :], gains_ref[:, 1, :]], axis=1)
    wide = dot(gains, ex_ref[...])
    running = jnp.zeros((rows, inner), f32)
    for k in range(places):
        at = places - 1 - k if reverse else k
        out_ref[at] = running.astype(bf16)
        running = wide[at : at + 1] * running + states_ref[at, :, :inner].astype(f32)


def join_rows(parts, wholes):
    @pl.when(pl.program_id(0) == 0)
    def _():
        for part, whole in zip(parts, wholes):
            whole[...] = part[...].astype(f32).reshape(whole.shape).astype(bf16)


def project_kernel(
    normed_ref, meta_ref, cot_ref, wo_ref, *refs, inner, sides
):
    gate_ref, gg_ref, back_ref = refs[sides : sides + 3]
    gates = refs[sides + 3 :]
    join_rows(refs[:sides], gates)
    width = gates[0].shape[1]
    wo = wo_ref[...].reshape(inner, width)
    back = (meta_ref[:, 0:1] * cot_ref[...].astype(f32)).astype(bf16)
    back_ref[...] = back
    for s in range(0, inner, STRIP):
        cols = slice(s, s + STRIP)
        w_here = gates[s // width][:, s % width : s % width + STRIP]
        gate_ref[:, cols] = dot(normed_ref[...], w_here).astype(bf16)
        gg_ref[:, cols] = dot_nt(back, wo[cols, :]).astype(bf16)


def intra_kernel(act_ref, dt_ref, cum_ref, inc_ref, ex_ref, y_ref, *, inner):
    dt_split = split_lanes(dt_ref[...])
    at_row = lax.broadcasted_iota(jnp.int32, (HALF, HALF), 0)
    at_col = lax.broadcasted_iota(jnp.int32, (HALF, HALF), 1)
    first_head = low_half((HALF, LANES))
    chunks = []
    for c in range(SPAN // HALF):
        rows = slice(c * HALF, (c + 1) * HALF)
        b_rows = act_ref[rows, inner : inner + LANES]
        c_rows = act_ref[rows, inner + LANES : inner + 2 * LANES]
        scores = jnp.where(at_row >= at_col, dot_nt(c_rows, b_rows), 0.0)
        cumul = LOG2E * cum_ref[rows, :]
        chunks.append((rows, c_rows, scores, cumul, cumul.T))

    def prepare(c, s, q, dt_wide):
        rows, _, scores, cumul, across = chunks[c]
        wide = slice(s + q * LANES, s + (q + 1) * LANES)
        h = s // 64 + 2 * q
        falls = [column(cumul, h), column(cumul, h + 1)]
        mixes = [
            (scores * jnp.exp2(jnp.minimum(fall - across[h + k : h + k + 1, :], 0.0))).astype(bf16)
            for k, fall in enumerate(falls)
        ]
        grown = jnp.exp2(jnp.where(first_head, falls[0], falls[1]))
        lanes = slice(q * LANES, (q + 1) * LANES)
        steps = (act_ref[rows, wide].astype(f32) * dt_wide[:, lanes]).astype(bf16)
        return jnp.concatenate(mixes, axis=1), block_diag(steps), grown

    work = [(c, s, q) for s in range(0, inner, STRIP) for c in range(SPAN // HALF) for q in range(2)]
    ready = {}
    strip = {}
    for k in range(len(work) + 1):
        if k < len(work):
            c, s, q = work[k]
            if (c, q) == (0, 0):
                dt_strip = dot(dt_split, ex_ref[:, s : s + STRIP])
            if q == 0:
                strip[c, s] = dot(chunks[c][1], inc_ref[chunks[c][0], s : s + STRIP])
            ready[k] = prepare(c, s, q, dt_strip[chunks[c][0]])
        if k > 0:
            c, s, q = work[k - 1]
            mixes, steps, grown = ready.pop(k - 1)
            lanes = slice(q * LANES, (q + 1) * LANES)
            y_ref[chunks[c][0], s + q * LANES : s + (q + 1) * LANES] = (
                dot(mixes, steps) + strip[c, s][:, lanes] * grown
            )


def gate_kernel(
    y_ref, act_ref, prefix_ref, cumdev_ref, meta_ref, gate_ref, gg_ref, skip_ref, gain_ref,
    ex_ref, red_ref,
    low_ref, gm_ref, dgate_ref, r_ref, gdev_ref, sums_ref,
    y_all, g_all, d_all, s_all, t_all, e_all, v_all, gdev,
    *, inner,
):
    step = pl.program_id(0)

    @pl.when(step == 0)
    def _():
        gdev[...] = jnp.zeros_like(gdev)
        sums_ref[...] = jnp.zeros_like(sums_ref)

    c_rows = act_ref[:, inner + LANES : inner + 2 * LANES]
    reach = split_lanes(jnp.exp(cumdev_ref[...]) * meta_ref[:, 1:2])
    tiles = [slice(base, base + TILE) for base in range(0, SPAN, TILE)]
    squares = [jnp.zeros((TILE, 1), f32) for _ in tiles]
    for s in range(0, inner, STRIP):
        cols = slice(s, s + STRIP)
        reached = dot(reach, ex_ref[:, cols])
        e_all[:, cols] = reached.astype(bf16)
        from_prefix = dot(c_rows, prefix_ref[:, cols])
        for at, rows in enumerate(tiles):
            y = y_ref[rows, cols] + reached[rows] * from_prefix[rows]
            y_all[rows, cols] = y
            z = gate_ref[rows, cols].astype(f32)
            mixed = y + skip_ref[0:1, cols] * act_ref[rows, cols].astype(f32)
            half = 0.5 * z
            turn = jnp.tanh(half)
            raised = 1.0 + turn
            sl = half * raised
            g = mixed * sl
            g_all[rows, cols] = g
            s_all[rows, cols] = sl
            t_all[rows, cols] = mixed * (raised + sl * (1.0 - turn))
            squares[at] = squares[at] + jnp.sum(g * g, axis=1, keepdims=True)
    factors = [lax.rsqrt(v / inner + EPS_NORM) for v in squares]
    inner_sums = [jnp.zeros((TILE, 1), f32) for _ in tiles]
    for s in range(0, inner, STRIP):
        cols = slice(s, s + STRIP)
        gain = gain_ref[0:1, cols]
        gain_sum = jnp.zeros((8, STRIP), f32)
        for at, rows in enumerate(tiles):
            gn = g_all[rows, cols] * factors[at]
            g_all[rows, cols] = gn
            low_ref[rows, cols] = (gn * gain).astype(bf16)
            raw = gg_ref[rows, cols].astype(f32)
            both = raw * gn
            gain_sum = gain_sum + eight_rows(both)
            d_all[rows, cols] = raw * gain
            inner_sums[at] = inner_sums[at] + jnp.sum(both * gain, axis=1, keepdims=True)
        sums_ref[:, cols] = sums_ref[:, cols] + gain_sum
    means = [v / inner for v in inner_sums]

    def gather_strip(cols):
        gdev[:, cols] = gdev[:, cols] + dot_tn(c_rows, e_all[:, cols])
        part = dot(v_all[:, cols], red_ref[cols, :])
        return part[:SPAN] + part[SPAN:]

    r_ref[...] = jnp.zeros_like(r_ref)
    waiting = None
    for s in range(0, inner, STRIP):
        cols = slice(s, s + STRIP)
        if waiting is not None:
            r_ref[...] = r_ref[...] + gather_strip(waiting)
        waiting = cols
        for at, rows in enumerate(tiles):
            dg = factors[at] * (d_all[rows, cols] - g_all[rows, cols] * means[at])
            gm = dg * s_all[rows, cols]
            gm_low = gm.astype(bf16)
            gm_ref[rows, cols] = gm_low
            dgate_ref[rows, cols] = (dg * t_all[rows, cols]).astype(bf16)
            high, low = two_terms(gm_low.astype(f32) * y_all[rows, cols])
            v_all[rows, cols] = high
            v_all[SPAN + rows.start : SPAN + rows.stop, cols] = low
            e_all[rows, cols] = gm_low * e_all[rows, cols]
    r_ref[...] = r_ref[...] + gather_strip(waiting)

    @pl.when(step == pl.num_programs(0) - 1)
    def _():
        gdev_ref[...] = gdev[...].astype(bf16)


def intra_back_kernel(
    act_ref, gm_ref, dt_ref, cum_ref, meta_ref, inc_ref, start_ref, prefix_ref, r_ref,
    red_ref, tri_up_ref,
    dx_ref, dbc_ref, xd_ref, da_ref, skip_ref,
    de, dlast, v_all, d_scores, d_b, d_c, reduced,
    *, inner,
):
    @pl.when(pl.program_id(0) == 0)
    def _():
        de[...] = jnp.zeros_like(de)
        dlast[...] = jnp.zeros_like(dlast)
        skip_ref[...] = jnp.zeros_like(skip_ref)

    at_row = lax.broadcasted_iota(jnp.int32, (HALF, HALF), 0)
    at_col = lax.broadcasted_iota(jnp.int32, (HALF, HALF), 1)
    first_head = low_half((HALF, LANES))
    upper = at_row <= at_col
    halves = SPAN // HALF
    d_scores[...] = jnp.zeros_like(d_scores)
    d_b[...] = jnp.zeros_like(d_b)
    d_c[...] = jnp.zeros_like(d_c)
    chunks = []
    for c in range(halves):
        rows = slice(c * HALF, (c + 1) * HALF)
        b_rows = act_ref[rows, inner : inner + LANES]
        c_rows = act_ref[rows, inner + LANES : inner + 2 * LANES]
        scores = jnp.where(upper, dot_nt(b_rows, c_rows), 0.0)
        cumul = LOG2E * cum_ref[rows, :]
        chunks.append((rows, b_rows, c_rows, scores, cumul, cumul.T))

    def prepare(c, s):
        rows, _, _, scores, cumul, across = chunks[c]
        cols = slice(s, s + STRIP)
        dt_here = dt_ref[rows, :]
        pairs = []
        for q in range(STRIP // LANES):
            h = s // 64 + 2 * q
            falls = [column(cumul, h), column(cumul, h + 1)]
            decays = [
                jnp.exp2(jnp.minimum(across[h + k : h + k + 1, :] - falls[k], 0.0)) for k in range(2)
            ]
            mixes = jnp.concatenate([(scores * decay).astype(bf16) for decay in decays], axis=1)
            cum_wide = jnp.where(first_head, falls[0], falls[1])
            dt_wide = jnp.where(first_head, column(dt_here, h), column(dt_here, h + 1))
            pairs.append((decays, mixes, cum_wide, dt_wide))
        cum_wide = jnp.concatenate([pair[2] for pair in pairs], axis=1)
        grown = jnp.exp2(cum_wide)
        left = jnp.exp2(cum_wide[HALF - 1 : HALF] - cum_wide)
        x = act_ref[rows, cols].astype(f32)
        gm = gm_ref[rows, cols]
        gm_wide = gm.astype(f32)
        skip_ref[:, cols] = skip_ref[:, cols] + eight_rows(gm_wide * x)
        steps_wide = x * jnp.concatenate([pair[3] for pair in pairs], axis=1)
        gm_grown = (gm_wide * grown).astype(bf16)
        left_steps = (steps_wide * left).astype(bf16)
        return pairs, grown[HALF - 1 : HALF], left, steps_wide.astype(bf16), gm_grown, left_steps

    def finish(c, s, made):
        pairs, fade, left, steps, gm_grown, left_steps = made
        rows, b_rows, c_rows = chunks[c][:3]
        cols = slice(s, s + STRIP)
        keep = meta_ref[c * HALF : c * HALF + 1, 3:4]
        arrived = inc_ref[rows, cols].astype(f32) + start_ref[8 * c : 8 * c + 1, cols] * prefix_ref[
            :, cols
        ].astype(f32)
        d_c[c] = d_c[c] + dot_nt(gm_grown, arrived.astype(bf16))
        de_here = de[:, cols]
        de_low = de_here.astype(bf16)
        dx_far = left * dot(b_rows, de_low)
        d_b[c] = d_b[c] + dot_nt(left_steps, de_low)
        gm = gm_ref[rows, cols]
        x = act_ref[rows, cols].astype(f32)
        for q, (decays, mixes, _, _) in enumerate(pairs):
            lanes = slice(q * LANES, (q + 1) * LANES)
            wide = slice(s + q * LANES, s + (q + 1) * LANES)
            gm_diag = block_diag(gm[:, lanes])
            d_mix = dot_nt(steps[:, lanes], gm_diag)
            dx = dot(mixes, gm_diag) + dx_far[:, lanes]
            dx_ref[rows, wide] = dx.astype(bf16)
            high, low = two_terms(x[:, lanes] * dx)
            v_all[rows, wide] = high
            v_all[SPAN + c * HALF : SPAN + (c + 1) * HALF, wide] = low
            d_scores[c] = d_scores[c] + (d_mix[:, :HALF] * decays[0] + d_mix[:, HALF:] * decays[1])
        de_new = keep * (dot_tn(c_rows, gm_grown) + fade * de_here)
        de[:, cols] = de_new
        v_all[2 * SPAN + 16 * c : 2 * SPAN + 16 * (c + 1), cols] = jnp.concatenate(
            two_terms(eight_rows(de_new * arrived)), axis=0
        )

    work = [(c, s) for s in range(0, inner, STRIP) for c in reversed(range(halves))]
    made = None
    reduced[...] = jnp.zeros_like(reduced)
    for k in range(len(work) + 2):
        before, made = made, prepare(*work[k]) if k < len(work) else None
        if 0 < k <= len(work):
            finish(*work[k - 1], before)
        if k > 1 and work[k - 2][0] == 0:
            cols = slice(work[k - 2][1], work[k - 2][1] + STRIP)
            reduced[...] = reduced[...] + dot(v_all[:, cols], red_ref[cols, :])
    for c in range(halves):
        rows, b_rows, c_rows = chunks[c][:3]
        d_low = jnp.where(upper, d_scores[c], 0.0).astype(bf16)
        dbc_ref[rows, :LANES] = dot(d_low, c_rows) + d_b[c]
        dbc_ref[rows, LANES:] = dot_tn(d_low, b_rows) + d_c[c]
    x_dot = reduced[:SPAN] + reduced[SPAN : 2 * SPAN]
    xd_ref[...] = x_dot
    d_cum = r_ref[...] - dt_ref[...] * x_dot
    for c in reversed(range(halves)):
        rows = slice(c * HALF, (c + 1) * HALF)
        da_ref[rows, :] = exact_dot(tri_up_ref[...], d_cum[rows]) + dlast[0:1, :]
        ends = reduced[2 * SPAN + 16 * c : 2 * SPAN + 16 * (c + 1)]
        dlast[...] = jnp.broadcast_to(jnp.sum(ends, axis=0, keepdims=True), dlast.shape)


def store_blocks(out_ref, parts):
    count = out_ref.shape[0] * out_ref.shape[1] * out_ref.shape[2]
    cores, sides, places = out_ref.shape[:3]
    for at in range(count):
        place, rest = at // (cores * sides), at % (cores * sides)
        rows = [part[at * (part.shape[0] // count) : (at + 1) * (part.shape[0] // count), :] for part in parts]
        block = rows[0] if len(rows) == 1 else jnp.concatenate(rows, axis=0)
        out_ref[rest % cores, rest // cores, place] = block.astype(bf16)


def outer_kernel(low_ref, back_ref, unit_ref, dgate_ref, out_ref, out_sum, *gate_sums):
    step = pl.program_id(0)
    width = gate_sums[0].shape[1]

    @pl.when(step == 0)
    def _():
        out_sum[...] = dot_tn(low_ref[...], back_ref[...])
        for k, part in enumerate(gate_sums):
            part[...] = dot_tn(unit_ref[...], dgate_ref[:, k * width : (k + 1) * width])

    @pl.when(step > 0)
    def _():
        out_sum[...] = out_sum[...] + dot_tn(low_ref[...], back_ref[...])
        for k, part in enumerate(gate_sums):
            part[...] = part[...] + dot_tn(unit_ref[...], dgate_ref[:, k * width : (k + 1) * width])

    @pl.when(step == pl.num_programs(0) - 1)
    def _():
        store_blocks(out_ref, [out_sum] + list(gate_sums))


def branch_kernel(u_ref, meta_ref, low_ref, w_ref, out_ref):
    branch = dot(low_ref[...], w_ref[...].reshape(low_ref.shape[1], out_ref.shape[1]))
    out_ref[...] = (u_ref[...].astype(f32) + meta_ref[:, 0:1] * branch).astype(bf16)


def conv_back_kernel(
    act_ref, slope_ref, conv_ref, dx_ref, gm_ref, dbc_ref, dt_ref, cumdev_ref, raw_ref, xd_ref,
    da_ref, meta_ref, above_ref, prefix_ref, total_ref, skip_ref, taps_ref, heads_ref, rim_ref,
    ex_ref, red_ref, tri_ref, origin_ref, unit_ref, rim_unit_ref, gate_sums_ref,
    dconv_ref, first_ref, sums_ref, hsums_ref, grad_ref,
    dt_fresh, dt_kept, flow, v_all, turned, grad, reduced, *scratch,
    inner, conv_dim, num_heads, own_rows, slots,
):
    step = pl.program_id(0)
    blocks = pl.num_programs(0) - 1
    keep = meta_ref[0:1, 3:4]
    strips = conv_dim // STRIP
    fresh, kept, ext = scratch[:strips], scratch[strips : 2 * strips], scratch[2 * strips :]
    tiles = [slice(base, base + TILE) for base in range(0, SPAN, TILE)]
    origin = pl.multiple_of(origin_ref[0, 1], 8)

    def finish(s):
        part = kept[s // STRIP]
        for q in range(STRIP // LANES):
            lanes = slice(s + q * LANES, s + (q + 1) * LANES)
            for base in range(0, SPAN, TILE):
                total = taps_ref[3:4, lanes] * part[q, base : base + TILE, :]
                for k in range(3):
                    total = total + taps_ref[k : k + 1, lanes] * part[
                        q, pl.ds(origin + base + 3 - k, TILE), :
                    ]
                dconv_ref[base : base + TILE, lanes] = total.astype(bf16)

    def add_grad(cols):
        grad[:, cols] = grad[:, cols] + dot(turned[...], dconv_ref[:, cols])

    dconv_ref[:, conv_dim:] = dt_kept[...]

    @pl.when(step == 0)
    def _():
        rim_rows = jnp.concatenate(
            [jnp.zeros((SPAN - 16, rim_unit_ref.shape[1]), f32), rim_unit_ref[...].astype(f32)], axis=0
        )
        turned[...] = rim_rows.T.astype(bf16)
        grad[...] = jnp.zeros_like(grad)
        dt_kept[...] = jnp.zeros_like(dt_kept)
        dconv_ref[:, conv_dim:] = jnp.zeros_like(dt_kept)
        for part in kept:
            part[...] = jnp.zeros_like(part)
        for j, lanes in strips_of(conv_dim):
            ext[j // 2][j % 2, 0:8, :] = rim_ref[8:16, lanes].astype(f32) * keep
        sums_ref[...] = jnp.zeros_like(sums_ref)
        hsums_ref[...] = jnp.zeros_like(hsums_ref)
        start = jnp.zeros((16, LANES), f32)
        for s in range(0, inner, STRIP):
            cols = slice(s, s + STRIP)
            both = above_ref[:, cols].astype(f32) * prefix_ref[:, cols].astype(f32)
            start = start + dot(
                jnp.concatenate(two_terms(eight_rows(both)), axis=0), red_ref[cols, :]
            )
        start = jnp.sum(start, axis=0, keepdims=True)
        flow[...] = start * jnp.exp(total_ref[0:8, :]) * total_ref[8:16, :]

    @pl.when(step > 0)
    def _():
        turned[...] = unit_ref[...].astype(f32).T.astype(bf16)

    @pl.when((step > 0) & (step < blocks))
    def _():
        for part in ext:
            part[:, 0:8, :] = part[:, SPAN : SPAN + 8, :] * keep

    @pl.when(step < blocks)
    def _():
        b_rows = act_ref[:, inner : inner + LANES]
        dt_here = dt_ref[...]
        ahead = jnp.exp(total_ref[0:1, :] - cumdev_ref[...]) * meta_ref[:, 2:3]
        spread = split_lanes(jnp.concatenate([dt_here, ahead], axis=0))
        d_b = dbc_ref[:, :LANES]
        pending = [slice(conv_dim, conv_dim + LANES)]
        strips_here = list(range(0, inner, STRIP)) + [inner]
        products = {}

        def multiply(s):
            cols = slice(s, s + STRIP)
            products[s] = dot(spread, ex_ref[:, cols]), dot(b_rows, above_ref[:, cols])

        reduced[...] = jnp.zeros_like(reduced)
        multiply(0)
        for n, s in enumerate(strips_here):
            cols = slice(s, s + STRIP)
            new, old, rows_in = fresh[s // STRIP], kept[s // STRIP], ext[s // STRIP]
            for q in range(STRIP // LANES):
                lanes = slice(s + q * LANES, s + (q + 1) * LANES)
                rows_in[q, 8 : 8 + SPAN, :] = conv_ref[:, lanes].astype(f32)
            if n + 2 < len(strips_here):
                multiply(strips_here[n + 1])
            add_grad(pending.pop())
            if n > 0:
                done = slice(s - STRIP, s)
                reduced[...] = reduced[...] + dot(v_all[:, done], red_ref[done, :])
            if s < inner:
                wide, passed = products.pop(s)
                lows = []
                for rows in tiles:
                    dt_wide = wide[rows]
                    ahead_wide = wide[SPAN + rows.start : SPAN + rows.stop]
                    x = act_ref[rows, cols].astype(f32)
                    far = ahead_wide * passed[rows]
                    dx = dt_wide * (dx_ref[rows, cols].astype(f32) + far)
                    dx = dx + skip_ref[0:1, cols] * gm_ref[rows, cols].astype(f32)
                    dx = dx * slope_ref[rows, cols].astype(f32)
                    for q in range(STRIP // LANES):
                        new[q, rows, :] = dx[:, q * LANES : (q + 1) * LANES]
                    high, low = two_terms(x * far)
                    v_all[rows, cols] = high
                    v_all[SPAN + rows.start : SPAN + rows.stop, cols] = low
                    lows.append((x * dt_wide * ahead_wide).astype(bf16))
                d_b = d_b + dot_nt(jnp.concatenate(lows, axis=0), above_ref[:, cols])
            else:
                b_cols = slice(inner, inner + LANES)
                c_cols = slice(inner + LANES, inner + 2 * LANES)
                new[0, :, :] = d_b * slope_ref[:, b_cols].astype(f32)
                new[1, :, :] = dbc_ref[:, LANES:] * slope_ref[:, c_cols].astype(f32)
            for q in range(STRIP // LANES):
                lanes = slice(s + q * LANES, s + (q + 1) * LANES)
                sums = [jnp.zeros((8, LANES), f32) for _ in range(5)]
                for base in range(0, SPAN, TILE):
                    d = new[q, base : base + TILE, :]
                    sums[4] = sums[4] + eight_rows(d)
                    for k in range(4):
                        shifted = rows_in[q, pl.ds(origin + base + 5 + k, TILE), :]
                        sums[k] = sums[k] + eight_rows(d * shifted)
                for k in range(5):
                    here = slice(8 * k, 8 * k + 8)
                    sums_ref[here, lanes] = sums_ref[here, lanes] + sums[k]
            old[:, SPAN : SPAN + 8, :] = new[:, 0:8, :] * keep
            finish(s)
            pending.append(cols)
            old[:, 0:SPAN, :] = new[...]
        add_grad(pending.pop())
        x_dot = reduced[:SPAN] + reduced[SPAN:]
        moved = dt_here * x_dot
        rate = heads_ref[1:2, :]
        for c in range(SPAN // HALF):
            rows = slice(c * HALF, (c + 1) * HALF)
            da = da_ref[rows, :] + flow[0:1, :] + exact_dot(tri_ref[...], moved[rows]) - moved[rows]
            flow[...] = flow[...] + jnp.sum(moved[rows], axis=0, keepdims=True)
            hsums_ref[8:16, :] = hsums_ref[8:16, :] + eight_rows(da * rate * dt_here[rows])
            d_dt = xd_ref[rows, :] + x_dot[rows] + rate * da
            d_raw = meta_ref[rows, 0:1] * sigmoid(raw_ref[rows, :]) * d_dt
            real = lax.broadcasted_iota(jnp.int32, d_raw.shape, 1) < num_heads
            d_raw = jnp.where(real, d_raw, 0.0)
            hsums_ref[0:8, :] = hsums_ref[0:8, :] + eight_rows(d_raw)
            dt_fresh[rows, :] = d_raw.astype(bf16)

    @pl.when(step == 0)
    def _():
        for j, lanes in strips_of(conv_dim):
            first_ref[:, lanes] = fresh[j // 2][j % 2, 0:8, :] * keep

    @pl.when(step == blocks)
    def _():
        for s in range(0, conv_dim, STRIP):
            kept[s // STRIP][:, SPAN : SPAN + 8, :] = jnp.zeros((2, 8, LANES), f32)
            finish(s)
            add_grad(slice(s, s + STRIP))
        add_grad(slice(conv_dim, conv_dim + LANES))
        tap_rows = [
            0.5 * jnp.sum(sums_ref[8 * k : 8 * k + 8, :], axis=0, keepdims=True) for k in range(5)
        ]
        gate_row = jnp.sum(gate_sums_ref[...], axis=0, keepdims=True)
        model = grad.shape[0]
        vecs = jnp.concatenate([jnp.zeros((1, model), f32), gate_row, tap_rows[4]], axis=1)
        taps_at = [0] * 4
        vec_at = 0
        for r in range(model // own_rows):
            row_parts = {}
            for k, (row, lane, size) in enumerate(slots):
                if k < 4:
                    part = tap_rows[k][:, taps_at[k] : taps_at[k] + size]
                    taps_at[k] += size
                else:
                    part = vecs[:, vec_at : vec_at + size]
                    vec_at += size
                row_parts.setdefault(row, []).append((lane, size, part))
            for row, parts in row_parts.items():
                lane, size = parts[-1][0], parts[-1][1]
                at = r * own_rows + row
                here = slice(conv_dim + num_heads, conv_dim + num_heads + lane + size)
                grad[at : at + 1, here] = jnp.concatenate([part for _, _, part in parts], axis=1)
        store_blocks(grad_ref, [grad])

    dt_kept[...] = dt_fresh[...]


def input_grad_kernel(
    dconv_ref, dgate_ref, near_ref, far_ref, u_ref, cot_ref, gain_ref, *refs
):
    cut = near_ref.shape[1]
    grad = dot_nt(dconv_ref[:, :cut], near_ref[...]) + dot_nt(dconv_ref[:, cut:], far_ref[...])
    out_ref, gates = refs[-1], refs[:-1]
    width = gates[0].shape[1]
    side = dot_nt(dgate_ref[:, :width], gates[0][...])
    for k in range(1, len(gates)):
        side = side + dot_nt(dgate_ref[:, k * width : (k + 1) * width], gates[k][...])
    grad = grad + 0.5 * side
    for base in range(0, u_ref.shape[0], TILE):
        rows = slice(base, base + TILE)
        wide = u_ref[rows, :].astype(f32)
        factor = lax.rsqrt(jnp.mean(wide * wide, axis=-1, keepdims=True) + EPS_NORM)
        unit = wide * factor
        d = grad[rows] * gain_ref[...]
        mean = jnp.mean(d * unit, axis=-1, keepdims=True)
        du = factor * (d - unit * mean)
        out_ref[rows, :] = (cot_ref[rows, :].astype(f32) + du).astype(bf16)


def place_sum_kernel(parts_ref, out_ref):
    out_ref[...] = jnp.sum(parts_ref[...].astype(f32), axis=0)


def owner_kernel(
    conv_ref, both_ref, w_ref, gain_ref, heads_ref, in_ref, out_ref, small_sum_ref, row_ref,
    *, num_heads, slots,
):
    conv = jnp.sum(conv_ref[...].astype(f32), axis=0)
    both = both_ref[...]
    own_rows, width = in_ref.shape
    out_rows, side = out_ref.shape
    out_sum = both[:out_rows]
    out_ref[...] = out_sum
    spare = conv[:, conv.shape[1] - LANES :]
    small_sum_ref[...] = jnp.zeros_like(small_sum_ref)
    squares = jnp.sum(out_sum * out_sum)
    vec_at = 0
    for k, (row, lane, size) in enumerate(slots):
        part = spare[row : row + 1, num_heads + lane : num_heads + lane + size]
        squares = squares + jnp.sum(part * part)
        if k < 4:
            small_sum_ref[1 + k : 2 + k, :size] = part
        else:
            small_sum_ref[0:1, vec_at : vec_at + size] = part
            vec_at += size
    gates = (both.shape[0] - out_rows) // own_rows
    gain = gain_ref[...]
    norm_rows = jnp.zeros((own_rows, 1), f32)
    tail = width - gates * side
    pieces = [
        (k * side, 0.5 * both[out_rows + k * own_rows : out_rows + (k + 1) * own_rows]) for k in range(gates)
    ] + [(gates * side, conv[:, :tail])]
    for at, piece in pieces:
        cols = slice(at, at + piece.shape[1])
        scaled = piece * gain
        in_ref[:, cols] = scaled
        squares = squares + jnp.sum(scaled * scaled)
        norm_rows = norm_rows + jnp.sum(
            piece * w_ref[:, cols].astype(bf16).astype(f32), axis=1, keepdims=True
        )
    squares = squares + jnp.sum(norm_rows * norm_rows)
    lane = lax.broadcasted_iota(jnp.int32, (own_rows, LANES), 1)
    row = lax.broadcasted_iota(jnp.int32, (own_rows, LANES), 0)
    spread = jnp.where(lane == 3 * num_heads + 1 + row, jnp.broadcast_to(norm_rows, lane.shape), 0.0)
    first_lane = lax.broadcasted_iota(jnp.int32, (1, LANES), 1)
    packed = (
        heads_ref[...]
        + jnp.where(first_lane == 3 * num_heads, squares, 0.0)
        + jnp.sum(spread, axis=0, keepdims=True)
    )
    row_ref[...] = jnp.broadcast_to(packed[None], row_ref.shape)


def update_kernel(*refs, num_heads, own_rows, taps_own):
    rank_ref, rows_ref, in_sum_ref, out_sum_ref, small_ref = refs[:5]
    states, norm_ref, outs = refs[5:20], refs[20], refs[21:]
    rows = rows_ref[:, 0, :]
    total = jnp.sum(rows, axis=0, keepdims=True)
    lane = lax.broadcasted_iota(jnp.int32, (1, LANES), 1)
    heads = jnp.concatenate(
        [total[:, k * num_heads : (k + 1) * num_heads] for k in range(3)], axis=0
    )
    norm_sq = (
        jnp.sum(jnp.where(lane == 3 * num_heads, total, 0.0), axis=1, keepdims=True)
        + jnp.sum(jnp.sum(heads * heads, axis=0, keepdims=True), axis=1, keepdims=True)
    )
    grad_norm = jnp.sqrt(norm_sq)
    norm_ref[...] = grad_norm
    factor = jnp.minimum(1.0, MAX_NORM / (grad_norm + 1e-06))
    vec_width = states[9].shape[1]
    place = lax.broadcasted_iota(jnp.int32, (rows.shape[0], vec_width), 0)
    wanted = rank_ref[0, 0] * vec_width + lax.broadcasted_iota(jnp.int32, (rows.shape[0], vec_width), 1)
    mine = jnp.zeros((rows.shape[0], vec_width), f32)
    for j in range(own_rows):
        at = 3 * num_heads + 1 + j
        here = jnp.broadcast_to(rows[:, at : at + 1], mine.shape)
        mine = mine + jnp.where(place * own_rows + j == wanted, here, 0.0)
    vec = small_ref[0:1, :vec_width] + jnp.sum(mine, axis=0, keepdims=True)
    sums = (in_sum_ref[...], out_sum_ref[...], small_ref[1:5, :taps_own], vec, heads)
    rates = (
        (RATE_MAT, DECAY_MAT), (RATE_MAT, DECAY_MAT), (RATE_CONV, DECAY_MAT), (RATE_VEC, 0.0),
        (RATE_HEAD, 0.0),
    )
    for k, (summed, (rate, decay)) in enumerate(zip(sums, rates)):
        master, first, second = (ref[...] for ref in states[3 * k : 3 * k + 3])
        clipped_ref, first_ref, second_ref, master_ref, copy_ref = outs[5 * k : 5 * k + 5]
        clipped = summed * factor
        clipped_ref[...] = clipped
        first = BETA_ONE * first + (1.0 - BETA_ONE) * clipped
        second = BETA_TWO * second + (1.0 - BETA_TWO) * clipped * clipped
        first_ref[...] = first
        second_ref[...] = second
        first_hat = first / (1.0 - BETA_ONE**STEP)
        second_hat = second / (1.0 - BETA_TWO**STEP)
        master = master - rate * (first_hat / (jnp.sqrt(second_hat) + ADAM_EPS) + decay * master)
        master_ref[...] = master
        copy_ref[...] = master.astype(bf16)


def shift(value, axis, steps):
    count = lax.axis_size(axis)
    initial, last = (max(0, -steps), min(count, count - steps))
    return lax.ppermute(value, axis, [(source, source + steps) for source in range(initial, last)])


def axis_bits(axis):
    return [(axis, 1 << k) for k in reversed(range(lax.axis_size(axis).bit_length() - 1))]


def swap(value, axis, bit):
    count = lax.axis_size(axis)
    return lax.ppermute(value, axis, [(k, k ^ bit) for k in range(count)])


def my_bit(axis, bit):
    return (lax.axis_index(axis) // bit) % 2


def zero_from(value):
    return jnp.minimum(jnp.abs(value[(0,) * value.ndim].astype(f32)), 0.0)


def rank_bits():
    return axis_bits("seq") + axis_bits("rep")


def gather_step(value, known, axis, bit):
    order = rank_bits()
    place = sum(order.index(k) < order.index((axis, bit)) for k in known)
    other = swap(value, axis, bit)
    value = jnp.where(
        my_bit(axis, bit) == 0,
        jnp.stack([value, other], axis=place),
        jnp.stack([other, value], axis=place),
    )
    return value, known + [(axis, bit)]


def gather_ring(value, axis, stride):
    count = lax.axis_size(axis)
    groups = count // stride
    parts = [value]
    for k in range(1, groups):
        parts.append(lax.ppermute(value, axis, [(i, (i - k * stride) % count) for i in range(count)]))
    mine = lax.axis_index(axis) // stride
    return lax.dynamic_slice_in_dim(jnp.stack(parts + parts), (groups - mine) % groups, groups, 0)


def gather_steps(value, known, steps):
    for axis, bit in steps:
        value, known = gather_step(value, known, axis, bit)
    return value, known


def halve_step(value, axis, bit, token=0, done=0):
    mine = my_bit(axis, bit)
    given = lax.dynamic_index_in_dim(value, 1 - mine + token, 0, keepdims=False)
    held = lax.dynamic_index_in_dim(value, mine + done, 0, keepdims=False)
    return (held.astype(f32) + swap(given, axis, bit).astype(f32)).astype(bf16)


def call(kernel, grid, ins, in_blocks, outs, out_blocks, scratch, flops, after=(), token=False, passed=0, **fixed):
    first = len(after)
    own_outs = len(outs)
    if token:
        outs = outs + [like(1, 1, dtype=jnp.int32)]
        out_blocks = out_blocks + [pl.BlockSpec(memory_space=pltpu.SMEM)]

    def body(*refs):
        refs = list(refs[first:])
        if token:
            refs.pop(count_in + own_outs)[0, 0] = jnp.int32(0)
        del refs[count_in + own_outs : count_in + own_outs + passed]
        kernel(*refs, **fixed)

    count_in = len(ins)
    aliases = {k: len(outs) + k for k in range(passed)}
    outs = outs + [like(*v.shape, dtype=v.dtype) for v in after[:passed]]
    out_blocks = out_blocks + [pl.BlockSpec(memory_space=pl.ANY)] * passed
    ins = list(after) + ins
    in_blocks = [pl.BlockSpec(memory_space=pl.ANY)] * first + in_blocks
    moved = sum(v.size * v.dtype.itemsize for v in ins) + sum(v.size * v.dtype.itemsize for v in outs)
    return pl.pallas_call(
        body,
        name=kernel.__name__,
        grid=(grid,),
        in_specs=in_blocks,
        out_specs=out_blocks,
        out_shape=outs,
        scratch_shapes=scratch,
        input_output_aliases=aliases,
        compiler_params=pltpu.CompilerParams(
            dimension_semantics=("arbitrary",), vmem_limit_bytes=VMEM_BYTES
        ),
        cost_estimate=pl.CostEstimate(flops=int(flops), bytes_accessed=moved, transcendentals=0),
    )(*ins)


def full(shape):
    return pl.BlockSpec(shape, lambda i: (0,) * len(shape))


def rows_of(count, width, index=lambda i: i):
    return pl.BlockSpec((count, width), lambda i: (index(i), 0))


def like(*shape, dtype=f32):
    return jax.ShapeDtypeStruct(shape, dtype)


def shards(
    tokens,
    cotangent,
    seq_lengths,
    in_weight,
    in_first,
    in_second,
    out_weight,
    out_first,
    out_second,
    conv_weight,
    conv_first,
    conv_second,
    vectors,
    vec_first,
    vec_second,
    head_params,
    head_first,
    head_second,
):
    u = tokens[0]
    cot = cotangent[0]
    rows, model = u.shape
    places = lax.axis_size("seq")
    ranks = places * lax.axis_size("rep")
    taps_own = conv_weight.shape[1]
    vecs_own = vectors.shape[0]
    conv_dim = taps_own * ranks
    inner = out_weight.shape[0] * ranks
    heads = head_params.shape[1]
    head_dim = inner // heads
    nblk = rows // SPAN
    quarter = rows // 4
    third = rows // 3
    wide = conv_dim + LANES
    cut = -(-wide // (2 * STRIP)) * STRIP

    own_rows, out_rows = in_weight.shape[0], out_weight.shape[0]
    sides = inner // model
    start = (lax.axis_index("seq") * rows).astype(jnp.int32)
    offset = jnp.stack([start, jnp.zeros_like(start)]).reshape(1, 2)
    bits = rank_bits()
    far_steps = [k for k in bits if k[0] == "seq" and k[1] > 1][::-1]
    near_step, rep_steps = ("seq", 1), axis_bits("rep")
    before = shift(u[rows - 16 :], "seq", 1)
    in_low = in_weight.astype(bf16)
    spare_lanes = LANES - heads
    pieces = [conv_weight[k] for k in range(4)]
    pieces += [vectors[at : at + LANES // 2] for at in range(0, vecs_own, LANES // 2)]
    slots, spare_rows, fill = [], [[]], 0
    for piece in pieces:
        size = piece.shape[0]
        if fill + size > spare_lanes:
            spare_rows.append([])
            fill = 0
        slots.append((len(spare_rows) - 1, fill, size))
        spare_rows[-1].append(piece)
        fill += size
    spare_rows = [jnp.concatenate(row) for row in spare_rows]
    spare = jnp.stack([jnp.pad(row, (0, spare_lanes - row.shape[0])) for row in spare_rows])
    spare = jnp.pad(spare, ((0, own_rows - len(spare_rows)), (0, 0))).astype(bf16)
    conv_shard = jnp.concatenate([in_low[:, inner:], spare], axis=1)
    known = far_steps[::-1]
    if len(known) == 2:
        shard = gather_ring(conv_shard, "seq", 2)
        shard = shard.reshape((2, 2) + conv_shard.shape)
    else:
        shard, _ = gather_steps(conv_shard, [], far_steps)
    w_near, known_near = gather_steps(shard[..., :cut], known, [near_step])
    w_far, known_far = gather_steps(shard[..., cut:], known, rep_steps[:1])
    w_near, known_near = gather_steps(w_near, known_near, rep_steps[:1])
    w_far, known_far = gather_steps(w_far, known_far, [near_step])
    w_near, _ = gather_steps(w_near, known_near, rep_steps[1:])
    w_far, _ = gather_steps(w_far, known_far, rep_steps[1:])
    w_near = w_near.reshape(model, cut)
    w_far = w_far.reshape(model, wide - cut)
    others = [out_weight.astype(bf16)] + [in_low[:, s : s + model] for s in range(0, inner, model)]
    others = lax.all_gather(jnp.concatenate(others, axis=0), ("seq", "rep"), axis=0)
    if own_rows % 8 == 0:
        out_part, gate_parts = others, [others] * sides
        b_out_w = pl.BlockSpec((ranks, out_rows, model), lambda i: (0, 0, 0))
        b_gates = [
            pl.BlockSpec((ranks, own_rows, model), lambda i, at=out_rows // own_rows + k: (0, at, 0))
            for k in range(sides)
        ]
    else:
        out_part = others[:, :out_rows].reshape(1, inner, model)
        gate_parts = [
            others[:, out_rows + k * own_rows : out_rows + (k + 1) * own_rows].reshape(1, model, model)
            for k in range(sides)
        ]
        b_out_w, b_gates = full((1, inner, model)), [full((1, model, model))] * sides

    head_rows = jnp.stack([head_params[0], -jnp.exp(head_params[1])])
    head_rows = jnp.pad(head_rows, ((0, 6), (0, LANES - heads)))
    skip_wide = jnp.repeat(head_params[2], head_dim)[None]

    lane_head = np.arange(inner) // head_dim
    spread = (np.arange(LANES)[:, None] == lane_head[None]).astype(np.float32)
    ex = jnp.asarray(np.concatenate([spread, spread], axis=0), bf16)
    red = jnp.asarray(spread.T, bf16)
    order = np.arange(HALF)
    tri = jnp.asarray((order[:, None] >= order[None]).astype(np.float32), bf16)
    tri_up = jnp.asarray((order[:, None] <= order[None]).astype(np.float32), bf16)

    b_act = rows_of(SPAN, conv_dim)
    b_in = rows_of(SPAN, inner)
    b_lane = rows_of(SPAN, LANES)
    b_model = rows_of(SPAN, model)
    b_meta = rows_of(SPAN, 8)
    b_ex = full((2 * LANES, inner))
    b_red = full((inner, LANES))
    b_tri = full((HALF, HALF))
    b_heads = full((8, LANES))
    b_state = full((LANES, inner))
    b_one = full((1, inner))
    b_scalar = pl.BlockSpec(memory_space=pltpu.SMEM)
    q_model = rows_of(quarter, model)
    q_in = rows_of(quarter, inner)
    q_meta = rows_of(quarter, 8)
    t_model = rows_of(third, model)
    t_in = rows_of(third, inner)
    lane_out = like(rows, LANES)
    low_in = like(rows, inner, dtype=bf16)
    low_conv = like(rows, conv_dim, dtype=bf16)
    low_model = like(rows, model, dtype=bf16)
    strip_scratch = pltpu.VMEM((STRIP // LANES, SPAN + 8, LANES), f32)
    strips = conv_dim // STRIP

    (
        unit, normed, conv_in, act, slope, meta, dt_values, cumul, cumdev, raw, own_inc, starts, rim,
        rim_unit, state_out, total, half_taps, norm_gain, gate_gain, _,
    ) = call(
        front_kernel,
        nblk,
        [
            seq_lengths, offset, u, before, w_near, w_far, head_rows, ex, tri,
        ],
        [
            b_scalar, b_scalar, b_model, full((16, model)), full((model, cut)),
            full((model, wide - cut)), b_heads, b_ex, b_tri,
        ],
        [
            low_model, low_model, low_conv, low_conv, low_conv, like(rows, 8),
            lane_out, lane_out, lane_out, lane_out, low_in, like(16 * nblk, inner),
            like(16, conv_dim, dtype=bf16), like(16, model, dtype=bf16),
            like(LANES, inner + LANES, dtype=bf16), like(16, LANES), like(4, conv_dim), like(1, model),
            like(1, inner), like(1, conv_dim),
        ],
        [
            b_model, b_model, b_act, b_act, b_act, b_meta, b_lane, b_lane, b_lane, b_lane, b_in,
            rows_of(16, inner), full((16, conv_dim)), full((16, model)),
            full((LANES, inner + LANES)), full((16, LANES)), full((4, conv_dim)), full((1, model)), b_one,
            full((1, conv_dim)),
        ],
        [pltpu.VMEM((LANES, inner), f32), pltpu.VMEM((8, LANES), f32)] + [strip_scratch] * strips,
        2 * rows * model * wide * 4,
        conv_dim=conv_dim,
        inner=inner,
        places=places,
        num_rows=rows,
        own_rows=own_rows,
        slots=tuple(slots),
        heads=heads,
    )

    def chain(states, gains, reverse, after, passed=0):
        whole = (places, LANES // places, inner)
        return call(
            chain_kernel, 1, [states, gains, ex],
            [full(states.shape), full(gains.shape), b_ex],
            [like(*whole, dtype=bf16)], [full(whole)], [], 1e7, after, passed=passed, reverse=reverse,
        )

    def exchange(blocks):
        return lax.all_to_all(blocks, "seq", 0, 0, tiled=True)

    arrived = exchange(state_out.reshape(places, LANES // places, inner + LANES))
    gains = arrived[:, :2, inner:]
    y_own = call(
        intra_kernel,
        nblk,
        [act, dt_values, cumul, own_inc, ex],
        [b_act, b_lane, b_lane, b_in, b_ex],
        [like(rows, inner)],
        [b_in],
        [],
        2 * rows * model * inner * 4,
        inner=inner,
    )[0]
    chained = chain(arrived, gains, False, [y_own])[0]
    prefix = exchange(chained).reshape(LANES, inner)
    gate_in, grad_gated, back_rows, *w_gates = call(
        project_kernel,
        4,
        [normed, meta, cot, out_part] + gate_parts,
        [q_model, q_meta, q_model, b_out_w] + b_gates,
        [low_in, low_in, low_model] + [like(model, model, dtype=bf16)] * sides,
        [q_in, q_in, q_model] + [full((model, model))] * sides,
        [],
        2 * rows * model * inner * 2,
        [chained],
        inner=inner,
        sides=sides,
    )

    wide_scratch = pltpu.VMEM((SPAN, inner), f32)
    gated_low, grad_mixed, grad_gate, r_sums, gdev, gate_sums = call(
        gate_kernel,
        nblk,
        [
            y_own, act, prefix, cumdev, meta, gate_in, grad_gated, skip_wide, gate_gain, ex, red,
        ],
        [b_in, b_act, b_state, b_lane, b_meta, b_in, b_in, b_one, b_one, b_ex, b_red],
        [low_in, low_in, low_in, lane_out, like(LANES, inner, dtype=bf16), like(8, inner)],
        [b_in, b_in, b_in, b_lane, b_state, full((8, inner))],
        [wide_scratch] * 5
        + [
            pltpu.VMEM((SPAN, inner), bf16),
            pltpu.VMEM((2 * SPAN, inner), bf16),
            pltpu.VMEM((LANES, inner), f32),
        ],
        2 * rows * model * inner * 3,
        inner=inner,
    )

    gathered = exchange(gdev.reshape(places, LANES // places, inner))
    block_shape = tuple(lax.axis_size("rep") // 2 if k == 0 else 2 for k in range(2))[::-1] + (places,)
    rep_shape = (lax.axis_size("rep"), 1, places)
    both_grad = call(
        outer_kernel,
        3,
        [gated_low, back_rows, unit, grad_gate],
        [t_in, t_model, t_model, t_in],
        [like(*rep_shape, out_rows + sides * own_rows, model, dtype=bf16)],
        [full(rep_shape + (out_rows + sides * own_rows, model))],
        [pltpu.VMEM((inner, model), f32)] + [pltpu.VMEM((model, model), f32)] * sides,
        2 * rows * model * inner * 2,
    )[0]
    chained_back, both_grad = chain(gathered, gains, True, [both_grad], passed=1)
    above = exchange(chained_back).reshape(LANES, inner)
    both_all = exchange(lax.psum_scatter(both_grad[:, 0], "rep", scatter_dimension=0, tiled=True)[0])

    flip = lambda i: nblk - 1 - i
    f_lane = rows_of(SPAN, LANES, flip)
    f_in = rows_of(SPAN, inner, flip)
    dx_own, dbc_own, xd_own, da_own, skip_sums = call(
        intra_back_kernel,
        nblk,
        [
            act, grad_mixed, dt_values, cumul, meta, own_inc, starts, prefix, r_sums, red, tri_up,
        ],
        [
            rows_of(SPAN, conv_dim, flip), f_in, f_lane, f_lane, rows_of(SPAN, 8, flip), f_in,
            rows_of(16, inner, flip), b_state, f_lane, b_red, b_tri,
        ],
        [low_in, like(rows, 2 * LANES), lane_out, lane_out, like(8, inner)],
        [f_in, rows_of(SPAN, 2 * LANES, flip), f_lane, f_lane, full((8, inner))],
        [
            pltpu.VMEM((LANES, inner), f32),
            pltpu.VMEM((8, LANES), f32),
            pltpu.VMEM((2 * SPAN + 32, inner), bf16),
        ]
        + [pltpu.VMEM((SPAN // HALF, HALF, LANES), f32)] * 3
        + [pltpu.VMEM((2 * SPAN + 32, LANES), f32)],
        2 * rows * model * inner * 6,
        [chained_back],
        inner=inner,
    )
    capped = lambda i: jnp.minimum(i, nblk - 1)
    late = lambda i: jnp.maximum(i - 1, 0)
    c_lane = rows_of(SPAN, LANES, capped)
    c_in = rows_of(SPAN, inner, capped)
    c_act = rows_of(SPAN, conv_dim, capped)
    dconv, first_rows, _, head_sum_rows, conv_grad = call(
        conv_back_kernel,
        nblk + 1,
        [
            act, slope, conv_in, dx_own, grad_mixed, dbc_own, dt_values, cumdev, raw, xd_own, da_own,
            meta, above, prefix, total, skip_wide, half_taps, head_rows, rim, ex, red, tri,
            offset, unit, rim_unit, gate_sums,
        ],
        [
            c_act, c_act, c_act, c_in, c_in, rows_of(SPAN, 2 * LANES, capped), c_lane, c_lane, c_lane,
            c_lane, c_lane, rows_of(SPAN, 8, capped), b_state, b_state,
            full((16, LANES)), b_one, full((4, conv_dim)), b_heads, full((16, conv_dim)),
            b_ex, b_red, b_tri, b_scalar, rows_of(SPAN, model, late), full((16, model)), full((8, inner)),
        ],
        [
            like(rows, wide, dtype=bf16), like(8, conv_dim), like(40, conv_dim), like(16, LANES),
            like(*block_shape, own_rows, wide, dtype=bf16),
        ],
        [
            rows_of(SPAN, wide, late), full((8, conv_dim)), full((40, conv_dim)), full((16, LANES)),
            full(block_shape + (own_rows, wide)),
        ],
        [
            pltpu.VMEM((SPAN, LANES), bf16),
            pltpu.VMEM((SPAN, LANES), bf16),
            pltpu.VMEM((8, LANES), f32),
            pltpu.VMEM((2 * SPAN, inner), bf16),
            pltpu.VMEM((model, SPAN), bf16),
            pltpu.VMEM((model, wide), f32),
            pltpu.VMEM((2 * SPAN, LANES), f32),
        ]
        + [pltpu.VMEM((STRIP // LANES, SPAN, LANES), f32)] * strips
        + [strip_scratch] * (2 * strips),
        2 * rows * model * inner * 3,
        inner=inner,
        conv_dim=conv_dim,
        num_heads=heads,
        own_rows=own_rows,
        slots=tuple(slots),
    )
    after = shift(first_rows, "seq", -1)
    late_rows = jnp.stack(
        [sum(half_taps[k] * after[j - k] for k in range(j + 1)) for j in range(3)]
    )
    tail = dconv[rows - 16 :, :conv_dim].astype(f32) + jnp.pad(late_rows, ((13, 0), (0, 0)))
    dconv = lax.dynamic_update_slice(dconv, tail.astype(bf16), (rows - 16, 0))


    conv_part = halve_step(conv_grad, *rep_steps[1])
    block_out = call(
        branch_kernel,
        4,
        [u, meta, gated_low, out_part],
        [q_model, q_meta, q_in, b_out_w],
        [low_model],
        [q_model],
        [],
        2 * rows * model * inner,
        [conv_part],
    )[0]
    both_sum, both_token = call(
        place_sum_kernel, 1, [both_all], [full(both_all.shape)], [like(*both_all.shape[1:])],
        [full(both_all.shape[1:])], [], 1e6, [block_out], token=True,
    )
    conv_part = halve_step(conv_part, *rep_steps[0], done=both_token[0, 0])
    input_grad = call(
        input_grad_kernel,
        4,
        [dconv, grad_gate, w_near, w_far, u, cot, norm_gain] + w_gates,
        [
            rows_of(quarter, wide), q_in, full((model, cut)), full((model, wide - cut)),
            q_model, q_model, full((1, model)),
        ]
        + [full((model, model))] * sides,
        [low_model],
        [q_model],
        [],
        2 * rows * model * (wide + inner),
        [conv_part],
    )[0]
    conv_all = exchange(conv_part)

    rank = lax.axis_index("seq") * lax.axis_size("rep") + lax.axis_index("rep")
    own_gain = lax.dynamic_slice_in_dim(norm_gain[0], rank * own_rows, own_rows)[:, None]
    grad_skip = jnp.sum(jnp.sum(skip_sums, axis=0).reshape(heads, head_dim), axis=1)
    head_local = jnp.concatenate(
        [
            jnp.sum(head_sum_rows.reshape(2, 8, LANES), axis=1)[:, :heads].reshape(-1),
            grad_skip,
        ]
    )
    head_local = jnp.pad(head_local, (0, LANES - 3 * heads))[None]
    small_shape = (8, LANES)
    in_sum, out_sum, small_sum, row = call(
        owner_kernel,
        1,
        [conv_all, both_sum, in_weight, own_gain, head_local],
        [full(v.shape) for v in (conv_all, both_sum, in_weight, own_gain, head_local)],
        [like(*in_weight.shape), like(*out_weight.shape), like(*small_shape), like(ranks, 1, LANES)],
        [full(in_weight.shape), full(out_weight.shape), full(small_shape), full((ranks, 1, LANES))],
        [],
        1e6,
        [input_grad],
        num_heads=heads,
        slots=tuple(slots),
    )
    all_rows = lax.all_to_all(row, ("seq", "rep"), 0, 0, tiled=True)
    states = [
        in_weight, in_first, in_second, out_weight, out_first, out_second, conv_weight, conv_first,
        conv_second, vectors[None], vec_first[None], vec_second[None], head_params, head_first, head_second,
    ]
    shapes = [states[3 * k].shape for k in range(5)]
    updated = call(
        update_kernel,
        1,
        [rank.astype(jnp.int32).reshape(1, 1), all_rows, in_sum, out_sum, small_sum] + states,
        [b_scalar]
        + [full(v.shape) for v in [all_rows, in_sum, out_sum, small_sum] + states],
        [like(1, 1)]
        + [like(*shape, dtype=kind) for shape in shapes for kind in (f32, f32, f32, f32, bf16)],
        [full((1, 1))] + [full(shape) for shape in shapes for _ in range(5)],
        [],
        1e6,
        num_heads=heads,
        own_rows=own_rows,
        taps_own=taps_own,
    )
    grad_norm, updated = updated[0][0, 0], list(updated[1:])
    updated[15:20] = [v[0] for v in updated[15:20]]
    return (block_out[None], input_grad[None], grad_norm) + tuple(updated)


def solution(mesh):
    tokens = P("rep", "seq", None)
    row_split = P(("seq", "rep"), None)
    column_split = P(None, ("seq", "rep"))
    flat_split = P(("seq", "rep"))
    return jax.shard_map(
        shards,
        mesh=mesh,
        in_specs=(tokens, tokens, P("rep", None))
        + (row_split,) * 6
        + (column_split,) * 3
        + (flat_split,) * 3
        + (P(),) * 3,
        out_specs=(tokens, tokens, P())
        + (row_split,) * 10
        + (column_split,) * 5
        + (flat_split,) * 5
        + (P(),) * 5,
        check_vma=False,
    )
```

```python
import jax
import jax.numpy as jnp
import numpy as np
from jax import lax
from jax.experimental import pallas as pl
from jax.experimental.pallas import tpu as pltpu
from jax.sharding import PartitionSpec as P

SPAN = 256
HALF = 128
LANES = 128
STRIP = 256
TILE = 64
STEP = 10

EPS_NORM = 1e-05
MAX_NORM = 1.0
BETA_ONE = 0.9
BETA_TWO = 0.95
ADAM_EPS = 1e-08
DECAY_MAT = 0.1
RATE_MAT = 0.05
RATE_CONV = 0.5
RATE_VEC = 1.0
RATE_HEAD = 2.0
LOG2E = 1.4426950408889634
VMEM_BYTES = 58 * 1024 * 1024

f32 = jnp.float32
bf16 = jnp.bfloat16


def dot(a, b):
    return jnp.dot(a, b, preferred_element_type=f32)


def dot_nt(a, b):
    return lax.dot_general(a, b, (((1,), (1,)), ((), ())), preferred_element_type=f32)


def dot_tn(a, b):
    return lax.dot_general(a, b, (((0,), (0,)), ((), ())), preferred_element_type=f32)


def two_terms(v):
    high = v.astype(bf16)
    return high, (v - high.astype(f32)).astype(bf16)


def split_lanes(v):
    return jnp.concatenate(two_terms(v), axis=-1)


def exact_dot(ones_matrix, v):
    high, rest = two_terms(v)
    middle, low = two_terms(v - high.astype(f32))
    return dot(ones_matrix, high) + (dot(ones_matrix, middle) + dot(ones_matrix, low))


def sigmoid(v):
    return 0.5 * jnp.tanh(0.5 * v) + 0.5


def low_half(shape):
    return lax.broadcasted_iota(jnp.int32, shape, 1) < LANES // 2


def block_diag(pair):
    low_lanes = low_half(pair.shape)
    none = jnp.zeros_like(pair)
    return jnp.concatenate(
        [jnp.where(low_lanes, pair, none), jnp.where(low_lanes, none, pair)], axis=0
    )


def column(v, h):
    return jnp.broadcast_to(v[:, h : h + 1], (v.shape[0], LANES))


def eight_rows(v):
    return jnp.sum(v.reshape(v.shape[0] // 8, 8, v.shape[1]), axis=0)


def row_norm(rows, gain):
    wide = rows.astype(f32)
    factor = lax.rsqrt(jnp.mean(wide * wide, axis=-1, keepdims=True) + EPS_NORM)
    return (wide * factor * gain).astype(bf16)


def strips_of(width):
    return [(j, slice(j * LANES, (j + 1) * LANES)) for j in range(width // LANES)]


def shifted_sum(taps_ref, lanes, source, q, start, total):
    for k in range(4):
        total = total + taps_ref[k : k + 1, lanes] * source[q, pl.ds(start + k, TILE), :]
    return total


def front_kernel(
    lengths_ref, offset_ref, u_ref, before_ref, near_ref, far_ref, heads_ref,
    ex_ref, tri_ref,
    unit_ref, normed_ref, conv_ref, act_ref, slope_ref, meta_ref, dt_ref, cum_ref, cumdev_ref, raw_ref,
    inc_ref, start_ref, rim_ref, rim_unit_ref, state_out_ref, total_ref, taps_ref, gain_ref,
    gate_gain_ref, bias_ref, state, offset, *ext,
    conv_dim, inner, places, num_rows, own_rows, slots, heads,
):
    step = pl.program_id(0)
    cut = near_ref.shape[1]

    @pl.when(step == 0)
    def _():
        spare = far_ref[:, conv_dim - cut :].astype(f32)
        model = spare.shape[0]

        def piece(r, k):
            row, lane, size = slots[k]
            return spare[r * own_rows + row : r * own_rows + row + 1, heads + lane : heads + lane + size]

        ranks = range(model // own_rows)
        for k in range(4):
            taps_ref[k : k + 1, :] = 0.5 * jnp.concatenate([piece(r, k) for r in ranks], axis=1)
        vecs = jnp.concatenate([piece(r, k) for r in ranks for k in range(4, len(slots))], axis=1)
        gain_ref[...] = vecs[:, :model]
        gate_gain_ref[...] = vecs[:, model : model + inner]
        bias_ref[...] = 0.5 * vecs[:, model + inner :]

    gain = gain_ref[...]

    device_start = offset_ref[0, 0]
    row = lax.broadcasted_iota(jnp.int32, (SPAN, 8), 0)
    flag = lax.broadcasted_iota(jnp.int32, (SPAN, 8), 1)
    position = device_start + step * SPAN + row
    begin = jnp.int32(0)
    first = jnp.zeros((SPAN, 8), jnp.int32)
    last_first = jnp.int32(0)
    live = jnp.zeros((SPAN, 8), jnp.bool_)
    for k in range(lengths_ref.shape[1]):
        length = lengths_ref[0, k]
        after = position >= begin
        first = jnp.where(after, begin, first)
        last_first = jnp.where(device_start + num_rows - 1 >= begin, begin, last_first)
        live = live | (after & (position < begin + length))
        begin = begin + (length + SPAN - 1) // SPAN * SPAN
    meta = jnp.where(
        flag == 0,
        live.astype(f32),
        jnp.where(
            flag == 1,
            (first < device_start).astype(f32),
            jnp.where(
                flag == 2,
                (first == last_first).astype(f32),
                (first < position - (row & (HALF - 1))).astype(f32),
            ),
        ),
    )
    meta_ref[...] = meta
    keep = meta[0:1, 3:4]

    @pl.when(step == 0)
    def _():
        normed_rim = row_norm(before_ref[...], gain)
        rim_unit_ref[...] = row_norm(before_ref[...], 1.0)
        rim = jnp.concatenate(
            [dot(normed_rim, near_ref[...]), dot(normed_rim, far_ref[:, : conv_dim - cut])], axis=1
        ).astype(bf16)
        rim_ref[...] = rim
        for j, lanes in strips_of(conv_dim):
            ext[j // 2][j % 2, 0:8, :] = rim[8:16, lanes].astype(f32) * keep
        state[...] = jnp.zeros_like(state)
        offset[...] = jnp.zeros_like(offset)

    @pl.when(step > 0)
    def _():
        for part in ext:
            part[:, 0:8, :] = part[:, SPAN : SPAN + 8, :] * keep

    wide_u = u_ref[...].astype(f32)
    unit = wide_u * lax.rsqrt(jnp.mean(wide_u * wide_u, axis=-1, keepdims=True) + EPS_NORM)
    unit_ref[...] = unit.astype(bf16)
    normed_ref[...] = (unit * gain).astype(bf16)
    raw = dot(normed_ref[...], far_ref[:, conv_dim - cut :]).astype(bf16).astype(f32)
    raw = raw + heads_ref[0:1, :]
    raw_ref[...] = raw
    dt_values = meta[:, 0:1] * (jnp.maximum(raw, 0.0) + jnp.log1p(jnp.exp(-jnp.abs(raw))))
    dt_ref[...] = dt_values

    parts, fades, starts = [], [], []
    for c in range(SPAN // HALF):
        rows = slice(c * HALF, (c + 1) * HALF)
        dt_here = dt_values[rows]
        cumul = exact_dot(tri_ref[...], heads_ref[1:2, :] * dt_here)
        cum_ref[rows, :] = cumul
        cumdev_ref[rows, :] = offset[0:1, :] + cumul
        last = cumul[HALF - 1 : HALF]
        parts.append(jnp.exp(last - cumul) * dt_here)
        fades.append(jnp.broadcast_to(jnp.exp(last), (8, LANES)))
        starts.append(jnp.exp(offset[...]) * meta[c * HALF : c * HALF + 1, 1:2])
        offset[...] = offset[...] + last
    spread = split_lanes(jnp.concatenate(parts + fades + starts, axis=0))
    origin = pl.multiple_of(offset_ref[0, 1], 8)

    def project(s):
        part = ext[s // STRIP]
        w_here = near_ref[:, s : s + STRIP] if s < cut else far_ref[:, s - cut : s - cut + STRIP]
        piece = dot(normed_ref[...], w_here).astype(bf16)
        conv_ref[:, s : s + STRIP] = piece
        for q in range(STRIP // LANES):
            part[q, 8 : 8 + SPAN, :] = piece[:, q * LANES : (q + 1) * LANES].astype(f32)

    def activate(s):
        part = ext[s // STRIP]
        for q in range(STRIP // LANES):
            lanes = slice(s + q * LANES, s + (q + 1) * LANES)
            for base in range(0, SPAN, TILE):
                half = shifted_sum(taps_ref, lanes, part, q, origin + base + 5, bias_ref[0:1, lanes])
                turn = jnp.tanh(half)
                value = half + half * turn
                act_ref[base : base + TILE, lanes] = value.astype(bf16)
                slope_ref[base : base + TILE, lanes] = (
                    (1.0 + value) + turn * (1.0 - value)
                ).astype(bf16)

    def accumulate(s):
        cols = slice(s, s + STRIP)
        wide = dot(spread, ex_ref[:, cols])
        start_ref[:, cols] = wide[SPAN + 16 :]
        for c in range(SPAN // HALF):
            rows = slice(c * HALF, (c + 1) * HALF)
            b_rows = act_ref[rows, inner : inner + LANES]
            scaled = (act_ref[rows, cols].astype(f32) * wide[rows]).astype(bf16)
            arrived = meta[c * HALF : c * HALF + 1, 3:4] * state[:, cols]
            inc_ref[rows, cols] = arrived.astype(bf16)
            fade = wide[SPAN + 8 * c : SPAN + 8 * c + 1]
            state[:, cols] = fade * arrived + dot_tn(b_rows, scaled)

    order = [inner] + list(range(0, inner, STRIP))
    for k in range(len(order) + 2):
        if k < len(order):
            project(order[k])
        if 2 <= k and order[k - 2] != inner:
            accumulate(order[k - 2])
        if 1 <= k <= len(order):
            activate(order[k - 1])

    @pl.when(step == pl.num_programs(0) - 1)
    def _():
        state_out_ref[:, :inner] = state[...].astype(bf16)
        gain_row = jnp.exp(offset[0:1, :]) * meta[SPAN - 1 : SPAN, 1:2]
        high, low = two_terms(jnp.broadcast_to(gain_row, (HALF, LANES)))
        place = lax.broadcasted_iota(jnp.int32, (HALF, LANES), 0) % (HALF // places)
        none = jnp.zeros_like(high)
        state_out_ref[:, inner:] = jnp.where(
            place == 0, high, jnp.where(place == 1, low, none)
        )
        total_ref[0:8, :] = offset[...]
        total_ref[8:16, :] = jnp.broadcast_to(meta[SPAN - 1 : SPAN, 1:2], offset.shape)


def chain_kernel(states_ref, gains_ref, ex_ref, out_ref, *, reverse):
    places, rows, inner = out_ref.shape
    gains = jnp.concatenate([gains_ref[:, 0, :], gains_ref[:, 1, :]], axis=1)
    wide = dot(gains, ex_ref[...])
    running = jnp.zeros((rows, inner), f32)
    for k in range(places):
        at = places - 1 - k if reverse else k
        out_ref[at] = running.astype(bf16)
        running = wide[at : at + 1] * running + states_ref[at, :, :inner].astype(f32)


def join_rows(parts, wholes):
    @pl.when(pl.program_id(0) == 0)
    def _():
        for part, whole in zip(parts, wholes):
            whole[...] = part[...].astype(f32).reshape(whole.shape).astype(bf16)


def project_kernel(
    normed_ref, meta_ref, cot_ref, wo_ref, *refs, inner, sides
):
    gate_ref, gg_ref, back_ref = refs[sides : sides + 3]
    gates = refs[sides + 3 :]
    join_rows(refs[:sides], gates)
    width = gates[0].shape[1]
    wo = wo_ref[...].reshape(inner, width)
    back = (meta_ref[:, 0:1] * cot_ref[...].astype(f32)).astype(bf16)
    back_ref[...] = back
    for s in range(0, inner, STRIP):
        cols = slice(s, s + STRIP)
        w_here = gates[s // width][:, s % width : s % width + STRIP]
        gate_ref[:, cols] = dot(normed_ref[...], w_here).astype(bf16)
        gg_ref[:, cols] = dot_nt(back, wo[cols, :]).astype(bf16)


def intra_kernel(act_ref, dt_ref, cum_ref, inc_ref, ex_ref, y_ref, *, inner):
    dt_split = split_lanes(dt_ref[...])
    at_row = lax.broadcasted_iota(jnp.int32, (HALF, HALF), 0)
    at_col = lax.broadcasted_iota(jnp.int32, (HALF, HALF), 1)
    first_head = low_half((HALF, LANES))
    chunks = []
    for c in range(SPAN // HALF):
        rows = slice(c * HALF, (c + 1) * HALF)
        b_rows = act_ref[rows, inner : inner + LANES]
        c_rows = act_ref[rows, inner + LANES : inner + 2 * LANES]
        scores = jnp.where(at_row >= at_col, dot_nt(c_rows, b_rows), 0.0)
        cumul = LOG2E * cum_ref[rows, :]
        chunks.append((rows, c_rows, scores, cumul, cumul.T))

    def prepare(c, s, q, dt_wide):
        rows, _, scores, cumul, across = chunks[c]
        wide = slice(s + q * LANES, s + (q + 1) * LANES)
        h = s // 64 + 2 * q
        falls = [column(cumul, h), column(cumul, h + 1)]
        mixes = [
            (scores * jnp.exp2(jnp.minimum(fall - across[h + k : h + k + 1, :], 0.0))).astype(bf16)
            for k, fall in enumerate(falls)
        ]
        grown = jnp.exp2(jnp.where(first_head, falls[0], falls[1]))
        lanes = slice(q * LANES, (q + 1) * LANES)
        steps = (act_ref[rows, wide].astype(f32) * dt_wide[:, lanes]).astype(bf16)
        return jnp.concatenate(mixes, axis=1), block_diag(steps), grown

    work = [(c, s, q) for s in range(0, inner, STRIP) for c in range(SPAN // HALF) for q in range(2)]
    ready = {}
    strip = {}
    for k in range(len(work) + 1):
        if k < len(work):
            c, s, q = work[k]
            if (c, q) == (0, 0):
                dt_strip = dot(dt_split, ex_ref[:, s : s + STRIP])
            if q == 0:
                strip[c, s] = dot(chunks[c][1], inc_ref[chunks[c][0], s : s + STRIP])
            ready[k] = prepare(c, s, q, dt_strip[chunks[c][0]])
        if k > 0:
            c, s, q = work[k - 1]
            mixes, steps, grown = ready.pop(k - 1)
            lanes = slice(q * LANES, (q + 1) * LANES)
            y_ref[chunks[c][0], s + q * LANES : s + (q + 1) * LANES] = (
                dot(mixes, steps) + strip[c, s][:, lanes] * grown
            )


def gate_kernel(
    y_ref, act_ref, prefix_ref, cumdev_ref, meta_ref, gate_ref, gg_ref, skip_ref, gain_ref,
    ex_ref, red_ref,
    low_ref, gm_ref, dgate_ref, r_ref, gdev_ref, sums_ref,
    y_all, g_all, d_all, s_all, t_all, e_all, v_all, gdev,
    *, inner,
):
    step = pl.program_id(0)

    @pl.when(step == 0)
    def _():
        gdev[...] = jnp.zeros_like(gdev)
        sums_ref[...] = jnp.zeros_like(sums_ref)

    c_rows = act_ref[:, inner + LANES : inner + 2 * LANES]
    reach = split_lanes(jnp.exp(cumdev_ref[...]) * meta_ref[:, 1:2])
    tiles = [slice(base, base + TILE) for base in range(0, SPAN, TILE)]
    squares = [jnp.zeros((TILE, 1), f32) for _ in tiles]
    for s in range(0, inner, STRIP):
        cols = slice(s, s + STRIP)
        reached = dot(reach, ex_ref[:, cols])
        e_all[:, cols] = reached.astype(bf16)
        from_prefix = dot(c_rows, prefix_ref[:, cols])
        for at, rows in enumerate(tiles):
            y = y_ref[rows, cols] + reached[rows] * from_prefix[rows]
            y_all[rows, cols] = y
            z = gate_ref[rows, cols].astype(f32)
            mixed = y + skip_ref[0:1, cols] * act_ref[rows, cols].astype(f32)
            half = 0.5 * z
            turn = jnp.tanh(half)
            raised = 1.0 + turn
            sl = half * raised
            g = mixed * sl
            g_all[rows, cols] = g
            s_all[rows, cols] = sl
            t_all[rows, cols] = mixed * (raised + sl * (1.0 - turn))
            squares[at] = squares[at] + jnp.sum(g * g, axis=1, keepdims=True)
    factors = [lax.rsqrt(v / inner + EPS_NORM) for v in squares]
    inner_sums = [jnp.zeros((TILE, 1), f32) for _ in tiles]
    for s in range(0, inner, STRIP):
        cols = slice(s, s + STRIP)
        gain = gain_ref[0:1, cols]
        gain_sum = jnp.zeros((8, STRIP), f32)
        for at, rows in enumerate(tiles):
            gn = g_all[rows, cols] * factors[at]
            g_all[rows, cols] = gn
            low_ref[rows, cols] = (gn * gain).astype(bf16)
            raw = gg_ref[rows, cols].astype(f32)
            both = raw * gn
            gain_sum = gain_sum + eight_rows(both)
            d_all[rows, cols] = raw * gain
            inner_sums[at] = inner_sums[at] + jnp.sum(both * gain, axis=1, keepdims=True)
        sums_ref[:, cols] = sums_ref[:, cols] + gain_sum
    means = [v / inner for v in inner_sums]

    def gather_strip(cols):
        gdev[:, cols] = gdev[:, cols] + dot_tn(c_rows, e_all[:, cols])
        part = dot(v_all[:, cols], red_ref[cols, :])
        return part[:SPAN] + part[SPAN:]

    r_ref[...] = jnp.zeros_like(r_ref)
    waiting = None
    for s in range(0, inner, STRIP):
        cols = slice(s, s + STRIP)
        if waiting is not None:
            r_ref[...] = r_ref[...] + gather_strip(waiting)
        waiting = cols
        for at, rows in enumerate(tiles):
            dg = factors[at] * (d_all[rows, cols] - g_all[rows, cols] * means[at])
            gm = dg * s_all[rows, cols]
            gm_low = gm.astype(bf16)
            gm_ref[rows, cols] = gm_low
            dgate_ref[rows, cols] = (dg * t_all[rows, cols]).astype(bf16)
            high, low = two_terms(gm_low.astype(f32) * y_all[rows, cols])
            v_all[rows, cols] = high
            v_all[SPAN + rows.start : SPAN + rows.stop, cols] = low
            e_all[rows, cols] = gm_low * e_all[rows, cols]
    r_ref[...] = r_ref[...] + gather_strip(waiting)

    @pl.when(step == pl.num_programs(0) - 1)
    def _():
        gdev_ref[...] = gdev[...].astype(bf16)


def intra_back_kernel(
    act_ref, gm_ref, dt_ref, cum_ref, meta_ref, inc_ref, start_ref, prefix_ref, r_ref,
    red_ref, tri_up_ref,
    dx_ref, dbc_ref, xd_ref, da_ref, skip_ref,
    de, dlast, v_all, d_scores, d_b, d_c, reduced,
    *, inner,
):
    @pl.when(pl.program_id(0) == 0)
    def _():
        de[...] = jnp.zeros_like(de)
        dlast[...] = jnp.zeros_like(dlast)
        skip_ref[...] = jnp.zeros_like(skip_ref)

    at_row = lax.broadcasted_iota(jnp.int32, (HALF, HALF), 0)
    at_col = lax.broadcasted_iota(jnp.int32, (HALF, HALF), 1)
    first_head = low_half((HALF, LANES))
    upper = at_row <= at_col
    halves = SPAN // HALF
    d_scores[...] = jnp.zeros_like(d_scores)
    d_b[...] = jnp.zeros_like(d_b)
    d_c[...] = jnp.zeros_like(d_c)
    chunks = []
    for c in range(halves):
        rows = slice(c * HALF, (c + 1) * HALF)
        b_rows = act_ref[rows, inner : inner + LANES]
        c_rows = act_ref[rows, inner + LANES : inner + 2 * LANES]
        scores = jnp.where(upper, dot_nt(b_rows, c_rows), 0.0)
        cumul = LOG2E * cum_ref[rows, :]
        chunks.append((rows, b_rows, c_rows, scores, cumul, cumul.T))

    def prepare(c, s):
        rows, _, _, scores, cumul, across = chunks[c]
        cols = slice(s, s + STRIP)
        dt_here = dt_ref[rows, :]
        pairs = []
        for q in range(STRIP // LANES):
            h = s // 64 + 2 * q
            falls = [column(cumul, h), column(cumul, h + 1)]
            decays = [
                jnp.exp2(jnp.minimum(across[h + k : h + k + 1, :] - falls[k], 0.0)) for k in range(2)
            ]
            mixes = jnp.concatenate([(scores * decay).astype(bf16) for decay in decays], axis=1)
            cum_wide = jnp.where(first_head, falls[0], falls[1])
            dt_wide = jnp.where(first_head, column(dt_here, h), column(dt_here, h + 1))
            pairs.append((decays, mixes, cum_wide, dt_wide))
        cum_wide = jnp.concatenate([pair[2] for pair in pairs], axis=1)
        grown = jnp.exp2(cum_wide)
        left = jnp.exp2(cum_wide[HALF - 1 : HALF] - cum_wide)
        x = act_ref[rows, cols].astype(f32)
        gm = gm_ref[rows, cols]
        gm_wide = gm.astype(f32)
        skip_ref[:, cols] = skip_ref[:, cols] + eight_rows(gm_wide * x)
        steps_wide = x * jnp.concatenate([pair[3] for pair in pairs], axis=1)
        gm_grown = (gm_wide * grown).astype(bf16)
        left_steps = (steps_wide * left).astype(bf16)
        return pairs, grown[HALF - 1 : HALF], left, steps_wide.astype(bf16), gm_grown, left_steps

    def finish(c, s, made):
        pairs, fade, left, steps, gm_grown, left_steps = made
        rows, b_rows, c_rows = chunks[c][:3]
        cols = slice(s, s + STRIP)
        keep = meta_ref[c * HALF : c * HALF + 1, 3:4]
        arrived = inc_ref[rows, cols].astype(f32) + start_ref[8 * c : 8 * c + 1, cols] * prefix_ref[
            :, cols
        ].astype(f32)
        d_c[c] = d_c[c] + dot_nt(gm_grown, arrived.astype(bf16))
        de_here = de[:, cols]
        de_low = de_here.astype(bf16)
        dx_far = left * dot(b_rows, de_low)
        d_b[c] = d_b[c] + dot_nt(left_steps, de_low)
        gm = gm_ref[rows, cols]
        x = act_ref[rows, cols].astype(f32)
        for q, (decays, mixes, _, _) in enumerate(pairs):
            lanes = slice(q * LANES, (q + 1) * LANES)
            wide = slice(s + q * LANES, s + (q + 1) * LANES)
            gm_diag = block_diag(gm[:, lanes])
            d_mix = dot_nt(steps[:, lanes], gm_diag)
            dx = dot(mixes, gm_diag) + dx_far[:, lanes]
            dx_ref[rows, wide] = dx.astype(bf16)
            high, low = two_terms(x[:, lanes] * dx)
            v_all[rows, wide] = high
            v_all[SPAN + c * HALF : SPAN + (c + 1) * HALF, wide] = low
            d_scores[c] = d_scores[c] + (d_mix[:, :HALF] * decays[0] + d_mix[:, HALF:] * decays[1])
        de_new = keep * (dot_tn(c_rows, gm_grown) + fade * de_here)
        de[:, cols] = de_new
        v_all[2 * SPAN + 16 * c : 2 * SPAN + 16 * (c + 1), cols] = jnp.concatenate(
            two_terms(eight_rows(de_new * arrived)), axis=0
        )

    work = [(c, s) for s in range(0, inner, STRIP) for c in reversed(range(halves))]
    made = None
    reduced[...] = jnp.zeros_like(reduced)
    for k in range(len(work) + 2):
        before, made = made, prepare(*work[k]) if k < len(work) else None
        if 0 < k <= len(work):
            finish(*work[k - 1], before)
        if k > 1 and work[k - 2][0] == 0:
            cols = slice(work[k - 2][1], work[k - 2][1] + STRIP)
            reduced[...] = reduced[...] + dot(v_all[:, cols], red_ref[cols, :])
    for c in range(halves):
        rows, b_rows, c_rows = chunks[c][:3]
        d_low = jnp.where(upper, d_scores[c], 0.0).astype(bf16)
        dbc_ref[rows, :LANES] = dot(d_low, c_rows) + d_b[c]
        dbc_ref[rows, LANES:] = dot_tn(d_low, b_rows) + d_c[c]
    x_dot = reduced[:SPAN] + reduced[SPAN : 2 * SPAN]
    xd_ref[...] = x_dot
    d_cum = r_ref[...] - dt_ref[...] * x_dot
    for c in reversed(range(halves)):
        rows = slice(c * HALF, (c + 1) * HALF)
        da_ref[rows, :] = exact_dot(tri_up_ref[...], d_cum[rows]) + dlast[0:1, :]
        ends = reduced[2 * SPAN + 16 * c : 2 * SPAN + 16 * (c + 1)]
        dlast[...] = jnp.broadcast_to(jnp.sum(ends, axis=0, keepdims=True), dlast.shape)


def store_blocks(out_ref, parts):
    count = out_ref.shape[0] * out_ref.shape[1] * out_ref.shape[2]
    cores, sides, places = out_ref.shape[:3]
    for at in range(count):
        place, rest = at // (cores * sides), at % (cores * sides)
        rows = [part[at * (part.shape[0] // count) : (at + 1) * (part.shape[0] // count), :] for part in parts]
        block = rows[0] if len(rows) == 1 else jnp.concatenate(rows, axis=0)
        out_ref[rest % cores, rest // cores, place] = block.astype(bf16)


def outer_kernel(low_ref, back_ref, unit_ref, dgate_ref, out_ref, out_sum, *gate_sums):
    step = pl.program_id(0)
    width = gate_sums[0].shape[1]

    @pl.when(step == 0)
    def _():
        out_sum[...] = dot_tn(low_ref[...], back_ref[...])
        for k, part in enumerate(gate_sums):
            part[...] = dot_tn(unit_ref[...], dgate_ref[:, k * width : (k + 1) * width])

    @pl.when(step > 0)
    def _():
        out_sum[...] = out_sum[...] + dot_tn(low_ref[...], back_ref[...])
        for k, part in enumerate(gate_sums):
            part[...] = part[...] + dot_tn(unit_ref[...], dgate_ref[:, k * width : (k + 1) * width])

    @pl.when(step == pl.num_programs(0) - 1)
    def _():
        store_blocks(out_ref, [out_sum] + list(gate_sums))


def pass_kernel(in_ref, out_ref):
    out_ref[...] = in_ref[...]


def branch_kernel(u_ref, meta_ref, low_ref, w_ref, out_ref):
    branch = dot(low_ref[...], w_ref[...].reshape(low_ref.shape[1], out_ref.shape[1]))
    out_ref[...] = (u_ref[...].astype(f32) + meta_ref[:, 0:1] * branch).astype(bf16)


def conv_back_kernel(
    act_ref, slope_ref, conv_ref, dx_ref, gm_ref, dbc_ref, dt_ref, cumdev_ref, raw_ref, xd_ref,
    da_ref, meta_ref, above_ref, prefix_ref, total_ref, skip_ref, taps_ref, heads_ref, rim_ref,
    ex_ref, red_ref, tri_ref, origin_ref, unit_ref, rim_unit_ref, gate_sums_ref,
    dconv_ref, first_ref, sums_ref, hsums_ref, grad_ref,
    dt_fresh, dt_kept, flow, v_all, turned, grad, reduced, *scratch,
    inner, conv_dim, num_heads, own_rows, slots,
):
    step = pl.program_id(0)
    blocks = pl.num_programs(0) - 1
    keep = meta_ref[0:1, 3:4]
    strips = conv_dim // STRIP
    fresh, kept, ext = scratch[:strips], scratch[strips : 2 * strips], scratch[2 * strips :]
    tiles = [slice(base, base + TILE) for base in range(0, SPAN, TILE)]
    origin = pl.multiple_of(origin_ref[0, 1], 8)

    def finish(s):
        part = kept[s // STRIP]
        for q in range(STRIP // LANES):
            lanes = slice(s + q * LANES, s + (q + 1) * LANES)
            for base in range(0, SPAN, TILE):
                total = taps_ref[3:4, lanes] * part[q, base : base + TILE, :]
                for k in range(3):
                    total = total + taps_ref[k : k + 1, lanes] * part[
                        q, pl.ds(origin + base + 3 - k, TILE), :
                    ]
                dconv_ref[base : base + TILE, lanes] = total.astype(bf16)

    def add_grad(cols):
        grad[:, cols] = grad[:, cols] + dot(turned[...], dconv_ref[:, cols])

    dconv_ref[:, conv_dim:] = dt_kept[...]

    @pl.when(step == 0)
    def _():
        rim_rows = jnp.concatenate(
            [jnp.zeros((SPAN - 16, rim_unit_ref.shape[1]), f32), rim_unit_ref[...].astype(f32)], axis=0
        )
        turned[...] = rim_rows.T.astype(bf16)
        grad[...] = jnp.zeros_like(grad)
        dt_kept[...] = jnp.zeros_like(dt_kept)
        dconv_ref[:, conv_dim:] = jnp.zeros_like(dt_kept)
        for part in kept:
            part[...] = jnp.zeros_like(part)
        for j, lanes in strips_of(conv_dim):
            ext[j // 2][j % 2, 0:8, :] = rim_ref[8:16, lanes].astype(f32) * keep
        sums_ref[...] = jnp.zeros_like(sums_ref)
        hsums_ref[...] = jnp.zeros_like(hsums_ref)
        start = jnp.zeros((16, LANES), f32)
        for s in range(0, inner, STRIP):
            cols = slice(s, s + STRIP)
            both = above_ref[:, cols].astype(f32) * prefix_ref[:, cols].astype(f32)
            start = start + dot(
                jnp.concatenate(two_terms(eight_rows(both)), axis=0), red_ref[cols, :]
            )
        start = jnp.sum(start, axis=0, keepdims=True)
        flow[...] = start * jnp.exp(total_ref[0:8, :]) * total_ref[8:16, :]

    @pl.when(step > 0)
    def _():
        turned[...] = unit_ref[...].astype(f32).T.astype(bf16)

    @pl.when((step > 0) & (step < blocks))
    def _():
        for part in ext:
            part[:, 0:8, :] = part[:, SPAN : SPAN + 8, :] * keep

    @pl.when(step < blocks)
    def _():
        b_rows = act_ref[:, inner : inner + LANES]
        dt_here = dt_ref[...]
        ahead = jnp.exp(total_ref[0:1, :] - cumdev_ref[...]) * meta_ref[:, 2:3]
        spread = split_lanes(jnp.concatenate([dt_here, ahead], axis=0))
        d_b = dbc_ref[:, :LANES]
        pending = [slice(conv_dim, conv_dim + LANES)]
        strips_here = list(range(0, inner, STRIP)) + [inner]
        products = {}

        def multiply(s):
            cols = slice(s, s + STRIP)
            products[s] = dot(spread, ex_ref[:, cols]), dot(b_rows, above_ref[:, cols])

        reduced[...] = jnp.zeros_like(reduced)
        multiply(0)
        for n, s in enumerate(strips_here):
            cols = slice(s, s + STRIP)
            new, old, rows_in = fresh[s // STRIP], kept[s // STRIP], ext[s // STRIP]
            for q in range(STRIP // LANES):
                lanes = slice(s + q * LANES, s + (q + 1) * LANES)
                rows_in[q, 8 : 8 + SPAN, :] = conv_ref[:, lanes].astype(f32)
            if n + 2 < len(strips_here):
                multiply(strips_here[n + 1])
            add_grad(pending.pop())
            if n > 0:
                done = slice(s - STRIP, s)
                reduced[...] = reduced[...] + dot(v_all[:, done], red_ref[done, :])
            if s < inner:
                wide, passed = products.pop(s)
                lows = []
                for rows in tiles:
                    dt_wide = wide[rows]
                    ahead_wide = wide[SPAN + rows.start : SPAN + rows.stop]
                    x = act_ref[rows, cols].astype(f32)
                    far = ahead_wide * passed[rows]
                    dx = dt_wide * (dx_ref[rows, cols].astype(f32) + far)
                    dx = dx + skip_ref[0:1, cols] * gm_ref[rows, cols].astype(f32)
                    dx = dx * slope_ref[rows, cols].astype(f32)
                    for q in range(STRIP // LANES):
                        new[q, rows, :] = dx[:, q * LANES : (q + 1) * LANES]
                    v_all[rows, cols] = (x * far).astype(bf16)
                    lows.append((x * dt_wide * ahead_wide).astype(bf16))
                d_b = d_b + dot_nt(jnp.concatenate(lows, axis=0), above_ref[:, cols])
            else:
                b_cols = slice(inner, inner + LANES)
                c_cols = slice(inner + LANES, inner + 2 * LANES)
                new[0, :, :] = d_b * slope_ref[:, b_cols].astype(f32)
                new[1, :, :] = dbc_ref[:, LANES:] * slope_ref[:, c_cols].astype(f32)
            for q in range(STRIP // LANES):
                lanes = slice(s + q * LANES, s + (q + 1) * LANES)
                sums = [jnp.zeros((8, LANES), f32) for _ in range(5)]
                for base in range(0, SPAN, TILE):
                    d = new[q, base : base + TILE, :]
                    sums[4] = sums[4] + eight_rows(d)
                    for k in range(4):
                        shifted = rows_in[q, pl.ds(origin + base + 5 + k, TILE), :]
                        sums[k] = sums[k] + eight_rows(d * shifted)
                for k in range(5):
                    here = slice(8 * k, 8 * k + 8)
                    sums_ref[here, lanes] = sums_ref[here, lanes] + sums[k]
            old[:, SPAN : SPAN + 8, :] = new[:, 0:8, :] * keep
            finish(s)
            pending.append(cols)
            old[:, 0:SPAN, :] = new[...]
        add_grad(pending.pop())
        x_dot = reduced[...]
        moved = dt_here * x_dot
        rate = heads_ref[1:2, :]
        for c in range(SPAN // HALF):
            rows = slice(c * HALF, (c + 1) * HALF)
            da = da_ref[rows, :] + flow[0:1, :] + exact_dot(tri_ref[...], moved[rows]) - moved[rows]
            flow[...] = flow[...] + jnp.sum(moved[rows], axis=0, keepdims=True)
            hsums_ref[8:16, :] = hsums_ref[8:16, :] + eight_rows(da * rate * dt_here[rows])
            d_dt = xd_ref[rows, :] + x_dot[rows] + rate * da
            d_raw = meta_ref[rows, 0:1] * sigmoid(raw_ref[rows, :]) * d_dt
            real = lax.broadcasted_iota(jnp.int32, d_raw.shape, 1) < num_heads
            d_raw = jnp.where(real, d_raw, 0.0)
            hsums_ref[0:8, :] = hsums_ref[0:8, :] + eight_rows(d_raw)
            dt_fresh[rows, :] = d_raw.astype(bf16)

    @pl.when(step == 0)
    def _():
        for j, lanes in strips_of(conv_dim):
            first_ref[:, lanes] = fresh[j // 2][j % 2, 0:8, :] * keep

    @pl.when(step == blocks)
    def _():
        for s in range(0, conv_dim, STRIP):
            kept[s // STRIP][:, SPAN : SPAN + 8, :] = jnp.zeros((2, 8, LANES), f32)
            finish(s)
            add_grad(slice(s, s + STRIP))
        add_grad(slice(conv_dim, conv_dim + LANES))
        tap_rows = [
            0.5 * jnp.sum(sums_ref[8 * k : 8 * k + 8, :], axis=0, keepdims=True) for k in range(5)
        ]
        gate_row = jnp.sum(gate_sums_ref[...], axis=0, keepdims=True)
        model = grad.shape[0]
        vecs = jnp.concatenate([jnp.zeros((1, model), f32), gate_row, tap_rows[4]], axis=1)
        taps_at = [0] * 4
        vec_at = 0
        for r in range(model // own_rows):
            row_parts = {}
            for k, (row, lane, size) in enumerate(slots):
                if k < 4:
                    part = tap_rows[k][:, taps_at[k] : taps_at[k] + size]
                    taps_at[k] += size
                else:
                    part = vecs[:, vec_at : vec_at + size]
                    vec_at += size
                row_parts.setdefault(row, []).append((lane, size, part))
            for row, parts in row_parts.items():
                lane, size = parts[-1][0], parts[-1][1]
                at = r * own_rows + row
                here = slice(conv_dim + num_heads, conv_dim + num_heads + lane + size)
                grad[at : at + 1, here] = jnp.concatenate([part for _, _, part in parts], axis=1)
        store_blocks(grad_ref, [grad])

    dt_kept[...] = dt_fresh[...]


def input_grad_kernel(
    dconv_ref, dgate_ref, near_ref, far_ref, u_ref, cot_ref, gain_ref, *refs
):
    cut = near_ref.shape[1]
    grad = dot_nt(dconv_ref[:, :cut], near_ref[...]) + dot_nt(dconv_ref[:, cut:], far_ref[...])
    out_ref, gates = refs[-1], refs[:-1]
    width = gates[0].shape[1]
    side = dot_nt(dgate_ref[:, :width], gates[0][...])
    for k in range(1, len(gates)):
        side = side + dot_nt(dgate_ref[:, k * width : (k + 1) * width], gates[k][...])
    grad = grad + 0.5 * side
    for base in range(0, u_ref.shape[0], TILE):
        rows = slice(base, base + TILE)
        wide = u_ref[rows, :].astype(f32)
        factor = lax.rsqrt(jnp.mean(wide * wide, axis=-1, keepdims=True) + EPS_NORM)
        unit = wide * factor
        d = grad[rows] * gain_ref[...]
        mean = jnp.mean(d * unit, axis=-1, keepdims=True)
        du = factor * (d - unit * mean)
        out_ref[rows, :] = (cot_ref[rows, :].astype(f32) + du).astype(bf16)


def owner_kernel(
    conv_ref, both_ref, w_ref, gain_ref, hsums_ref, skip_ref, red_ref, in_ref, out_ref, small_sum_ref,
    row_ref,
    *, num_heads, slots,
):
    conv = jnp.sum(conv_ref[...].astype(f32), axis=0)
    both = jnp.sum(both_ref[...].astype(f32), axis=0)
    own_rows, width = in_ref.shape
    out_rows, side = out_ref.shape
    out_sum = both[:out_rows]
    out_ref[...] = out_sum
    spare = conv[:, conv.shape[1] - LANES :]
    small_sum_ref[...] = jnp.zeros_like(small_sum_ref)
    squares = jnp.sum(out_sum * out_sum)
    vec_at = 0
    for k, (row, lane, size) in enumerate(slots):
        part = spare[row : row + 1, num_heads + lane : num_heads + lane + size]
        squares = squares + jnp.sum(part * part)
        if k < 4:
            small_sum_ref[1 + k : 2 + k, :size] = part
        else:
            small_sum_ref[0:1, vec_at : vec_at + size] = part
            vec_at += size
    gates = (both.shape[0] - out_rows) // own_rows
    gain = gain_ref[...]
    norm_rows = jnp.zeros((own_rows, 1), f32)
    tail = width - gates * side
    pieces = [
        (k * side, 0.5 * both[out_rows + k * own_rows : out_rows + (k + 1) * own_rows]) for k in range(gates)
    ] + [(gates * side, conv[:, :tail])]
    for at, piece in pieces:
        cols = slice(at, at + piece.shape[1])
        scaled = piece * gain
        in_ref[:, cols] = scaled
        squares = squares + jnp.sum(scaled * scaled)
        norm_rows = norm_rows + jnp.sum(
            piece * w_ref[:, cols].astype(bf16).astype(f32), axis=1, keepdims=True
        )
    squares = squares + jnp.sum(norm_rows * norm_rows)
    lane = lax.broadcasted_iota(jnp.int32, (own_rows, LANES), 1)
    row = lax.broadcasted_iota(jnp.int32, (own_rows, LANES), 0)
    spread = jnp.where(lane == 3 * num_heads + 1 + row, jnp.broadcast_to(norm_rows, lane.shape), 0.0)
    first_lane = lax.broadcasted_iota(jnp.int32, (1, LANES), 1)
    parts = [jnp.sum(hsums_ref[8 * k : 8 * k + 8, :], axis=0, keepdims=True) for k in range(2)]
    high, rest = two_terms(skip_ref[...])
    middle, low = two_terms(skip_ref[...] - high.astype(f32))
    skip = dot(high, red_ref[...]) + (dot(middle, red_ref[...]) + dot(low, red_ref[...]))
    parts.append(jnp.sum(skip, axis=0, keepdims=True))
    heads_row = jnp.concatenate(
        [part[:, :num_heads] for part in parts] + [jnp.zeros((1, LANES - 3 * num_heads), f32)], axis=1
    )
    packed = (
        heads_row
        + jnp.where(first_lane == 3 * num_heads, squares, 0.0)
        + jnp.sum(spread, axis=0, keepdims=True)
    )
    row_ref[...] = jnp.broadcast_to(packed[None], row_ref.shape)


def update_kernel(*refs, num_heads, own_rows, taps_own):
    rank_ref, rows_ref, in_sum_ref, out_sum_ref, small_ref = refs[:5]
    states, norm_ref, outs = refs[5:20], refs[20], refs[21:]
    rows = rows_ref[:, 0, :]
    total = jnp.sum(rows, axis=0, keepdims=True)
    lane = lax.broadcasted_iota(jnp.int32, (1, LANES), 1)
    heads = jnp.concatenate(
        [total[:, k * num_heads : (k + 1) * num_heads] for k in range(3)], axis=0
    )
    norm_sq = (
        jnp.sum(jnp.where(lane == 3 * num_heads, total, 0.0), axis=1, keepdims=True)
        + jnp.sum(jnp.sum(heads * heads, axis=0, keepdims=True), axis=1, keepdims=True)
    )
    grad_norm = jnp.sqrt(norm_sq)
    norm_ref[...] = grad_norm
    factor = jnp.minimum(1.0, MAX_NORM / (grad_norm + 1e-06))
    vec_width = states[9].shape[1]
    place = lax.broadcasted_iota(jnp.int32, (rows.shape[0], vec_width), 0)
    wanted = rank_ref[0, 0] * vec_width + lax.broadcasted_iota(jnp.int32, (rows.shape[0], vec_width), 1)
    mine = jnp.zeros((rows.shape[0], vec_width), f32)
    for j in range(own_rows):
        at = 3 * num_heads + 1 + j
        here = jnp.broadcast_to(rows[:, at : at + 1], mine.shape)
        mine = mine + jnp.where(place * own_rows + j == wanted, here, 0.0)
    vec = small_ref[0:1, :vec_width] + jnp.sum(mine, axis=0, keepdims=True)
    sums = (in_sum_ref[...], out_sum_ref[...], small_ref[1:5, :taps_own], vec, heads)
    rates = (
        (RATE_MAT, DECAY_MAT), (RATE_MAT, DECAY_MAT), (RATE_CONV, DECAY_MAT), (RATE_VEC, 0.0),
        (RATE_HEAD, 0.0),
    )
    for k, (summed, (rate, decay)) in enumerate(zip(sums, rates)):
        master, first, second = (ref[...] for ref in states[3 * k : 3 * k + 3])
        clipped_ref, first_ref, second_ref, master_ref, copy_ref = outs[5 * k : 5 * k + 5]
        clipped = summed * factor
        clipped_ref[...] = clipped
        first = BETA_ONE * first + (1.0 - BETA_ONE) * clipped
        second = BETA_TWO * second + (1.0 - BETA_TWO) * clipped * clipped
        first_ref[...] = first
        second_ref[...] = second
        first_hat = first / (1.0 - BETA_ONE**STEP)
        second_hat = second / (1.0 - BETA_TWO**STEP)
        master = master - rate * (first_hat / (jnp.sqrt(second_hat) + ADAM_EPS) + decay * master)
        master_ref[...] = master
        copy_ref[...] = master.astype(bf16)


def shift(value, axis, steps):
    count = lax.axis_size(axis)
    initial, last = (max(0, -steps), min(count, count - steps))
    return lax.ppermute(value, axis, [(source, source + steps) for source in range(initial, last)])


def axis_bits(axis):
    return [(axis, 1 << k) for k in reversed(range(lax.axis_size(axis).bit_length() - 1))]


def swap(value, axis, bit):
    count = lax.axis_size(axis)
    return lax.ppermute(value, axis, [(k, k ^ bit) for k in range(count)])


def my_bit(axis, bit):
    return (lax.axis_index(axis) // bit) % 2


def zero_from(value):
    return jnp.minimum(jnp.abs(value[(0,) * value.ndim].astype(f32)), 0.0)


def rank_bits():
    return axis_bits("seq") + axis_bits("rep")


def gather_step(value, known, axis, bit):
    order = rank_bits()
    place = sum(order.index(k) < order.index((axis, bit)) for k in known)
    other = swap(value, axis, bit)
    value = jnp.where(
        my_bit(axis, bit) == 0,
        jnp.stack([value, other], axis=place),
        jnp.stack([other, value], axis=place),
    )
    return value, known + [(axis, bit)]


def gather_ring(value, axis, stride):
    count = lax.axis_size(axis)
    groups = count // stride
    parts = [value]
    for k in range(1, groups):
        parts.append(lax.ppermute(value, axis, [(i, (i - k * stride) % count) for i in range(count)]))
    mine = lax.axis_index(axis) // stride
    return lax.dynamic_slice_in_dim(jnp.stack(parts + parts), (groups - mine) % groups, groups, 0)


def gather_steps(value, known, steps):
    for axis, bit in steps:
        value, known = gather_step(value, known, axis, bit)
    return value, known


def halves(value, axis, bit, at=0):
    mine = my_bit(axis, bit)
    given = lax.dynamic_index_in_dim(value, 1 - mine, at, keepdims=False)
    return lax.dynamic_index_in_dim(value, mine, at, keepdims=False), given


def join(parts, axis, bit):
    own, given = parts
    return (own.astype(f32) + swap(given, axis, bit).astype(f32)).astype(bf16)


def pair_sends(total, axis):
    count = lax.axis_size(axis)
    here = lax.axis_index(axis) // 2
    return [
        lax.dynamic_index_in_dim(total, (here + k) % (count // 2), 0, keepdims=False)
        for k in range(count // 2)
    ]


def pair_parts(sends, axis):
    count = lax.axis_size(axis)
    parts = [
        lax.ppermute(sent, axis, [(i, (i + 2 * k) % count) for i in range(count)])
        for k, sent in enumerate(sends)
        if k > 0
    ]
    return jnp.stack(sends[:1] + parts)


def call(kernel, grid, ins, in_blocks, outs, out_blocks, scratch, flops, after=(), token=False, passed=0, **fixed):
    first = len(after)
    own_outs = len(outs)
    if token:
        outs = outs + [like(1, 1, dtype=jnp.int32)]
        out_blocks = out_blocks + [pl.BlockSpec(memory_space=pltpu.SMEM)]

    def body(*refs):
        refs = list(refs[first:])
        if token:
            refs.pop(count_in + own_outs)[0, 0] = jnp.int32(0)
        del refs[count_in + own_outs : count_in + own_outs + passed]
        kernel(*refs, **fixed)

    count_in = len(ins)
    aliases = {k: len(outs) + k for k in range(passed)}
    outs = outs + [like(*v.shape, dtype=v.dtype) for v in after[:passed]]
    out_blocks = out_blocks + [pl.BlockSpec(memory_space=pl.ANY)] * passed
    ins = list(after) + ins
    in_blocks = [pl.BlockSpec(memory_space=pl.ANY)] * first + in_blocks
    moved = sum(v.size * v.dtype.itemsize for v in ins) + sum(v.size * v.dtype.itemsize for v in outs)
    return pl.pallas_call(
        body,
        name=kernel.__name__,
        grid=(grid,),
        in_specs=in_blocks,
        out_specs=out_blocks,
        out_shape=outs,
        scratch_shapes=scratch,
        input_output_aliases=aliases,
        compiler_params=pltpu.CompilerParams(
            dimension_semantics=("arbitrary",), vmem_limit_bytes=VMEM_BYTES
        ),
        cost_estimate=pl.CostEstimate(flops=int(flops), bytes_accessed=moved, transcendentals=0),
    )(*ins)


def full(shape):
    return pl.BlockSpec(shape, lambda i: (0,) * len(shape))


def held(shape):
    return pl.BlockSpec(shape, lambda i: (0,) * len(shape), pipeline_mode=pl.Buffered(1))


def rows_of(count, width, index=lambda i: i):
    return pl.BlockSpec((count, width), lambda i: (index(i), 0))


def like(*shape, dtype=f32):
    return jax.ShapeDtypeStruct(shape, dtype)


def shards(
    tokens,
    cotangent,
    seq_lengths,
    in_weight,
    in_first,
    in_second,
    out_weight,
    out_first,
    out_second,
    conv_weight,
    conv_first,
    conv_second,
    vectors,
    vec_first,
    vec_second,
    head_params,
    head_first,
    head_second,
):
    u = tokens[0]
    cot = cotangent[0]
    rows, model = u.shape
    places = lax.axis_size("seq")
    ranks = places * lax.axis_size("rep")
    taps_own = conv_weight.shape[1]
    vecs_own = vectors.shape[0]
    conv_dim = taps_own * ranks
    inner = out_weight.shape[0] * ranks
    heads = head_params.shape[1]
    head_dim = inner // heads
    nblk = rows // SPAN
    quarter = rows // 4
    third = rows // 3
    wide = conv_dim + LANES
    cut = -(-wide // (2 * STRIP)) * STRIP

    own_rows, out_rows = in_weight.shape[0], out_weight.shape[0]
    sides = inner // model
    start = (lax.axis_index("seq") * rows).astype(jnp.int32)
    offset = jnp.stack([start, jnp.zeros_like(start)]).reshape(1, 2)
    bits = rank_bits()
    far_steps = [k for k in bits if k[0] == "seq" and k[1] > 1][::-1]
    near_step, rep_steps = ("seq", 1), axis_bits("rep")
    before = shift(u[rows - 16 :], "seq", 1)
    in_low = in_weight.astype(bf16)
    spare_lanes = LANES - heads
    pieces = [conv_weight[k] for k in range(4)]
    pieces += [vectors[at : at + LANES // 2] for at in range(0, vecs_own, LANES // 2)]
    slots, spare_rows, fill = [], [[]], 0
    for piece in pieces:
        size = piece.shape[0]
        if fill + size > spare_lanes:
            spare_rows.append([])
            fill = 0
        slots.append((len(spare_rows) - 1, fill, size))
        spare_rows[-1].append(piece)
        fill += size
    spare_rows = [jnp.concatenate(row) for row in spare_rows]
    spare = jnp.stack([jnp.pad(row, (0, spare_lanes - row.shape[0])) for row in spare_rows])
    spare = jnp.pad(spare, ((0, own_rows - len(spare_rows)), (0, 0))).astype(bf16)
    conv_shard = jnp.concatenate([in_low[:, inner:], spare], axis=1)
    known = far_steps[::-1]
    if len(known) == 2:
        shard = gather_ring(conv_shard, "seq", 2)
        shard = shard.reshape((2, 2) + conv_shard.shape)
    else:
        shard, _ = gather_steps(conv_shard, [], far_steps)
    w_near, known_near = gather_steps(shard[..., :cut], known, [near_step])
    w_far, known_far = gather_steps(shard[..., cut:], known, rep_steps[:1])
    w_near, known_near = gather_steps(w_near, known_near, rep_steps[:1])
    w_far, known_far = gather_steps(w_far, known_far, [near_step])
    w_near, _ = gather_steps(w_near, known_near, rep_steps[1:])
    w_far, _ = gather_steps(w_far, known_far, rep_steps[1:])
    w_near = w_near.reshape(model, cut)
    w_far = w_far.reshape(model, wide - cut)
    others = [out_weight.astype(bf16)] + [in_low[:, s : s + model] for s in range(0, inner, model)]
    others = lax.all_gather(jnp.concatenate(others, axis=0), ("seq", "rep"), axis=0)
    if own_rows % 8 == 0:
        out_part, gate_parts = others, [others] * sides
        b_out_w = pl.BlockSpec((ranks, out_rows, model), lambda i: (0, 0, 0))
        b_gates = [
            pl.BlockSpec((ranks, own_rows, model), lambda i, at=out_rows // own_rows + k: (0, at, 0))
            for k in range(sides)
        ]
    else:
        out_part = others[:, :out_rows].reshape(1, inner, model)
        gate_parts = [
            others[:, out_rows + k * own_rows : out_rows + (k + 1) * own_rows].reshape(1, model, model)
            for k in range(sides)
        ]
        b_out_w, b_gates = full((1, inner, model)), [full((1, model, model))] * sides

    head_rows = jnp.stack([head_params[0], -jnp.exp(head_params[1])])
    head_rows = jnp.pad(head_rows, ((0, 6), (0, LANES - heads)))
    skip_wide = jnp.repeat(head_params[2], head_dim)[None]

    lane_head = np.arange(inner) // head_dim
    spread = (np.arange(LANES)[:, None] == lane_head[None]).astype(np.float32)
    ex = jnp.asarray(np.concatenate([spread, spread], axis=0), bf16)
    red = jnp.asarray(spread.T, bf16)
    order = np.arange(HALF)
    tri = jnp.asarray((order[:, None] >= order[None]).astype(np.float32), bf16)
    tri_up = jnp.asarray((order[:, None] <= order[None]).astype(np.float32), bf16)

    b_act = rows_of(SPAN, conv_dim)
    b_in = rows_of(SPAN, inner)
    b_lane = rows_of(SPAN, LANES)
    b_model = rows_of(SPAN, model)
    b_meta = rows_of(SPAN, 8)
    b_ex = full((2 * LANES, inner))
    b_red = full((inner, LANES))
    b_tri = full((HALF, HALF))
    b_heads = full((8, LANES))
    b_state = full((LANES, inner))
    b_one = full((1, inner))
    b_scalar = pl.BlockSpec(memory_space=pltpu.SMEM)
    q_model = rows_of(quarter, model)
    q_in = rows_of(quarter, inner)
    q_meta = rows_of(quarter, 8)
    t_model = rows_of(third, model)
    t_in = rows_of(third, inner)
    lane_out = like(rows, LANES)
    low_in = like(rows, inner, dtype=bf16)
    low_conv = like(rows, conv_dim, dtype=bf16)
    low_model = like(rows, model, dtype=bf16)
    strip_scratch = pltpu.VMEM((STRIP // LANES, SPAN + 8, LANES), f32)
    strips = conv_dim // STRIP

    (
        unit, normed, conv_in, act, slope, meta, dt_values, cumul, cumdev, raw, own_inc, starts, rim,
        rim_unit, state_out, total, half_taps, norm_gain, gate_gain, _,
    ) = call(
        front_kernel,
        nblk,
        [
            seq_lengths, offset, u, before, w_near, w_far, head_rows, ex, tri,
        ],
        [
            b_scalar, b_scalar, b_model, held((16, model)), held((model, cut)),
            held((model, wide - cut)), b_heads, b_ex, b_tri,
        ],
        [
            low_model, low_model, low_conv, low_conv, low_conv, like(rows, 8),
            lane_out, lane_out, lane_out, lane_out, low_in, like(16 * nblk, inner),
            like(16, conv_dim, dtype=bf16), like(16, model, dtype=bf16),
            like(LANES, inner + LANES, dtype=bf16), like(16, LANES), like(4, conv_dim), like(1, model),
            like(1, inner), like(1, conv_dim),
        ],
        [
            b_model, b_model, b_act, b_act, b_act, b_meta, b_lane, b_lane, b_lane, b_lane, b_in,
            rows_of(16, inner), full((16, conv_dim)), full((16, model)),
            full((LANES, inner + LANES)), full((16, LANES)), full((4, conv_dim)), full((1, model)), b_one,
            full((1, conv_dim)),
        ],
        [pltpu.VMEM((LANES, inner), f32), pltpu.VMEM((8, LANES), f32)] + [strip_scratch] * strips,
        2 * rows * model * wide * 4,
        conv_dim=conv_dim,
        inner=inner,
        places=places,
        num_rows=rows,
        own_rows=own_rows,
        slots=tuple(slots),
        heads=heads,
    )

    def chain(states, gains, reverse, after, passed=0):
        whole = (places, LANES // places, inner)
        return call(
            chain_kernel, 1, [states, gains, ex],
            [full(states.shape), full(gains.shape), b_ex],
            [like(*whole, dtype=bf16)], [full(whole)], [], 1e7, after, passed=passed, reverse=reverse,
        )

    def exchange(blocks):
        return lax.all_to_all(blocks, "seq", 0, 0, tiled=True)

    arrived = exchange(state_out.reshape(places, LANES // places, inner + LANES))
    gains = arrived[:, :2, inner:]
    y_own = call(
        intra_kernel,
        nblk,
        [act, dt_values, cumul, own_inc, ex],
        [b_act, b_lane, b_lane, b_in, b_ex],
        [like(rows, inner)],
        [b_in],
        [],
        2 * rows * model * inner * 4,
        inner=inner,
    )[0]
    chained = chain(arrived, gains, False, [y_own])[0]
    prefix = exchange(chained).reshape(LANES, inner)
    gate_in, grad_gated, back_rows, *w_gates = call(
        project_kernel,
        4,
        [normed, meta, cot, out_part] + gate_parts,
        [q_model, q_meta, q_model, b_out_w] + b_gates,
        [low_in, low_in, low_model] + [like(model, model, dtype=bf16)] * sides,
        [q_in, q_in, q_model] + [full((model, model))] * sides,
        [],
        2 * rows * model * inner * 2,
        [chained],
        inner=inner,
        sides=sides,
    )

    wide_scratch = pltpu.VMEM((SPAN, inner), f32)
    gated_low, grad_mixed, grad_gate, r_sums, gdev, gate_sums = call(
        gate_kernel,
        nblk,
        [
            y_own, act, prefix, cumdev, meta, gate_in, grad_gated, skip_wide, gate_gain, ex, red,
        ],
        [b_in, b_act, b_state, b_lane, b_meta, b_in, b_in, b_one, b_one, b_ex, b_red],
        [low_in, low_in, low_in, lane_out, like(LANES, inner, dtype=bf16), like(8, inner)],
        [b_in, b_in, b_in, b_lane, b_state, full((8, inner))],
        [wide_scratch] * 5
        + [
            pltpu.VMEM((SPAN, inner), bf16),
            pltpu.VMEM((2 * SPAN, inner), bf16),
            pltpu.VMEM((LANES, inner), f32),
        ],
        2 * rows * model * inner * 3,
        inner=inner,
    )

    gathered = exchange(gdev.reshape(places, LANES // places, inner))
    block_shape = tuple(lax.axis_size("rep") // 2 if k == 0 else 2 for k in range(2))[::-1] + (places,)
    rep_shape = (lax.axis_size("rep"), 1, places)
    both_grad = call(
        outer_kernel,
        3,
        [gated_low, back_rows, unit, grad_gate],
        [t_in, t_model, t_model, t_in],
        [like(*rep_shape, out_rows + sides * own_rows, model, dtype=bf16)],
        [full(rep_shape + (out_rows + sides * own_rows, model))],
        [pltpu.VMEM((inner, model), f32)] + [pltpu.VMEM((model, model), f32)] * sides,
        2 * rows * model * inner * 2,
    )[0]
    chained_back, both_grad = chain(gathered, gains, True, [both_grad], passed=1)
    above = exchange(chained_back).reshape(LANES, inner)
    both_half = lax.psum_scatter(both_grad[:, 0], "rep", scatter_dimension=0, tiled=True)[0]
    if places == 8:
        both_parts = halves(both_half.reshape((places // 2, 2) + both_half.shape[1:]), "seq", 1, at=1)
        sends = pair_sends(join(both_parts, "seq", 1), "seq")
        both_all = pair_parts(sends, "seq")
    else:
        both_parts, sends = (both_half,), []
        both_all = exchange(both_half)

    flip = lambda i: nblk - 1 - i
    f_lane = rows_of(SPAN, LANES, flip)
    f_in = rows_of(SPAN, inner, flip)
    dx_own, dbc_own, xd_own, da_own, skip_sums = call(
        intra_back_kernel,
        nblk,
        [
            act, grad_mixed, dt_values, cumul, meta, own_inc, starts, prefix, r_sums, red, tri_up,
        ],
        [
            rows_of(SPAN, conv_dim, flip), f_in, f_lane, f_lane, rows_of(SPAN, 8, flip), f_in,
            rows_of(16, inner, flip), b_state, f_lane, b_red, b_tri,
        ],
        [low_in, like(rows, 2 * LANES), lane_out, lane_out, like(8, inner)],
        [f_in, rows_of(SPAN, 2 * LANES, flip), f_lane, f_lane, full((8, inner))],
        [
            pltpu.VMEM((LANES, inner), f32),
            pltpu.VMEM((8, LANES), f32),
            pltpu.VMEM((2 * SPAN + 32, inner), bf16),
        ]
        + [pltpu.VMEM((SPAN // HALF, HALF, LANES), f32)] * 3
        + [pltpu.VMEM((2 * SPAN + 32, LANES), f32)],
        2 * rows * model * inner * 6,
        [chained_back],
        inner=inner,
    )
    capped = lambda i: jnp.minimum(i, nblk - 1)
    late = lambda i: jnp.maximum(i - 1, 0)
    c_lane = rows_of(SPAN, LANES, capped)
    c_in = rows_of(SPAN, inner, capped)
    c_act = rows_of(SPAN, conv_dim, capped)
    dconv, first_rows, _, head_sum_rows, conv_grad = call(
        conv_back_kernel,
        nblk + 1,
        [
            act, slope, conv_in, dx_own, grad_mixed, dbc_own, dt_values, cumdev, raw, xd_own, da_own,
            meta, above, prefix, total, skip_wide, half_taps, head_rows, rim, ex, red, tri,
            offset, unit, rim_unit, gate_sums,
        ],
        [
            c_act, c_act, c_act, c_in, c_in, rows_of(SPAN, 2 * LANES, capped), c_lane, c_lane, c_lane,
            c_lane, c_lane, rows_of(SPAN, 8, capped), b_state, b_state,
            held((16, LANES)), b_one, held((4, conv_dim)), b_heads, held((16, conv_dim)),
            b_ex, b_red, b_tri, b_scalar, rows_of(SPAN, model, late), held((16, model)), held((8, inner)),
        ],
        [
            like(rows, wide, dtype=bf16), like(8, conv_dim), like(40, conv_dim), like(16, LANES),
            like(*block_shape, own_rows, wide, dtype=bf16),
        ],
        [
            rows_of(SPAN, wide, late), full((8, conv_dim)), full((40, conv_dim)), full((16, LANES)),
            full(block_shape + (own_rows, wide)),
        ],
        [
            pltpu.VMEM((SPAN, LANES), bf16),
            pltpu.VMEM((SPAN, LANES), bf16),
            pltpu.VMEM((8, LANES), f32),
            pltpu.VMEM((SPAN, inner), bf16),
            pltpu.VMEM((model, SPAN), bf16),
            pltpu.VMEM((model, wide), f32),
            pltpu.VMEM((SPAN, LANES), f32),
        ]
        + [pltpu.VMEM((STRIP // LANES, SPAN, LANES), f32)] * strips
        + [strip_scratch] * (2 * strips),
        2 * rows * model * inner * 3,
        inner=inner,
        conv_dim=conv_dim,
        num_heads=heads,
        own_rows=own_rows,
        slots=tuple(slots),
    )
    conv_part = join(halves(conv_grad, *rep_steps[1]), *rep_steps[1])
    conv_parts = halves(conv_part, *rep_steps[0])
    block_out, first_rows = call(
        branch_kernel,
        4,
        [u, meta, gated_low, out_part],
        [q_model, q_meta, q_in, b_out_w],
        [low_model],
        [q_model],
        [],
        2 * rows * model * inner,
        [first_rows, conv_parts[1]] + list(both_parts[1:]),
        passed=1,
    )
    _, pass_token, first_rows = call(
        pass_kernel, 1, [tri], [b_tri], [like(HALF, HALF, dtype=bf16)], [b_tri], [], 1e4,
        [first_rows] + sends[1:], token=True, passed=1,
    )
    after = shift(first_rows, "seq", -1)
    late_rows = jnp.stack(
        [sum(half_taps[k] * after[j - k] for k in range(j + 1)) for j in range(3)]
    )
    tail = dconv[rows - 16 :, :conv_dim].astype(f32) + jnp.pad(late_rows, ((13, 0), (0, 0)))
    dconv = lax.dynamic_update_slice(dconv, tail.astype(bf16), (rows - 16, 0))


    own_part, given_part = conv_parts
    own_part = lax.dynamic_index_in_dim(
        conv_part, my_bit(*rep_steps[0]) + pass_token[0, 0], 0, keepdims=False
    )
    conv_part = join((own_part, given_part), *rep_steps[0])
    input_grad = call(
        input_grad_kernel,
        4,
        [dconv, grad_gate, w_near, w_far, u, cot, norm_gain] + w_gates,
        [
            rows_of(quarter, wide), q_in, held((model, cut)), held((model, wide - cut)),
            q_model, q_model, held((1, model)),
        ]
        + [held((model, model))] * sides,
        [low_model],
        [q_model],
        [],
        2 * rows * model * (wide + inner),
        [conv_part],
    )[0]
    conv_all = exchange(conv_part)

    rank = lax.axis_index("seq") * lax.axis_size("rep") + lax.axis_index("rep")
    own_gain = lax.dynamic_slice_in_dim(norm_gain[0], rank * own_rows, own_rows)[:, None]
    small_shape = (8, LANES)
    in_sum, out_sum, small_sum, row = call(
        owner_kernel,
        1,
        [conv_all, both_all, in_weight, own_gain, head_sum_rows, skip_sums, red],
        [
            full(v.shape)
            for v in (conv_all, both_all, in_weight, own_gain, head_sum_rows, skip_sums, red)
        ],
        [like(*in_weight.shape), like(*out_weight.shape), like(*small_shape), like(ranks, 1, LANES)],
        [full(in_weight.shape), full(out_weight.shape), full(small_shape), full((ranks, 1, LANES))],
        [],
        1e6,
        [input_grad],
        num_heads=heads,
        slots=tuple(slots),
    )
    all_rows = lax.all_to_all(row, ("seq", "rep"), 0, 0, tiled=True)
    states = [
        in_weight, in_first, in_second, out_weight, out_first, out_second, conv_weight, conv_first,
        conv_second, vectors[None], vec_first[None], vec_second[None], head_params, head_first, head_second,
    ]
    shapes = [states[3 * k].shape for k in range(5)]
    updated = call(
        update_kernel,
        1,
        [rank.astype(jnp.int32).reshape(1, 1), all_rows, in_sum, out_sum, small_sum] + states,
        [b_scalar]
        + [full(v.shape) for v in [all_rows, in_sum, out_sum, small_sum] + states],
        [like(1, 1)]
        + [like(*shape, dtype=kind) for shape in shapes for kind in (f32, f32, f32, f32, bf16)],
        [full((1, 1))] + [full(shape) for shape in shapes for _ in range(5)],
        [],
        1e6,
        num_heads=heads,
        own_rows=own_rows,
        taps_own=taps_own,
    )
    grad_norm, updated = updated[0][0, 0], list(updated[1:])
    updated[15:20] = [v[0] for v in updated[15:20]]
    return (block_out[None], input_grad[None], grad_norm) + tuple(updated)


def solution(mesh):
    tokens = P("rep", "seq", None)
    row_split = P(("seq", "rep"), None)
    column_split = P(None, ("seq", "rep"))
    flat_split = P(("seq", "rep"))
    return jax.shard_map(
        shards,
        mesh=mesh,
        in_specs=(tokens, tokens, P("rep", None))
        + (row_split,) * 6
        + (column_split,) * 3
        + (flat_split,) * 3
        + (P(),) * 3,
        out_specs=(tokens, tokens, P())
        + (row_split,) * 10
        + (column_split,) * 5
        + (flat_split,) * 5
        + (P(),) * 5,
        check_vma=False,
    )
```
